32 devices in a mesh: mom: 8 (over z, y), tm: 4 (over x, core).
Axes of the slice: x: 2, y: 2, z: 4, core: 2. Of those that a mesh axis runs over, the one named last changes fastest.
Arguments:
- hist_lesser: float32 [2, 256, 16, 2048], P(None, 'mom', None, 'tm'), may hold values from -2 to 6
- hist_retarded: float32 [2, 256, 16, 2048], P(None, 'mom', None, 'tm'), may hold values from -4 to 4
- propagator: float32 [2, 256, 16, 16], P(None, 'mom'), may hold values from -0.5 to 1.5
- coupling: float32 [256], replicated, may hold values from 0.15 to 0.4
- mf_weight: float32 [256], replicated, may hold values from 0.5 to 2
- lag_weight: float32 [8], replicated, may hold values from 0.05 to 0.2
Outputs:
- new_slice: float32 [2, 256, 16, 2048], P(None, 'mom', None, 'tm')
The draws below stay inside these ranges and needn't reach their ends.
All inputs are finite; a program needn't handle non-finite values.
Results may differ from the reference program's by a relative error of at most 0.0003.
Values sent between devices are 32-bit elements; how exact they have to be, the bound alone decides.
No kernel may reach another device: no remote copies, remote signals or barrier semaphores. Data moves between devices by JAX's collectives and lax.ppermute only.
A program may use at most 128 MiB of HBM per device.

```python
import math
import jax
import jax.numpy as jnp
from jax import lax

KX = 16
KY = 16
ORB = 16
W = 8
PASSES = 3
K = 256
H = 128


def draw_hist_lesser(key, part):
    base_key = jax.random.fold_in(key, 11)
    noise_key, rough_key = jax.random.split(base_key)
    shape = (2, K, ORB, H * ORB)
    base = jnp.clip(0.5 * jax.random.normal(noise_key, shape, jnp.float32), -2.0, 2.0)
    lowest = 0.5
    rough = jax.random.uniform(rough_key, (K, ORB, 1), jnp.float32, 0.7, 1.3)
    level = lowest + jnp.arange(K, dtype=jnp.float32) / (K - 1)
    column = jnp.arange(H * ORB, dtype=jnp.int32)
    orbital = jnp.arange(ORB, dtype=jnp.int32)
    marked = ((column[None, :] // ORB == H - 1) & (column[None, :] % ORB == orbital[:, None])).astype(jnp.float32)
    lifted = level[:, None, None] * rough * marked[None, :, :]
    return base.at[1].add(lifted)


def draw_propagator(key, part):
    noise_key = jax.random.fold_in(key, 23)
    shape = (2, K, ORB, ORB)
    noise = jnp.clip(0.1 * jax.random.normal(noise_key, shape, jnp.float32), -0.5, 0.5)
    identity = jnp.eye(ORB, dtype=jnp.float32)
    return noise.at[0].add(identity[None, :, :])


def level_of(key, shape, shards, low, largest):
    def one(position, blocks):
        draws = jax.random.uniform(jax.random.fold_in(jax.random.fold_in(key, 6), position), (blocks,), jnp.float32, low / len(shards), largest / len(shards))
        return jnp.repeat(jnp.exp(draws), shape[position] // blocks).reshape((-1,) + (1,) * (len(shape) - position - 1))

    loudness = one(*shards[0])
    for cut in shards[1:]:
        loudness = loudness * one(*cut)
    return loudness


def centred(stream_key, shape, scale, most, cuts=(), kind=jnp.bfloat16):
    gain = level_of(stream_key, shape, cuts, -0.22, 0.18) if cuts else 1.0
    drawn = jax.random.normal(stream_key, shape, jnp.float32) * scale * gain
    return jnp.minimum(jnp.maximum(drawn, -most), most).astype(kind)


def setup_inputs(seed: int = 0) -> dict:
    key_of = jax.random.split(jax.random.key(seed), 7)
    return {
        "hist_lesser": draw_hist_lesser(jax.random.fold_in(key_of[6], 71), 0),
        "hist_retarded": centred(key_of[1], (2, K, ORB, H * ORB), 1.0, 4.0, ((1, 8), (3, 4)), jnp.float32),
        "propagator": draw_propagator(jax.random.fold_in(key_of[6], 71), 0),
        "coupling": jnp.clip(jnp.exp(jax.random.uniform(key_of[3], (ORB * ORB,), jnp.float32, math.log(0.15), math.log(0.4))), 0.15, 0.4),
        "mf_weight": jnp.clip(jnp.exp(jax.random.uniform(key_of[4], (ORB * ORB,), jnp.float32, math.log(0.5), math.log(2.0))), 0.5, 2.0),
        "lag_weight": jnp.clip(jnp.exp(jax.random.uniform(key_of[5], (W,), jnp.float32, math.log(0.05), math.log(0.2))), 0.05, 0.2),
    }


HIGHEST = lax.Precision.HIGHEST

def momentum_tables():
    index = jnp.arange(KX * KY, dtype=jnp.int32)
    first = index // KY
    second = index % KY
    turn_x = first[:, None] * first[None, :] % KX
    turn_y = second[:, None] * second[None, :] % KY
    phase = 2.0 * math.pi * (turn_x.astype(jnp.float32) / KX + turn_y.astype(jnp.float32) / KY)
    scale = 1.0 / math.sqrt(KX * KY)
    return (jnp.cos(phase) * scale, jnp.sin(phase) * scale)

def complex_product(pattern, first, second):
    real = jnp.einsum(pattern, first[0], second[0], precision=HIGHEST) - jnp.einsum(pattern, first[1], second[1], precision=HIGHEST)
    imaginary = jnp.einsum(pattern, first[0], second[1], precision=HIGHEST) + jnp.einsum(pattern, first[1], second[0], precision=HIGHEST)
    return jnp.stack([real, imaginary])

def back_to_momenta(real, imaginary, cosine, sine):
    out_real = jnp.einsum('rk,rabm->kabm', cosine, real, precision=HIGHEST) + jnp.einsum('rk,rabm->kabm', sine, imaginary, precision=HIGHEST)
    out_imag = jnp.einsum('rk,rabm->kabm', cosine, imaginary, precision=HIGHEST) - jnp.einsum('rk,rabm->kabm', sine, real, precision=HIGHEST)
    return jnp.stack([out_real, out_imag])

def reference(hist_lesser, hist_retarded, propagator, coupling, mf_weight, lag_weight):
    cosine, sine = momentum_tables()
    lesser = hist_lesser.reshape(2, K, ORB, H, ORB)
    retarded = hist_retarded.reshape(2, K, ORB, H, ORB)
    start = complex_product('kab,kbjc->kajc', propagator, lesser)
    zeros = jnp.zeros((2, K, ORB, W - 1, ORB), jnp.float32)
    padded_r = jnp.concatenate([zeros, retarded], axis=3)
    padded_l = jnp.concatenate([zeros, lesser], axis=3)
    strength = (coupling * coupling).reshape(ORB, ORB, 1)
    mean_weight = mf_weight.reshape(ORB, ORB)
    last_mark = (jnp.arange(W) == W - 1).astype(jnp.float32)
    current = start
    for sweep in range(PASSES):
        window = jnp.transpose(current[:, :, :, H - W:, :], (0, 1, 2, 4, 3))
        space_real = jnp.einsum('rk,kabm->rabm', cosine, window[0], precision=HIGHEST) - jnp.einsum('rk,kabm->rabm', sine, window[1], precision=HIGHEST)
        space_imag = jnp.einsum('rk,kabm->rabm', cosine, window[1], precision=HIGHEST) + jnp.einsum('rk,kabm->rabm', sine, window[0], precision=HIGHEST)
        magnitude = strength * (space_real * space_real + space_imag * space_imag)
        lesser_k = back_to_momenta(magnitude * space_real, magnitude * space_imag, cosine, sine)
        pair_k = back_to_momenta(strength * (space_real * space_real - space_imag * space_imag), strength * 2.0 * space_real * space_imag, cosine, sine)
        occupation = lax.optimization_barrier(jnp.mean(window[..., W - 1], axis=1))
        sigma = lesser_k + (mean_weight * occupation)[:, None, :, :, None] * last_mark

        def add_lag(offset, total):
            offset = jnp.asarray(offset).astype(jnp.int32)
            part_r = lax.dynamic_slice_in_dim(padded_r, offset, H, 3)
            part_l = lax.dynamic_slice_in_dim(padded_l, offset, H, 3)
            sigma_lag = lax.dynamic_index_in_dim(sigma, offset, 4, keepdims=False)
            pair_lag = lax.dynamic_index_in_dim(pair_k, offset, 4, keepdims=False)
            weight = lax.dynamic_index_in_dim(lag_weight, offset, 0, keepdims=False)
            terms = complex_product('kab,kbjc->kajc', sigma_lag, part_r) + complex_product('kab,kbjc->kajc', pair_lag, part_l)
            return total + weight * terms
        collision = lax.fori_loop(0, W, add_lag, jnp.zeros_like(start))
        current = start + jnp.stack([collision[1], -collision[0]])
    return current.reshape(2, K, ORB, H * ORB)
```

```python
import functools
import math

import jax
import jax.numpy as jnp
import numpy as np
from jax import lax
from jax.experimental import pallas as pl
from jax.experimental.pallas import tpu as pltpu
from jax.sharding import PartitionSpec as P

KX = 16
KY = 16
ORB = 16
W = 8
PASSES = 3


HIGHEST = lax.Precision.HIGHEST


def shifted(x, axis, by):
    peers = lax.axis_size(axis)
    pairs = [(i, i + by) for i in range(peers) if 0 <= i + by < peers]
    return lax.ppermute(x, axis, pairs)


def broadcast(x, axis, root):
    mine = lax.axis_index(axis) == root
    return lax.psum(jnp.where(mine, x, jnp.zeros_like(x)), axis)


def momentum_tables():
    index = jnp.arange(KX * KY, dtype=jnp.int32)
    first = index // KY
    second = index % KY
    turn_x = first[:, None] * first[None, :] % KX
    turn_y = second[:, None] * second[None, :] % KY
    phase = 2.0 * math.pi * (turn_x.astype(jnp.float32) / KX + turn_y.astype(jnp.float32) / KY)
    scale = 1.0 / math.sqrt(KX * KY)
    return (jnp.cos(phase) * scale, jnp.sin(phase) * scale)


def complex_product(pattern, first, second):
    real = jnp.einsum(pattern, first[0], second[0], precision=HIGHEST) - jnp.einsum(
        pattern, first[1], second[1], precision=HIGHEST
    )
    imaginary = jnp.einsum(pattern, first[0], second[1], precision=HIGHEST) + jnp.einsum(
        pattern, first[1], second[0], precision=HIGHEST
    )
    return jnp.stack([real, imaginary])


def back_to_momenta(real, imaginary, cosine, sine):
    out_real = jnp.dot(cosine, real, precision=HIGHEST) + jnp.dot(
        sine, imaginary, precision=HIGHEST
    )
    out_imag = jnp.dot(cosine, imaginary, precision=HIGHEST) - jnp.dot(
        sine, real, precision=HIGHEST
    )
    return jnp.stack([out_real, out_imag])


def local_products(arrived, cosine, sine, strength, lag_mark):
    lag_count = lag_mark.shape[0]
    space_real = jnp.dot(cosine, arrived[0], precision=HIGHEST) - jnp.dot(
        sine, arrived[1], precision=HIGHEST
    )
    space_imag = jnp.dot(cosine, arrived[1], precision=HIGHEST) + jnp.dot(
        sine, arrived[0], precision=HIGHEST
    )
    column_strength = jnp.repeat(strength, lag_count)
    magnitude = column_strength * (space_real * space_real + space_imag * space_imag)
    lesser_real = magnitude * space_real
    lesser_imag = magnitude * space_imag
    pair_real = column_strength * (space_real * space_real - space_imag * space_imag)
    pair_imag = column_strength * 2.0 * space_real * space_imag
    return (
        back_to_momenta(lesser_real, lesser_imag, cosine, sine),
        back_to_momenta(pair_real, pair_imag, cosine, sine),
    )


def self_energies(window, cosine, sine, strength, mf_weight, last_mark):
    momenta_here = window.shape[1]
    outgoing = window.reshape(2, momenta_here, ORB * ORB * W)
    arrived = lax.all_to_all(outgoing, "mom", split_axis=2, concat_axis=1, tiled=True)
    lesser_r, pair_r = local_products(arrived, cosine, sine, strength, last_mark)
    back_lesser, back_pair = (
        lax.all_to_all(lesser_r, "mom", split_axis=1, concat_axis=2, tiled=True),
        lax.all_to_all(pair_r, "mom", split_axis=1, concat_axis=2, tiled=True),
    )
    sigma = back_lesser.reshape(2, momenta_here, ORB, ORB, W)
    pair_k = back_pair.reshape(2, momenta_here, ORB, ORB, W)
    own_total = jnp.sum(window[..., W - 1], axis=1)
    occupation = lax.psum(own_total, "mom") / (KX * KY)
    sigma = sigma + (mf_weight.reshape(ORB, ORB) * occupation)[:, None, :, :, None] * last_mark
    return (sigma, pair_k)


def collide(sigma, pair_k, lag_weight, padded_r, padded_l, first, count):
    weighted_sigma = sigma * lag_weight
    weighted_pair = pair_k * lag_weight

    def ladder(padded):
        region = lax.dynamic_slice_in_dim(padded, first * ORB, (count + W - 1) * ORB, 3)
        return jnp.stack(
            [region[..., offset * ORB : (offset + count) * ORB] for offset in range(W)], axis=3
        )

    return complex_product("kabm,kbmx->kax", weighted_sigma, ladder(padded_r)) + complex_product(
        "kabm,kbmx->kax", weighted_pair, ladder(padded_l)
    )


def on_device_any(hist_lesser, hist_retarded, propagator, coupling, mf_weight, lag_weight):
    momenta_here = hist_lesser.shape[1]
    times_here = hist_lesser.shape[3] // ORB
    cosine, sine = momentum_tables()
    lesser = hist_lesser.reshape(2, momenta_here, ORB, times_here, ORB)
    start = complex_product("kab,kbjc->kajc", propagator, lesser).reshape(
        2, momenta_here, ORB, times_here * ORB
    )
    rim_width = (W - 1) * ORB
    rim_retarded, rim_lesser = shifted(
        (
            hist_retarded[..., times_here * ORB - rim_width :],
            hist_lesser[..., times_here * ORB - rim_width :],
        ),
        "tm",
        1,
    )
    padded_r = jnp.concatenate([rim_retarded, hist_retarded], axis=3)
    padded_l = jnp.concatenate([rim_lesser, hist_lesser], axis=3)
    block = min(32, times_here)
    count_blocks = times_here // block
    window_start = (times_here - W) * ORB
    pair_count = ORB * ORB // lax.axis_size("mom")
    strength = lax.dynamic_slice_in_dim(
        coupling * coupling, lax.axis_index("mom") * pair_count, pair_count, 0
    )
    last_mark = (jnp.arange(W) == W - 1).astype(jnp.float32)
    owner = lax.axis_size("tm") - 1
    current = start[..., window_start:]
    full_slice = start
    for sweep in range(PASSES):
        shared = broadcast(current, "tm", owner)
        window = jnp.transpose(shared.reshape(2, momenta_here, ORB, W, ORB), (0, 1, 2, 4, 3))
        sigma, pair_k = self_energies(window, cosine, sine, strength, mf_weight, last_mark)
        if sweep + 1 < PASSES:
            collision = collide(sigma, pair_k, lag_weight, padded_r, padded_l, times_here - W, W)
            current = start[..., window_start:] + jnp.stack([collision[1], -collision[0]])
        else:
            blocks_out = lax.map(
                lambda number: collide(
                    sigma, pair_k, lag_weight, padded_r, padded_l, number * block, block
                ),
                jnp.arange(count_blocks, dtype=jnp.int32),
            )
            collision = jnp.moveaxis(blocks_out, 0, 3).reshape(
                2, momenta_here, ORB, times_here * ORB
            )
            full_slice = start + jnp.stack([collision[1], -collision[0]])
            current = full_slice[..., window_start:]
    return full_slice


VMEM = pl.BlockSpec(memory_space=pltpu.VMEM)
HALF = W * ORB // 2
TILE = W * ORB
PARAMS = pltpu.CompilerParams(vmem_limit_bytes=48 * 1024 * 1024)


def halves(x):
    high = x.astype(jnp.bfloat16)
    return high, (x - high.astype(jnp.float32)).astype(jnp.bfloat16)


def matmul(first, second):
    return jnp.dot(first, second, preferred_element_type=jnp.float32)


def fourier_tables():
    index = np.arange(KX * KY)
    turn = np.outer(index // KY, index // KY) / KX + np.outer(index % KY, index % KY) / KY
    phase = 2.0 * np.pi * (turn % 1.0)
    table = np.concatenate([np.cos(phase), np.sin(phase)]) / math.sqrt(KX * KY)
    high = table.astype(jnp.bfloat16)
    low = (table - high.astype(np.float64)).astype(jnp.bfloat16)
    return jnp.asarray(high), jnp.asarray(low)


def lower_lanes(shape):
    return lax.broadcasted_iota(jnp.int32, shape, 1) < HALF


def store_window(send_ref, k, own, real, imag):
    lower = lower_lanes(real.shape)
    turned_real = pltpu.roll(real, HALF, 1)
    turned_imag = pltpu.roll(imag, HALF, 1)
    send_ref[pl.ds(k, ORB, stride=2 * own), :] = jnp.where(lower, real, turned_imag)
    send_ref[pl.ds(own + k, ORB, stride=2 * own), :] = jnp.where(lower, turned_real, imag)


def first_window_kernel(own, propagator_ref, lesser_ref, send_ref):
    for k in range(own):
        left = jnp.concatenate([propagator_ref[0, k], propagator_ref[1, k]], axis=0)
        right = jnp.concatenate([lesser_ref[0, k], lesser_ref[1, k]], axis=1)
        both = jnp.dot(left, right, precision=HIGHEST, preferred_element_type=jnp.float32)
        real = both[:ORB, :TILE] - both[ORB:, TILE:]
        imag = both[:ORB, TILE:] + both[ORB:, :TILE]
        store_window(send_ref, k, own, real, imag)


def fourier_kernel(arrived_ref, high_ref, low_ref, strength_ref, mean_ref, out_ref):
    count = KX * KY
    x_high, x_low = halves(arrived_ref[...])
    main = matmul(high_ref[...], jnp.concatenate([x_high, x_low], axis=1))
    turned = main[:, :TILE] + main[:, TILE:] + matmul(low_ref[...], x_high)
    lower = lower_lanes((count, TILE))
    sine_part = pltpu.roll(turned[count:], HALF, 1)
    here = turned[:count] + jnp.where(lower, -sine_part, sine_part)
    swapped = pltpu.roll(here, HALF, 1)
    real = jnp.where(lower, here, swapped)
    imag = jnp.where(lower, swapped, here)
    real_square = real * real
    imag_square = imag * imag
    size = real_square + imag_square
    strength = strength_ref[...]
    out_real = strength * jnp.where(lower, size * real, real_square - imag_square)
    out_imag = strength * jnp.where(lower, size * imag, 2.0 * real * imag)
    origin = (lax.broadcasted_iota(jnp.int32, (count, TILE), 0) == 0).astype(jnp.float32)
    mean = origin * mean_ref[...]
    out_real = out_real + mean * real
    out_imag = out_imag + mean * imag
    real_high, real_low = halves(out_real)
    imag_high, imag_low = halves(out_imag)
    y_high = jnp.concatenate([real_high, imag_high], axis=1)
    y_low = jnp.concatenate([real_low, imag_low], axis=1)
    back = matmul(high_ref[...], y_high) + matmul(low_ref[...], y_high) + matmul(high_ref[...], y_low)
    devices, rows, _ = out_ref.shape
    own = rows // 2
    out_ref[:, :own] = (back[:count, :TILE] + back[count:, TILE:]).reshape(devices, own, TILE)
    out_ref[:, own:] = (back[:count, TILE:] - back[count:, :TILE]).reshape(devices, own, TILE)


def coefficients(arrived_ref, start_ref, k, k_start, own):
    def piece(part, half):
        return arrived_ref[pl.ds((2 * half + part) * own + k, ORB, stride=4 * own), :]

    rows = [
        jnp.concatenate([piece(part, 0), piece(part, 1) + start_ref[part, k_start]], axis=1) for part in range(2)
    ]
    return halves(jnp.concatenate(rows, axis=0))


def ladder(regions, width):
    rows = []
    for half in range(2):
        for kind in range(2):
            for lag in range(W // 2):
                offset = ORB * (1 + half * (W // 2) + lag)
                rows.append(jnp.concatenate([x[:, offset : offset + width] for x in regions[kind]], axis=1))
    return jnp.concatenate(rows, axis=0)


def contract(left_high, left_low, right_high, right_low, width):
    rows = 2 * ORB
    main = matmul(jnp.concatenate([left_high, left_low], axis=0), right_high)
    both = main[:rows] + main[rows:] + matmul(left_high, right_low)
    real = both[:ORB, :width] - both[ORB:, width:]
    imag = both[:ORB, width:] + both[ORB:, :width]
    return imag, -real


def window_ladder_kernel(own, retarded_ref, lesser_ref, high_ref, low_ref):
    for k in range(own):
        regions = [[ref[part, k] for part in range(2)] for ref in (retarded_ref, lesser_ref)]
        high_ref[k], low_ref[k] = halves(ladder(regions, TILE))


def window_kernel(own, arrived_ref, start_ref, high_ref, low_ref, send_ref):
    for k in range(own):
        left_high, left_low = coefficients(arrived_ref, start_ref, k, k, own)
        real, imag = contract(left_high, left_low, high_ref[k], low_ref[k], TILE)
        store_window(send_ref, k, own, real, imag)


def final_kernel(own, tm_ref, arrived_ref, start_ref, retarded_ref, lesser_ref, rim_retarded_ref, rim_lesser_ref, out_ref):
    width = retarded_ref.shape[3]

    def step(k, carry):
        left_high, left_low = coefficients(arrived_ref.at[0], start_ref, k, k, own)
        regions = [
            [jnp.concatenate([rim[part, k], ref[part, k]], axis=1) for part in range(2)]
            for rim, ref in ((rim_retarded_ref, retarded_ref), (rim_lesser_ref, lesser_ref))
        ]
        right_high, right_low = halves(ladder(regions, width))
        out_ref[0, k], out_ref[1, k] = contract(left_high, left_low, right_high, right_low, width)
        return carry

    lax.fori_loop(0, own, step, 0)


def own_block(x, own, axis):
    return lax.dynamic_slice_in_dim(x, lax.axis_index("tm") * own, own, axis)


def scatter(x, own):
    peers = lax.axis_size("tm")
    parts = [lax.ppermute(x[:, t * own : (t + 1) * own], "tm", [(peers - 1, t)]) for t in range(peers - 1)]
    mine = x[:, (peers - 1) * own :]
    arrived = functools.reduce(jnp.add, parts)
    return jnp.where(lax.axis_index("tm") == peers - 1, mine, arrived)


def on_device_tiled(hist_lesser, hist_retarded, propagator, coupling, mf_weight, lag_weight):
    both_axes = ("mom", "tm")
    momenta_here = hist_lesser.shape[1]
    columns = hist_lesser.shape[3]
    peers = lax.axis_size("tm")
    devices = lax.axis_size("mom") * peers
    own = momenta_here // peers
    count = KX * KY

    first = scatter(hist_lesser[..., columns - TILE :], own)
    rest = scatter(
        jnp.concatenate(
            [
                hist_retarded[..., columns - 2 * TILE : columns - TILE],
                hist_retarded[..., columns - TILE :],
                hist_lesser[..., columns - 2 * TILE : columns - TILE],
            ],
            axis=0,
        ),
        own,
    )
    near_retarded = jnp.concatenate([rest[0:2], rest[2:4]], axis=3)
    near_lesser = jnp.concatenate([rest[4:6], first], axis=3)
    rim_retarded, rim_lesser = shifted(
        (hist_retarded[..., columns - TILE :], hist_lesser[..., columns - TILE :]), "tm", 1
    )

    me = lax.axis_index("mom") * peers + lax.axis_index("tm")
    last_mark = (jnp.arange(W) == W - 1).astype(jnp.float32)
    strong = (coupling * coupling).reshape(ORB, 1, ORB) * lag_weight[:, None]
    mean = mf_weight.reshape(ORB, 1, ORB) * (lag_weight * last_mark)[:, None]
    strong = lax.dynamic_slice_in_dim(strong.reshape(devices, HALF), me, 1, 0)
    mean = lax.dynamic_slice_in_dim(mean.reshape(devices, HALF), me, 1, 0)
    strength = jnp.concatenate([strong, strong], axis=1)
    mean = jnp.concatenate([mean, jnp.zeros_like(mean)], axis=1)
    start = jnp.pad(
        jnp.stack([-propagator[1], propagator[0]]), ((0, 0), (0, 0), (0, 0), (TILE - ORB, 0))
    )
    start_own = own_block(start, own, 1)
    table_high, table_low = fourier_tables()

    def call(kernel, shapes, *operands):
        return pl.pallas_call(
            kernel,
            out_shape=shapes,
            in_specs=[VMEM] * len(operands),
            out_specs=jax.tree.map(lambda _: VMEM, shapes),
            compiler_params=PARAMS,
        )(*operands)

    f32 = functools.partial(jax.ShapeDtypeStruct, dtype=jnp.float32)
    bf16 = functools.partial(jax.ShapeDtypeStruct, dtype=jnp.bfloat16)
    send = call(
        functools.partial(first_window_kernel, own), f32((count, TILE)), own_block(propagator, own, 1), first
    )
    rungs = bf16((own, 2 * TILE, 2 * TILE))
    rungs_high, rungs_low = call(
        functools.partial(window_ladder_kernel, own), (rungs, rungs), near_retarded, near_lesser
    )
    for sweep in range(PASSES):
        arrived = lax.all_to_all(send.reshape(devices, own, TILE), both_axes, 0, 0, tiled=True)
        back = call(
            fourier_kernel,
            f32((devices, 2 * own, TILE)),
            arrived.reshape(count, TILE),
            table_high,
            table_low,
            strength,
            mean,
        )
        arrived = lax.all_to_all(back, both_axes, 0, 0, tiled=True).reshape(2 * count, TILE)
        if sweep + 1 < PASSES:
            send = call(
                functools.partial(window_kernel, own),
                f32((count, TILE)),
                arrived,
                start_own,
                rungs_high,
                rungs_low,
            )

    blocks = [arrived]
    distance = peers // 2
    gathered = {0: arrived}
    while distance:
        for known in list(gathered):
            gathered[known ^ distance] = lax.ppermute(
                gathered[known], "tm", [(t, t ^ distance) for t in range(peers)]
            )
        distance //= 2
    blocks = jnp.stack([gathered[s] for s in range(peers)])

    def momenta(s, tm_ref):
        return (0, tm_ref[0] ^ s, 0, 0)

    def spec(width):
        return pl.BlockSpec((2, own, ORB, width), momenta)

    return pl.pallas_call(
        functools.partial(final_kernel, own),
        out_shape=f32(hist_lesser.shape),
        grid_spec=pltpu.PrefetchScalarGridSpec(
            num_scalar_prefetch=1,
            grid=(peers,),
            in_specs=[
                pl.BlockSpec((1, 2 * count, TILE), lambda s, tm_ref: (s, 0, 0)),
                spec(TILE),
                spec(columns),
                spec(columns),
                spec(TILE),
                spec(TILE),
            ],
            out_specs=spec(columns),
        ),
        compiler_params=PARAMS,
    )(
        lax.axis_index("tm").reshape(1).astype(jnp.int32),
        blocks,
        start,
        hist_retarded,
        hist_lesser,
        rim_retarded,
        rim_lesser,
    )


def on_device(hist_lesser, *others):
    peers = lax.axis_size("tm")
    devices = lax.axis_size("mom") * peers
    own, rest = divmod(hist_lesser.shape[1], peers)
    fits = devices == 2 * ORB and rest == 0 and own % 8 == 0 and peers & (peers - 1) == 0
    fits = fits and hist_lesser.shape[3] >= 2 * TILE and hist_lesser.shape[3] % TILE == 0
    return (on_device_tiled if fits else on_device_any)(hist_lesser, *others)


def solution(mesh):
    return jax.shard_map(
        on_device,
        mesh=mesh,
        in_specs=(
            P(None, "mom", None, "tm"),
            P(None, "mom", None, "tm"),
            P(None, "mom", None, None),
            P(),
            P(),
            P(),
        ),
        out_specs=P(None, "mom", None, "tm"),
        check_vma=False,
    )
```

```python
import functools
import math

import jax
import jax.numpy as jnp
import numpy as np
from jax import lax
from jax.experimental import pallas as pl
from jax.experimental.pallas import tpu as pltpu
from jax.sharding import PartitionSpec as P

KX = 16
KY = 16
ORB = 16
W = 8
PASSES = 3


HIGHEST = lax.Precision.HIGHEST


def shifted(x, axis, by):
    peers = lax.axis_size(axis)
    pairs = [(i, i + by) for i in range(peers) if 0 <= i + by < peers]
    return lax.ppermute(x, axis, pairs)


def broadcast(x, axis, root):
    mine = lax.axis_index(axis) == root
    return lax.psum(jnp.where(mine, x, jnp.zeros_like(x)), axis)


def momentum_tables():
    index = jnp.arange(KX * KY, dtype=jnp.int32)
    first = index // KY
    second = index % KY
    turn_x = first[:, None] * first[None, :] % KX
    turn_y = second[:, None] * second[None, :] % KY
    phase = 2.0 * math.pi * (turn_x.astype(jnp.float32) / KX + turn_y.astype(jnp.float32) / KY)
    scale = 1.0 / math.sqrt(KX * KY)
    return (jnp.cos(phase) * scale, jnp.sin(phase) * scale)


def complex_product(pattern, first, second):
    real = jnp.einsum(pattern, first[0], second[0], precision=HIGHEST) - jnp.einsum(
        pattern, first[1], second[1], precision=HIGHEST
    )
    imaginary = jnp.einsum(pattern, first[0], second[1], precision=HIGHEST) + jnp.einsum(
        pattern, first[1], second[0], precision=HIGHEST
    )
    return jnp.stack([real, imaginary])


def back_to_momenta(real, imaginary, cosine, sine):
    out_real = jnp.dot(cosine, real, precision=HIGHEST) + jnp.dot(
        sine, imaginary, precision=HIGHEST
    )
    out_imag = jnp.dot(cosine, imaginary, precision=HIGHEST) - jnp.dot(
        sine, real, precision=HIGHEST
    )
    return jnp.stack([out_real, out_imag])


def local_products(arrived, cosine, sine, strength, lag_mark):
    lag_count = lag_mark.shape[0]
    space_real = jnp.dot(cosine, arrived[0], precision=HIGHEST) - jnp.dot(
        sine, arrived[1], precision=HIGHEST
    )
    space_imag = jnp.dot(cosine, arrived[1], precision=HIGHEST) + jnp.dot(
        sine, arrived[0], precision=HIGHEST
    )
    column_strength = jnp.repeat(strength, lag_count)
    magnitude = column_strength * (space_real * space_real + space_imag * space_imag)
    lesser_real = magnitude * space_real
    lesser_imag = magnitude * space_imag
    pair_real = column_strength * (space_real * space_real - space_imag * space_imag)
    pair_imag = column_strength * 2.0 * space_real * space_imag
    return (
        back_to_momenta(lesser_real, lesser_imag, cosine, sine),
        back_to_momenta(pair_real, pair_imag, cosine, sine),
    )


def self_energies(window, cosine, sine, strength, mf_weight, last_mark):
    momenta_here = window.shape[1]
    outgoing = window.reshape(2, momenta_here, ORB * ORB * W)
    arrived = lax.all_to_all(outgoing, "mom", split_axis=2, concat_axis=1, tiled=True)
    lesser_r, pair_r = local_products(arrived, cosine, sine, strength, last_mark)
    back_lesser, back_pair = (
        lax.all_to_all(lesser_r, "mom", split_axis=1, concat_axis=2, tiled=True),
        lax.all_to_all(pair_r, "mom", split_axis=1, concat_axis=2, tiled=True),
    )
    sigma = back_lesser.reshape(2, momenta_here, ORB, ORB, W)
    pair_k = back_pair.reshape(2, momenta_here, ORB, ORB, W)
    own_total = jnp.sum(window[..., W - 1], axis=1)
    occupation = lax.psum(own_total, "mom") / (KX * KY)
    sigma = sigma + (mf_weight.reshape(ORB, ORB) * occupation)[:, None, :, :, None] * last_mark
    return (sigma, pair_k)


def collide(sigma, pair_k, lag_weight, padded_r, padded_l, first, count):
    weighted_sigma = sigma * lag_weight
    weighted_pair = pair_k * lag_weight

    def ladder(padded):
        region = lax.dynamic_slice_in_dim(padded, first * ORB, (count + W - 1) * ORB, 3)
        return jnp.stack(
            [region[..., offset * ORB : (offset + count) * ORB] for offset in range(W)], axis=3
        )

    return complex_product("kabm,kbmx->kax", weighted_sigma, ladder(padded_r)) + complex_product(
        "kabm,kbmx->kax", weighted_pair, ladder(padded_l)
    )


def on_device_any(hist_lesser, hist_retarded, propagator, coupling, mf_weight, lag_weight):
    momenta_here = hist_lesser.shape[1]
    times_here = hist_lesser.shape[3] // ORB
    cosine, sine = momentum_tables()
    lesser = hist_lesser.reshape(2, momenta_here, ORB, times_here, ORB)
    start = complex_product("kab,kbjc->kajc", propagator, lesser).reshape(
        2, momenta_here, ORB, times_here * ORB
    )
    rim_width = (W - 1) * ORB
    rim_retarded, rim_lesser = shifted(
        (
            hist_retarded[..., times_here * ORB - rim_width :],
            hist_lesser[..., times_here * ORB - rim_width :],
        ),
        "tm",
        1,
    )
    padded_r = jnp.concatenate([rim_retarded, hist_retarded], axis=3)
    padded_l = jnp.concatenate([rim_lesser, hist_lesser], axis=3)
    block = min(32, times_here)
    count_blocks = times_here // block
    window_start = (times_here - W) * ORB
    pair_count = ORB * ORB // lax.axis_size("mom")
    strength = lax.dynamic_slice_in_dim(
        coupling * coupling, lax.axis_index("mom") * pair_count, pair_count, 0
    )
    last_mark = (jnp.arange(W) == W - 1).astype(jnp.float32)
    owner = lax.axis_size("tm") - 1
    current = start[..., window_start:]
    full_slice = start
    for sweep in range(PASSES):
        shared = broadcast(current, "tm", owner)
        window = jnp.transpose(shared.reshape(2, momenta_here, ORB, W, ORB), (0, 1, 2, 4, 3))
        sigma, pair_k = self_energies(window, cosine, sine, strength, mf_weight, last_mark)
        if sweep + 1 < PASSES:
            collision = collide(sigma, pair_k, lag_weight, padded_r, padded_l, times_here - W, W)
            current = start[..., window_start:] + jnp.stack([collision[1], -collision[0]])
        else:
            blocks_out = lax.map(
                lambda number: collide(
                    sigma, pair_k, lag_weight, padded_r, padded_l, number * block, block
                ),
                jnp.arange(count_blocks, dtype=jnp.int32),
            )
            collision = jnp.moveaxis(blocks_out, 0, 3).reshape(
                2, momenta_here, ORB, times_here * ORB
            )
            full_slice = start + jnp.stack([collision[1], -collision[0]])
            current = full_slice[..., window_start:]
    return full_slice


VMEM = pl.BlockSpec(memory_space=pltpu.VMEM)
SMEM = pl.BlockSpec(memory_space=pltpu.SMEM)
IN_HBM = pl.BlockSpec(memory_space=pltpu.HBM)
HALF = W * ORB // 2
TILE = W * ORB


def limit(mebibytes):
    return pltpu.CompilerParams(vmem_limit_bytes=mebibytes * 1024 * 1024)


def halves(x):
    high = x.astype(jnp.bfloat16)
    return high, (x - high.astype(jnp.float32)).astype(jnp.bfloat16)


def matmul(first, second):
    return jnp.dot(first, second, preferred_element_type=jnp.float32)


def fourier_tables():
    index = np.arange(KX * KY)
    turn = np.outer(index // KY, index // KY) / KX + np.outer(index % KY, index % KY) / KY
    phase = 2.0 * np.pi * (turn % 1.0)
    table = np.concatenate([np.cos(phase), np.sin(phase)]) / math.sqrt(KX * KY)
    high = table.astype(jnp.bfloat16)
    low = (table - high.astype(np.float64)).astype(jnp.bfloat16)
    return jnp.asarray(high), jnp.asarray(low)


def lower_lanes(shape):
    return lax.broadcasted_iota(jnp.int32, shape, 1) < HALF


def store_window(send_ref, k, own, real, imag):
    lower = lower_lanes(real.shape)
    turned_real = pltpu.roll(real, HALF, 1)
    turned_imag = pltpu.roll(imag, HALF, 1)
    send_ref[pl.ds(k, ORB, stride=2 * own), :] = jnp.where(lower, real, turned_imag)
    send_ref[pl.ds(own + k, ORB, stride=2 * own), :] = jnp.where(lower, turned_real, imag)


def start_all(copies):
    for copy in copies:
        copy.start()
    return copies


def wait_all(copies):
    for copy in copies:
        copy.wait()


def first_window_kernel(
    own, propagator_ref, retarded_ref, lesser_ref, low_ref, high_ref, near0_ref, near1_ref, window_ref, arrive, pass_on
):
    momenta, columns = lesser_ref.shape[1], lesser_ref.shape[3]
    half = momenta // 2
    fetches = start_all(
        [
            pltpu.make_async_copy(
                lesser_ref.at[:, first : first + own, :, columns - TILE :],
                window_ref.at[:, first : first + own],
                arrive.at[number],
            )
            for number, first in enumerate(range(0, momenta, own))
        ]
    )
    copies = start_all(
        [
            pltpu.make_async_copy(
                ref.at[:, tm * own : (tm + 1) * own, :, columns - 2 * TILE :],
                near_ref.at[2 * kind : 2 * kind + 2],
                pass_on.at[tm, kind],
            )
            for tm, near_ref in enumerate((near0_ref, near1_ref))
            for kind, ref in enumerate((retarded_ref, lesser_ref))
        ]
    )
    for number, fetch in enumerate(fetches):
        fetch.wait()
        for k in range(number * own, (number + 1) * own):
            left = jnp.concatenate([propagator_ref[0, k], propagator_ref[1, k]], axis=0)
            right = jnp.concatenate([window_ref[0, k], window_ref[1, k]], axis=1)
            imag, real = contract(*halves(left), *halves(right), TILE)
            store_window(low_ref if k < half else high_ref, k % half, half, -real, imag)
    wait_all(copies)


def fourier_kernel(arrived_ref, high_ref, low_ref, strength_ref, mean_ref, out_ref):
    count = KX * KY
    useful = count // (arrived_ref.shape[0] * arrived_ref.shape[2])
    x_high, x_low = halves(arrived_ref[:, arrived_ref.shape[1] - useful :].reshape(count, TILE))
    main = matmul(high_ref[...], jnp.concatenate([x_high, x_low], axis=1))
    turned = main[:, :TILE] + main[:, TILE:] + matmul(low_ref[...], x_high)
    lower = lower_lanes((count, TILE))
    sine_part = pltpu.roll(turned[count:], HALF, 1)
    here = turned[:count] + jnp.where(lower, -sine_part, sine_part)
    swapped = pltpu.roll(here, HALF, 1)
    real = jnp.where(lower, here, swapped)
    imag = jnp.where(lower, swapped, here)
    real_square = real * real
    imag_square = imag * imag
    size = real_square + imag_square
    strength = strength_ref[...]
    out_real = strength * jnp.where(lower, size * real, real_square - imag_square)
    out_imag = strength * jnp.where(lower, size * imag, 2.0 * real * imag)
    origin = (lax.broadcasted_iota(jnp.int32, (count, TILE), 0) == 0).astype(jnp.float32)
    mean = origin * mean_ref[...]
    out_real = out_real + mean * real
    out_imag = out_imag + mean * imag
    real_high, real_low = halves(out_real)
    imag_high, imag_low = halves(out_imag)
    y_high = jnp.concatenate([real_high, imag_high], axis=1)
    y_low = jnp.concatenate([real_low, imag_low], axis=1)
    back = matmul(high_ref[...], y_high) + matmul(low_ref[...], y_high) + matmul(high_ref[...], y_low)
    devices, rows, _ = out_ref.shape
    own = rows // 2
    out_ref[:, :own] = (back[:count, :TILE] + back[count:, TILE:]).reshape(devices, own, TILE)
    out_ref[:, own:] = (back[:count, TILE:] - back[count:, :TILE]).reshape(devices, own, TILE)


def coefficients(arrived_ref, propagator_ref, k, own):
    pieces = []
    for part, start in enumerate((-propagator_ref[1], propagator_ref[0])):
        first, second = (
            arrived_ref[pl.ds((2 * half + part) * own + k, ORB, stride=4 * own), :] for half in range(2)
        )
        start = jnp.concatenate([jnp.zeros((ORB, TILE - ORB), jnp.float32), start], axis=1)
        pieces.append((first, second + start))
    return pieces


def ladder(regions, width):
    rows = []
    for half in range(2):
        for kind in range(2):
            for lag in range(W // 2):
                offset = ORB * (1 + half * (W // 2) + lag)
                rows.append(jnp.concatenate([x[:, offset : offset + width] for x in regions[kind]], axis=1))
    return jnp.concatenate(rows, axis=0)


def contract(left_high, left_low, right_high, right_low, width):
    rows = left_high.shape[0]
    main = matmul(jnp.concatenate([left_high, left_low], axis=0), right_high)
    both = main[:rows] + main[rows:] + matmul(left_high, right_low)
    half = rows // 2
    real = both[:half, :width] - both[half:, width:]
    imag = both[:half, width:] + both[half:, :width]
    return imag, -real


def window_ladder_kernel(own, near_ref, high_ref, low_ref):
    for k in range(own):
        regions = [[near_ref[2 * kind + part, k] for part in range(2)] for kind in range(2)]
        high_ref[k], low_ref[k] = halves(ladder(regions, TILE))


def window_kernel(own, arrived_ref, propagator_ref, high_ref, low_ref, send_ref):
    for k in range(own):
        pieces = coefficients(arrived_ref, propagator_ref.at[:, k], k, own)
        left_high, left_low = halves(jnp.concatenate([jnp.concatenate(pair, axis=1) for pair in pieces], axis=0))
        real, imag = contract(left_high, left_low, high_ref[k], low_ref[k], TILE)
        store_window(send_ref, k, own, real, imag)


def trade(tiles):
    group = lax.broadcasted_iota(jnp.int32, tiles[0].shape, 1) // ORB
    for bit in (2, 1):
        first = (group & bit) == 0
        shift = bit * ORB
        traded = list(tiles)
        for i in range(4):
            if not i & bit:
                x, y = tiles[i], tiles[i | bit]
                traded[i] = jnp.where(first, x, pltpu.roll(y, shift, 1))
                traded[i | bit] = jnp.where(first, pltpu.roll(x, TILE - shift, 1), y)
        tiles = traded
    return tiles


def final_ladder_kernel(tm_ref, retarded_ref, lesser_ref, rim_ref, high_out, low_out, region_ref, high_ref, low_ref, arrive, leave):
    own = high_ref.shape[0]
    momenta = pl.ds(tm_ref[0] * own, own)
    fetches = []
    for kind, ref in enumerate((retarded_ref, lesser_ref)):
        both = pl.ds(2 * kind, 2)
        fetches += start_all(
            [
                pltpu.make_async_copy(
                    ref.at[:, momenta], region_ref.at[both, :, :, pl.ds(TILE, ref.shape[3])], arrive.at[kind, 0]
                ),
                pltpu.make_async_copy(
                    rim_ref.at[both, momenta], region_ref.at[both, :, :, pl.ds(0, TILE)], arrive.at[kind, 1]
                ),
            ]
        )
    wait_all(fetches)

    def leaving(k):
        return [
            pltpu.make_async_copy(ref.at[k], out.at[k], leave.at[k, which])
            for which, (ref, out) in enumerate(((high_ref, high_out), (low_ref, low_out)))
        ]

    def one(k, carry):
        for part in range(2):
            region = jnp.concatenate([region_ref[2 * kind + part, k] for kind in range(2)], axis=0)
            lanes = pl.ds(part * TILE, TILE)
            for turn in range(3):
                from_lane = turn * 4 * ORB
                tiles = trade([region[:, from_lane + t * TILE : from_lane + (t + 1) * TILE] for t in range(4)])
                for step in range(4 * turn - 1, 4 * turn + 3):
                    if step >= 0:
                        high, low = halves(tiles[step - 4 * turn + 1])
                        for kind in range(2):
                            rows = pl.ds(step // 4 * TILE + kind * HALF + step % 4 * ORB, ORB)
                            high_ref[k, rows, lanes] = high[kind * ORB : (kind + 1) * ORB]
                            low_ref[k, rows, lanes] = low[kind * ORB : (kind + 1) * ORB]
            for kind in range(2):
                rows = pl.ds(2 * TILE + kind * HALF + 3 * ORB, ORB)
                high_ref[k, rows, lanes] = jnp.zeros((ORB, TILE), jnp.bfloat16)
                low_ref[k, rows, lanes] = jnp.zeros((ORB, TILE), jnp.bfloat16)
        start_all(leaving(k))
        return carry

    lax.fori_loop(0, own, one, 0)
    lax.fori_loop(0, own, lambda k, c: (wait_all(leaving(k)), c)[1], 0)


def stepped(pair):
    first, second = pair
    place = lax.broadcasted_iota(jnp.int32, first.shape, 1) // ORB % 4
    rows = [jnp.concatenate([first, second, jnp.zeros_like(first)], axis=1)]
    for s in range(1, 4):
        stay = place >= s
        up, over = s * ORB, TILE + (s - 4) * ORB
        rows.append(
            jnp.concatenate(
                [
                    jnp.where(stay, pltpu.roll(first, up, 1), 0.0),
                    jnp.where(stay, pltpu.roll(second, up, 1), pltpu.roll(first, over, 1)),
                    jnp.where(stay, 0.0, pltpu.roll(second, over, 1)),
                ],
                axis=1,
            )
        )
    return jnp.concatenate(rows, axis=0)


def final_kernel(own, before, tm_ref, arrived_ref, propagator_ref, high_ref, low_ref, *others):
    out_ref, high_here, low_here, out_here, arrive, leave = others[before:]
    base = tm_ref[0] * own

    group = own // 2

    def arriving(number):
        momenta = pl.ds(number * group, group)
        return [
            pltpu.make_async_copy(ref.at[momenta], here.at[momenta], arrive.at[number, which])
            for which, (ref, here) in enumerate(((high_ref, high_here), (low_ref, low_here)))
        ]

    def leaving(number):
        return [
            pltpu.make_async_copy(
                out_here.at[:, pl.ds(number * group, group)],
                out_ref.at[:, pl.ds(base + number * group, group)],
                leave.at[number],
            )
        ]

    def one(number, carry):
        wait_all(arriving(number))
        for n in range(group):
            k = number * group + n
            pieces = coefficients(arrived_ref, propagator_ref.at[:, base + k], k, own)
            left_high, left_low = halves(jnp.concatenate([stepped(pair) for pair in pieces], axis=0))
            parts = contract(left_high, left_low, high_here[k], low_here[k], TILE)
            for part, value in enumerate(parts):
                tiles = trade([value[s * ORB : (s + 1) * ORB] for s in range(4)])
                for t, tile in enumerate(tiles):
                    out_here[part, k, :, t * TILE : (t + 1) * TILE] = tile
        start_all(leaving(number))
        return carry

    for number in range(own // group):
        start_all(arriving(number))
    lax.fori_loop(0, own // group, one, 0)
    for number in range(own // group):
        wait_all(leaving(number))


def own_block(x, own, axis):
    return lax.dynamic_slice_in_dim(x, lax.axis_index("tm") * own, own, axis)


def on_device_tiled(hist_lesser, hist_retarded, propagator, coupling, mf_weight, lag_weight):
    both_axes = ("mom", "tm")
    momenta_here = hist_lesser.shape[1]
    columns = hist_lesser.shape[3]
    peers = lax.axis_size("tm")
    devices = lax.axis_size("mom") * peers
    own = momenta_here // peers
    count = KX * KY

    f32 = functools.partial(jax.ShapeDtypeStruct, dtype=jnp.float32)
    bf16 = functools.partial(jax.ShapeDtypeStruct, dtype=jnp.bfloat16)

    def call(kernel, shapes, *operands):
        return pl.pallas_call(
            kernel,
            out_shape=shapes,
            in_specs=[VMEM] * len(operands),
            out_specs=jax.tree.map(lambda _: VMEM, shapes),
            compiler_params=limit(12),
        )(*operands)

    half = momenta_here // 2
    sent = f32((devices * half, TILE))
    near_shape = f32((4, own, ORB, 2 * TILE))
    low, high, *near = pl.pallas_call(
        functools.partial(first_window_kernel, own),
        out_shape=(sent, sent, near_shape, near_shape),
        in_specs=[VMEM, IN_HBM, IN_HBM],
        out_specs=(VMEM,) * 4,
        scratch_shapes=[
            pltpu.VMEM((2, momenta_here, ORB, TILE), jnp.float32),
            pltpu.SemaphoreType.DMA((momenta_here // own,)),
            pltpu.SemaphoreType.DMA((2, 2)),
        ],
        compiler_params=limit(8),
    )(propagator, *(pltpu.with_memory_space_constraint(x, pltpu.HBM) for x in (hist_retarded, hist_lesser)))
    here = lax.axis_index("tm")
    last = here == peers - 1
    low = lax.ppermute(low, "tm", [(3, 2)])
    near = [lax.ppermute(block, "tm", [(3, tm)]) for tm, block in enumerate(near)]
    send = jnp.where(last, high, low).reshape(devices, half, TILE)
    send, hist_lesser, hist_retarded, coupling, mf_weight, lag_weight = lax.optimization_barrier(
        (send, hist_lesser, hist_retarded, coupling, mf_weight, lag_weight)
    )

    def near_of(tm):
        momenta = slice(tm * own, (tm + 1) * own)
        return jnp.concatenate([x[:, momenta, :, columns - 2 * TILE :] for x in (hist_retarded, hist_lesser)], axis=0)

    near.append(lax.ppermute(near_of(2), "tm", [(3, 2)]))
    rim = jnp.concatenate([x[..., columns - TILE :] for x in (hist_retarded, hist_lesser)], axis=0)
    rim = shifted(rim, "tm", 1)

    me = lax.axis_index("mom") * peers + lax.axis_index("tm")
    last_mark = (jnp.arange(W) == W - 1).astype(jnp.float32)
    strong = (coupling * coupling).reshape(ORB, 1, ORB) * lag_weight[:, None]
    mean = mf_weight.reshape(ORB, 1, ORB) * (lag_weight * last_mark)[:, None]
    strong = lax.dynamic_slice_in_dim(strong.reshape(devices, HALF), me, 1, 0)
    mean = lax.dynamic_slice_in_dim(mean.reshape(devices, HALF), me, 1, 0)
    strength = jnp.concatenate([strong, strong], axis=1)
    mean = jnp.concatenate([mean, jnp.zeros_like(mean)], axis=1)
    table_high, table_low = fourier_tables()

    ladders = []
    ladder_shape = (own, 3 * TILE, 2 * TILE)

    def beside(arrived, sent):
        _, retarded, lesser, edge = lax.optimization_barrier((sent, hist_retarded, hist_lesser, rim))
        momenta = (here ^ len(ladders)).reshape(1).astype(jnp.int32)
        ladder = pl.pallas_call(
            final_ladder_kernel,
            out_shape=(pltpu.HBM(ladder_shape, jnp.bfloat16),) * 2,
            in_specs=[SMEM, IN_HBM, IN_HBM, IN_HBM],
            out_specs=(IN_HBM, IN_HBM),
            scratch_shapes=[
                pltpu.VMEM((4, own, ORB, TILE + columns), jnp.float32),
                pltpu.VMEM(ladder_shape, jnp.bfloat16),
                pltpu.VMEM(ladder_shape, jnp.bfloat16),
                pltpu.SemaphoreType.DMA((2, 2)),
                pltpu.SemaphoreType.DMA((own, 2)),
            ],
            compiler_params=limit(6),
        )(momenta, *(pltpu.with_memory_space_constraint(x, pltpu.HBM) for x in (retarded, lesser, edge)))
        arrived, *ladder = lax.optimization_barrier((arrived, *ladder))
        ladders.append(ladder)
        return arrived

    for sweep in range(PASSES):
        arrived = lax.all_to_all(send, both_axes, 0, 0, tiled=True)
        if sweep == 0:
            arrived, *near[:2] = lax.optimization_barrier((arrived, *near[:2]))
        else:
            arrived = beside(arrived, send)
        back = call(
            fourier_kernel,
            f32((devices, 2 * own, TILE)),
            arrived.reshape(devices // peers, peers, -1, TILE),
            table_high,
            table_low,
            strength,
            mean,
        )
        if sweep == 0:
            near[2], _ = lax.optimization_barrier((near[2], back))
            mine = near_of(peers - 1)
            for tm, received in enumerate(near):
                mine = jnp.where(here == tm, received, mine)
            rungs = bf16((own, 2 * TILE, 2 * TILE))
            rungs = call(functools.partial(window_ladder_kernel, own), (rungs, rungs), mine)
            rim, *rungs = lax.optimization_barrier((rim, *rungs))
            propagator_own = own_block(propagator, own, 1)
        arrived = lax.all_to_all(back, both_axes, 0, 0, tiled=True)
        if sweep:
            arrived = beside(arrived, back)
        arrived = arrived.reshape(2 * count, TILE)
        if sweep + 1 < PASSES:
            send = call(
                functools.partial(window_kernel, own),
                f32((count, TILE)),
                arrived,
                propagator_own,
                *rungs,
            ).reshape(devices, own, TILE)

    def finish(new_slice, coefficients_of, step):
        before = () if new_slice is None else (new_slice,)
        return pl.pallas_call(
            functools.partial(final_kernel, own, len(before)),
            out_shape=pltpu.HBM(hist_lesser.shape, jnp.float32),
            in_specs=[SMEM, VMEM, VMEM] + [IN_HBM] * (2 + len(before)),
            out_specs=IN_HBM,
            scratch_shapes=[
                pltpu.VMEM(ladder_shape, jnp.bfloat16),
                pltpu.VMEM(ladder_shape, jnp.bfloat16),
                pltpu.VMEM((2, own, ORB, columns), jnp.float32),
                pltpu.SemaphoreType.DMA((own, 2)),
                pltpu.SemaphoreType.DMA((own,)),
            ],
            input_output_aliases={5: 0} if before else {},
            compiler_params=limit(6),
        )(
            (here ^ step).reshape(1).astype(jnp.int32),
            coefficients_of,
            propagator,
            *[pltpu.with_memory_space_constraint(x, pltpu.HBM) for x in ladders[step]],
            *before,
        )

    def exchange(x, step):
        return lax.ppermute(x, "tm", [(t, t ^ step) for t in range(peers)])

    across = exchange(arrived, 2)
    beside_me = exchange(arrived, 1)
    new_slice = finish(None, arrived, 0)
    new_slice = finish(new_slice, beside_me, 1)
    across, new_slice = lax.optimization_barrier((across, new_slice))
    beyond = exchange(across, 1)
    new_slice = finish(new_slice, across, 2)
    return finish(new_slice, beyond, 3)


def on_device(hist_lesser, *others):
    peers = lax.axis_size("tm")
    devices = lax.axis_size("mom") * peers
    fits = devices == 2 * ORB and peers == 4 and hist_lesser.shape[1:] == (2 * ORB, ORB, 4 * TILE)
    return (on_device_tiled if fits else on_device_any)(hist_lesser, *others)


def solution(mesh):
    return jax.shard_map(
        on_device,
        mesh=mesh,
        in_specs=(
            P(None, "mom", None, "tm"),
            P(None, "mom", None, "tm"),
            P(None, "mom", None, None),
            P(),
            P(),
            P(),
        ),
        out_specs=P(None, "mom", None, "tm"),
        check_vma=False,
    )
```

```python
import functools
import math

import jax
import jax.numpy as jnp
import numpy as np
from jax import lax
from jax.experimental import pallas as pl
from jax.experimental.pallas import tpu as pltpu
from jax.sharding import PartitionSpec as P

KX = 16
KY = 16
ORB = 16
W = 8
PASSES = 3


HIGHEST = lax.Precision.HIGHEST


def shifted(x, axis, by):
    peers = lax.axis_size(axis)
    pairs = [(i, i + by) for i in range(peers) if 0 <= i + by < peers]
    return lax.ppermute(x, axis, pairs)


def broadcast(x, axis, root):
    mine = lax.axis_index(axis) == root
    return lax.psum(jnp.where(mine, x, jnp.zeros_like(x)), axis)


def momentum_tables():
    index = jnp.arange(KX * KY, dtype=jnp.int32)
    first = index // KY
    second = index % KY
    turn_x = first[:, None] * first[None, :] % KX
    turn_y = second[:, None] * second[None, :] % KY
    phase = 2.0 * math.pi * (turn_x.astype(jnp.float32) / KX + turn_y.astype(jnp.float32) / KY)
    scale = 1.0 / math.sqrt(KX * KY)
    return (jnp.cos(phase) * scale, jnp.sin(phase) * scale)


def complex_product(pattern, first, second):
    real = jnp.einsum(pattern, first[0], second[0], precision=HIGHEST) - jnp.einsum(
        pattern, first[1], second[1], precision=HIGHEST
    )
    imaginary = jnp.einsum(pattern, first[0], second[1], precision=HIGHEST) + jnp.einsum(
        pattern, first[1], second[0], precision=HIGHEST
    )
    return jnp.stack([real, imaginary])


def back_to_momenta(real, imaginary, cosine, sine):
    out_real = jnp.dot(cosine, real, precision=HIGHEST) + jnp.dot(
        sine, imaginary, precision=HIGHEST
    )
    out_imag = jnp.dot(cosine, imaginary, precision=HIGHEST) - jnp.dot(
        sine, real, precision=HIGHEST
    )
    return jnp.stack([out_real, out_imag])


def local_products(arrived, cosine, sine, strength, lag_mark):
    lag_count = lag_mark.shape[0]
    space_real = jnp.dot(cosine, arrived[0], precision=HIGHEST) - jnp.dot(
        sine, arrived[1], precision=HIGHEST
    )
    space_imag = jnp.dot(cosine, arrived[1], precision=HIGHEST) + jnp.dot(
        sine, arrived[0], precision=HIGHEST
    )
    column_strength = jnp.repeat(strength, lag_count)
    magnitude = column_strength * (space_real * space_real + space_imag * space_imag)
    lesser_real = magnitude * space_real
    lesser_imag = magnitude * space_imag
    pair_real = column_strength * (space_real * space_real - space_imag * space_imag)
    pair_imag = column_strength * 2.0 * space_real * space_imag
    return (
        back_to_momenta(lesser_real, lesser_imag, cosine, sine),
        back_to_momenta(pair_real, pair_imag, cosine, sine),
    )


def self_energies(window, cosine, sine, strength, mf_weight, last_mark):
    momenta_here = window.shape[1]
    outgoing = window.reshape(2, momenta_here, ORB * ORB * W)
    arrived = lax.all_to_all(outgoing, "mom", split_axis=2, concat_axis=1, tiled=True)
    lesser_r, pair_r = local_products(arrived, cosine, sine, strength, last_mark)
    back_lesser, back_pair = (
        lax.all_to_all(lesser_r, "mom", split_axis=1, concat_axis=2, tiled=True),
        lax.all_to_all(pair_r, "mom", split_axis=1, concat_axis=2, tiled=True),
    )
    sigma = back_lesser.reshape(2, momenta_here, ORB, ORB, W)
    pair_k = back_pair.reshape(2, momenta_here, ORB, ORB, W)
    own_total = jnp.sum(window[..., W - 1], axis=1)
    occupation = lax.psum(own_total, "mom") / (KX * KY)
    sigma = sigma + (mf_weight.reshape(ORB, ORB) * occupation)[:, None, :, :, None] * last_mark
    return (sigma, pair_k)


def collide(sigma, pair_k, lag_weight, padded_r, padded_l, first, count):
    weighted_sigma = sigma * lag_weight
    weighted_pair = pair_k * lag_weight

    def ladder(padded):
        region = lax.dynamic_slice_in_dim(padded, first * ORB, (count + W - 1) * ORB, 3)
        return jnp.stack(
            [region[..., offset * ORB : (offset + count) * ORB] for offset in range(W)], axis=3
        )

    return complex_product("kabm,kbmx->kax", weighted_sigma, ladder(padded_r)) + complex_product(
        "kabm,kbmx->kax", weighted_pair, ladder(padded_l)
    )


def on_device_any(hist_lesser, hist_retarded, propagator, coupling, mf_weight, lag_weight):
    momenta_here = hist_lesser.shape[1]
    times_here = hist_lesser.shape[3] // ORB
    cosine, sine = momentum_tables()
    lesser = hist_lesser.reshape(2, momenta_here, ORB, times_here, ORB)
    start = complex_product("kab,kbjc->kajc", propagator, lesser).reshape(
        2, momenta_here, ORB, times_here * ORB
    )
    rim_width = (W - 1) * ORB
    rim_retarded, rim_lesser = shifted(
        (
            hist_retarded[..., times_here * ORB - rim_width :],
            hist_lesser[..., times_here * ORB - rim_width :],
        ),
        "tm",
        1,
    )
    padded_r = jnp.concatenate([rim_retarded, hist_retarded], axis=3)
    padded_l = jnp.concatenate([rim_lesser, hist_lesser], axis=3)
    block = min(32, times_here)
    count_blocks = times_here // block
    window_start = (times_here - W) * ORB
    pair_count = ORB * ORB // lax.axis_size("mom")
    strength = lax.dynamic_slice_in_dim(
        coupling * coupling, lax.axis_index("mom") * pair_count, pair_count, 0
    )
    last_mark = (jnp.arange(W) == W - 1).astype(jnp.float32)
    owner = lax.axis_size("tm") - 1
    current = start[..., window_start:]
    full_slice = start
    for sweep in range(PASSES):
        shared = broadcast(current, "tm", owner)
        window = jnp.transpose(shared.reshape(2, momenta_here, ORB, W, ORB), (0, 1, 2, 4, 3))
        sigma, pair_k = self_energies(window, cosine, sine, strength, mf_weight, last_mark)
        if sweep + 1 < PASSES:
            collision = collide(sigma, pair_k, lag_weight, padded_r, padded_l, times_here - W, W)
            current = start[..., window_start:] + jnp.stack([collision[1], -collision[0]])
        else:
            blocks_out = lax.map(
                lambda number: collide(
                    sigma, pair_k, lag_weight, padded_r, padded_l, number * block, block
                ),
                jnp.arange(count_blocks, dtype=jnp.int32),
            )
            collision = jnp.moveaxis(blocks_out, 0, 3).reshape(
                2, momenta_here, ORB, times_here * ORB
            )
            full_slice = start + jnp.stack([collision[1], -collision[0]])
            current = full_slice[..., window_start:]
    return full_slice


VMEM = pl.BlockSpec(memory_space=pltpu.VMEM)
SMEM = pl.BlockSpec(memory_space=pltpu.SMEM)
IN_HBM = pl.BlockSpec(memory_space=pltpu.HBM)
HALF = W * ORB // 2
TILE = W * ORB


def limit(mebibytes):
    return pltpu.CompilerParams(vmem_limit_bytes=mebibytes * 1024 * 1024)


def halves(x):
    high = x.astype(jnp.bfloat16)
    return high, (x - high.astype(jnp.float32)).astype(jnp.bfloat16)


def matmul(first, second):
    return jnp.dot(first, second, preferred_element_type=jnp.float32)


def fourier_tables():
    index = np.arange(KX * KY)
    turn = np.outer(index // KY, index // KY) / KX + np.outer(index % KY, index % KY) / KY
    phase = 2.0 * np.pi * (turn % 1.0)
    table = np.concatenate([np.cos(phase), np.sin(phase)]) / math.sqrt(KX * KY)
    high = table.astype(jnp.bfloat16)
    low = (table - high.astype(np.float64)).astype(jnp.bfloat16)
    return jnp.asarray(high), jnp.asarray(low)


def lower_lanes(shape):
    return lax.broadcasted_iota(jnp.int32, shape, 1) < HALF


def store_window(send_ref, k, own, real, imag):
    lower = lower_lanes(real.shape)
    turned_real = pltpu.roll(real, HALF, 1)
    turned_imag = pltpu.roll(imag, HALF, 1)
    send_ref[pl.ds(k, ORB, stride=2 * own), :] = jnp.where(lower, real, turned_imag)
    send_ref[pl.ds(own + k, ORB, stride=2 * own), :] = jnp.where(lower, turned_real, imag)


def start_all(copies):
    for copy in copies:
        copy.start()
    return copies


def wait_all(copies):
    for copy in copies:
        copy.wait()


def first_window_kernel(own, propagator_ref, retarded_ref, lesser_ref, low_ref, high_ref, *others):
    *near_refs, rim_ref, window_ref, arrive, pass_on = others
    momenta, columns = lesser_ref.shape[1], lesser_ref.shape[3]
    half = momenta // 2
    fetches = start_all(
        [
            pltpu.make_async_copy(
                lesser_ref.at[:, first : first + own, :, columns - TILE :],
                window_ref.at[:, first : first + own],
                arrive.at[number],
            )
            for number, first in enumerate(range(0, momenta, own))
        ]
    )
    copies = []
    for kind, ref in enumerate((retarded_ref, lesser_ref)):
        both = pl.ds(2 * kind, 2)
        for tm, near_ref in enumerate(near_refs):
            source = ref.at[:, tm * own : (tm + 1) * own, :, columns - 2 * TILE :]
            copies.append(pltpu.make_async_copy(source, near_ref.at[both], pass_on.at[kind, tm]))
        copies.append(
            pltpu.make_async_copy(ref.at[:, :, :, columns - TILE :], rim_ref.at[both], pass_on.at[kind, len(near_refs)])
        )
    start_all(copies)
    for number, fetch in enumerate(fetches):
        fetch.wait()
        for k in range(number * own, (number + 1) * own):
            left = jnp.concatenate([propagator_ref[0, k], propagator_ref[1, k]], axis=0)
            right = jnp.concatenate([window_ref[0, k], window_ref[1, k]], axis=1)
            imag, real = contract(*halves(left), *halves(right), TILE)
            store_window(low_ref if k < half else high_ref, k % half, half, -real, imag)
    wait_all(copies)


def fourier_kernel(arrived_ref, high_ref, low_ref, strength_ref, mean_ref, out_ref):
    count = KX * KY
    useful = count // (arrived_ref.shape[0] * arrived_ref.shape[2])
    x_high, x_low = halves(arrived_ref[:, arrived_ref.shape[1] - useful :].reshape(count, TILE))
    main = matmul(high_ref[...], jnp.concatenate([x_high, x_low], axis=1))
    turned = main[:, :TILE] + main[:, TILE:] + matmul(low_ref[...], x_high)
    lower = lower_lanes((count, TILE))
    sine_part = pltpu.roll(turned[count:], HALF, 1)
    here = turned[:count] + jnp.where(lower, -sine_part, sine_part)
    swapped = pltpu.roll(here, HALF, 1)
    real = jnp.where(lower, here, swapped)
    imag = jnp.where(lower, swapped, here)
    real_square = real * real
    imag_square = imag * imag
    size = real_square + imag_square
    strength = strength_ref[...]
    out_real = strength * jnp.where(lower, size * real, real_square - imag_square)
    out_imag = strength * jnp.where(lower, size * imag, 2.0 * real * imag)
    origin = (lax.broadcasted_iota(jnp.int32, (count, TILE), 0) == 0).astype(jnp.float32)
    mean = origin * mean_ref[...]
    out_real = out_real + mean * real
    out_imag = out_imag + mean * imag
    real_high, real_low = halves(out_real)
    imag_high, imag_low = halves(out_imag)
    y_high = jnp.concatenate([real_high, imag_high], axis=1)
    y_low = jnp.concatenate([real_low, imag_low], axis=1)
    back = matmul(high_ref[...], y_high) + matmul(low_ref[...], y_high) + matmul(high_ref[...], y_low)
    devices, rows, _ = out_ref.shape
    own = rows // 2
    out_ref[:, :own] = (back[:count, :TILE] + back[count:, TILE:]).reshape(devices, own, TILE)
    out_ref[:, own:] = (back[:count, TILE:] - back[count:, :TILE]).reshape(devices, own, TILE)


def coefficients(arrived_ref, propagator_ref, k, own):
    pieces = []
    for part, start in enumerate((-propagator_ref[1], propagator_ref[0])):
        first, second = (
            arrived_ref[pl.ds((2 * half + part) * own + k, ORB, stride=4 * own), :] for half in range(2)
        )
        start = jnp.concatenate([jnp.zeros((ORB, TILE - ORB), jnp.float32), start], axis=1)
        pieces.append((first, second + start))
    return pieces


def ladder(regions, width):
    rows = []
    for half in range(2):
        for kind in range(2):
            for lag in range(W // 2):
                offset = ORB * (1 + half * (W // 2) + lag)
                rows.append(jnp.concatenate([x[:, offset : offset + width] for x in regions[kind]], axis=1))
    return jnp.concatenate(rows, axis=0)


def contract(left_high, left_low, right_high, right_low, width):
    rows = left_high.shape[0]
    main = matmul(jnp.concatenate([left_high, left_low], axis=0), right_high)
    both = main[:rows] + main[rows:] + matmul(left_high, right_low)
    half = rows // 2
    real = both[:half, :width] - both[half:, width:]
    imag = both[:half, width:] + both[half:, :width]
    return imag, -real


def window_ladder_kernel(own, near_ref, high_ref, low_ref):
    for k in range(own):
        regions = [[near_ref[2 * kind + part, k] for part in range(2)] for kind in range(2)]
        high_ref[k], low_ref[k] = halves(ladder(regions, TILE))


def window_kernel(own, arrived_ref, propagator_ref, high_ref, low_ref, send_ref):
    for k in range(own):
        pieces = coefficients(arrived_ref, propagator_ref.at[:, k], k, own)
        left_high, left_low = halves(jnp.concatenate([jnp.concatenate(pair, axis=1) for pair in pieces], axis=0))
        real, imag = contract(left_high, left_low, high_ref[k], low_ref[k], TILE)
        store_window(send_ref, k, own, real, imag)


def trade(tiles):
    group = lax.broadcasted_iota(jnp.int32, tiles[0].shape, 1) // ORB
    for bit in (2, 1):
        first = (group & bit) == 0
        shift = bit * ORB
        traded = list(tiles)
        for i in range(4):
            if not i & bit:
                x, y = tiles[i], tiles[i | bit]
                traded[i] = jnp.where(first, x, pltpu.roll(y, shift, 1))
                traded[i | bit] = jnp.where(first, pltpu.roll(x, TILE - shift, 1), y)
        tiles = traded
    return tiles


def final_ladder_kernel(tm_ref, retarded_ref, lesser_ref, rim_ref, high_out, low_out, region_ref, high_ref, low_ref, arrive, leave):
    own = high_ref.shape[0]
    momenta = pl.ds(tm_ref[0] * own, own)
    fetches = []
    for kind, ref in enumerate((retarded_ref, lesser_ref)):
        both = pl.ds(2 * kind, 2)
        fetches += start_all(
            [
                pltpu.make_async_copy(
                    ref.at[:, momenta], region_ref.at[both, :, :, pl.ds(TILE, ref.shape[3])], arrive.at[kind, 0]
                ),
                pltpu.make_async_copy(
                    rim_ref.at[both, momenta], region_ref.at[both, :, :, pl.ds(0, TILE)], arrive.at[kind, 1]
                ),
            ]
        )
    wait_all(fetches)

    def leaving(k):
        return [
            pltpu.make_async_copy(ref.at[k], out.at[k], leave.at[k, which])
            for which, (ref, out) in enumerate(((high_ref, high_out), (low_ref, low_out)))
        ]

    def one(k, carry):
        for part in range(2):
            region = jnp.concatenate([region_ref[2 * kind + part, k] for kind in range(2)], axis=0)
            lanes = pl.ds(part * TILE, TILE)
            for turn in range(3):
                from_lane = turn * 4 * ORB
                tiles = trade([region[:, from_lane + t * TILE : from_lane + (t + 1) * TILE] for t in range(4)])
                for step in range(4 * turn - 1, 4 * turn + 3):
                    if step >= 0:
                        high, low = halves(tiles[step - 4 * turn + 1])
                        for kind in range(2):
                            rows = pl.ds(step // 4 * TILE + kind * HALF + step % 4 * ORB, ORB)
                            high_ref[k, rows, lanes] = high[kind * ORB : (kind + 1) * ORB]
                            low_ref[k, rows, lanes] = low[kind * ORB : (kind + 1) * ORB]
            for kind in range(2):
                rows = pl.ds(2 * TILE + kind * HALF + 3 * ORB, ORB)
                high_ref[k, rows, lanes] = jnp.zeros((ORB, TILE), jnp.bfloat16)
                low_ref[k, rows, lanes] = jnp.zeros((ORB, TILE), jnp.bfloat16)
        start_all(leaving(k))
        return carry

    lax.fori_loop(0, own, one, 0)
    lax.fori_loop(0, own, lambda k, c: (wait_all(leaving(k)), c)[1], 0)


def stepped(pair):
    first, second = pair
    place = lax.broadcasted_iota(jnp.int32, first.shape, 1) // ORB % 4
    rows = [jnp.concatenate([first, second, jnp.zeros_like(first)], axis=1)]
    for s in range(1, 4):
        stay = place >= s
        up, over = s * ORB, TILE + (s - 4) * ORB
        rows.append(
            jnp.concatenate(
                [
                    jnp.where(stay, pltpu.roll(first, up, 1), 0.0),
                    jnp.where(stay, pltpu.roll(second, up, 1), pltpu.roll(first, over, 1)),
                    jnp.where(stay, 0.0, pltpu.roll(second, over, 1)),
                ],
                axis=1,
            )
        )
    return jnp.concatenate(rows, axis=0)


def final_kernel(own, before, tm_ref, arrived_ref, propagator_ref, high_ref, low_ref, *others):
    out_ref, high_here, low_here, out_here, arrive, leave = others[before:]
    base = tm_ref[0] * own

    group = own // 2

    def arriving(number):
        momenta = pl.ds(number * group, group)
        return [
            pltpu.make_async_copy(ref.at[momenta], here.at[momenta], arrive.at[number, which])
            for which, (ref, here) in enumerate(((high_ref, high_here), (low_ref, low_here)))
        ]

    def leaving(number):
        return [
            pltpu.make_async_copy(
                out_here.at[:, pl.ds(number * group, group)],
                out_ref.at[:, pl.ds(base + number * group, group)],
                leave.at[number],
            )
        ]

    def one(number, carry):
        wait_all(arriving(number))
        for n in range(group):
            k = number * group + n
            pieces = coefficients(arrived_ref, propagator_ref.at[:, base + k], k, own)
            left_high, left_low = halves(jnp.concatenate([stepped(pair) for pair in pieces], axis=0))
            parts = contract(left_high, left_low, high_here[k], low_here[k], TILE)
            for part, value in enumerate(parts):
                tiles = trade([value[s * ORB : (s + 1) * ORB] for s in range(4)])
                for t, tile in enumerate(tiles):
                    out_here[part, k, :, t * TILE : (t + 1) * TILE] = tile
        start_all(leaving(number))
        return carry

    for number in range(own // group):
        start_all(arriving(number))
    lax.fori_loop(0, own // group, one, 0)
    for number in range(own // group):
        wait_all(leaving(number))


def own_block(x, own, axis):
    return lax.dynamic_slice_in_dim(x, lax.axis_index("tm") * own, own, axis)


def on_device_tiled(hist_lesser, hist_retarded, propagator, coupling, mf_weight, lag_weight):
    both_axes = ("mom", "tm")
    momenta_here = hist_lesser.shape[1]
    columns = hist_lesser.shape[3]
    peers = lax.axis_size("tm")
    devices = lax.axis_size("mom") * peers
    own = momenta_here // peers
    count = KX * KY

    f32 = functools.partial(jax.ShapeDtypeStruct, dtype=jnp.float32)
    bf16 = functools.partial(jax.ShapeDtypeStruct, dtype=jnp.bfloat16)

    def call(kernel, shapes, *operands):
        return pl.pallas_call(
            kernel,
            out_shape=shapes,
            in_specs=[VMEM] * len(operands),
            out_specs=jax.tree.map(lambda _: VMEM, shapes),
            compiler_params=limit(12),
        )(*operands)

    half = momenta_here // 2
    sent = f32((devices * half, TILE))
    near_shape = f32((4, own, ORB, 2 * TILE))
    low, high, *near, rim = pl.pallas_call(
        functools.partial(first_window_kernel, own),
        out_shape=(sent, sent, *[near_shape] * peers, f32((4, momenta_here, ORB, TILE))),
        in_specs=[VMEM, IN_HBM, IN_HBM],
        out_specs=(VMEM,) * (peers + 3),
        scratch_shapes=[
            pltpu.VMEM((2, momenta_here, ORB, TILE), jnp.float32),
            pltpu.SemaphoreType.DMA((peers,)),
            pltpu.SemaphoreType.DMA((2, peers + 1)),
        ],
        compiler_params=limit(8),
    )(propagator, *(pltpu.with_memory_space_constraint(x, pltpu.HBM) for x in (hist_retarded, hist_lesser)))
    here = lax.axis_index("tm")
    last = here == peers - 1
    low = lax.ppermute(low, "tm", [(3, 2)])
    mine = near.pop()
    near[:2] = [lax.ppermute(block, "tm", [(3, tm)]) for tm, block in enumerate(near[:2])]
    send = jnp.where(last, high, low).reshape(devices, half, TILE)
    send, near[2], rim, hist_lesser, hist_retarded, coupling, mf_weight, lag_weight = lax.optimization_barrier(
        (send, near[2], rim, hist_lesser, hist_retarded, coupling, mf_weight, lag_weight)
    )
    near[2] = lax.ppermute(near[2], "tm", [(3, 2)])
    rim = shifted(rim, "tm", 1)
    me = lax.axis_index("mom") * peers + lax.axis_index("tm")
    last_mark = (jnp.arange(W) == W - 1).astype(jnp.float32)
    strong = (coupling * coupling).reshape(ORB, 1, ORB) * lag_weight[:, None]
    mean = mf_weight.reshape(ORB, 1, ORB) * (lag_weight * last_mark)[:, None]
    strong = lax.dynamic_slice_in_dim(strong.reshape(devices, HALF), me, 1, 0)
    mean = lax.dynamic_slice_in_dim(mean.reshape(devices, HALF), me, 1, 0)
    strength = jnp.concatenate([strong, strong], axis=1)
    mean = jnp.concatenate([mean, jnp.zeros_like(mean)], axis=1)
    table_high, table_low = fourier_tables()

    ladders = []
    ladder_shape = (own, 3 * TILE, 2 * TILE)

    def beside(arrived, sent):
        _, retarded, lesser, edge = lax.optimization_barrier((sent, hist_retarded, hist_lesser, rim))
        momenta = (here ^ len(ladders)).reshape(1).astype(jnp.int32)
        ladder = pl.pallas_call(
            final_ladder_kernel,
            out_shape=(pltpu.HBM(ladder_shape, jnp.bfloat16),) * 2,
            in_specs=[SMEM, IN_HBM, IN_HBM, IN_HBM],
            out_specs=(IN_HBM, IN_HBM),
            scratch_shapes=[
                pltpu.VMEM((4, own, ORB, TILE + columns), jnp.float32),
                pltpu.VMEM(ladder_shape, jnp.bfloat16),
                pltpu.VMEM(ladder_shape, jnp.bfloat16),
                pltpu.SemaphoreType.DMA((2, 2)),
                pltpu.SemaphoreType.DMA((own, 2)),
            ],
            compiler_params=limit(6),
        )(momenta, *(pltpu.with_memory_space_constraint(x, pltpu.HBM) for x in (retarded, lesser, edge)))
        arrived, *ladder = lax.optimization_barrier((arrived, *ladder))
        ladders.append(ladder)
        return arrived

    for sweep in range(PASSES):
        arrived = lax.all_to_all(send, both_axes, 0, 0, tiled=True)
        if sweep == 0:
            arrived, *near[:2] = lax.optimization_barrier((arrived, *near[:2]))
        else:
            arrived = beside(arrived, send)
        back = call(
            fourier_kernel,
            f32((devices, 2 * own, TILE)),
            arrived.reshape(devices // peers, peers, -1, TILE),
            table_high,
            table_low,
            strength,
            mean,
        )
        if sweep == 0:
            near[2], _ = lax.optimization_barrier((near[2], back))
            for tm, received in enumerate(near):
                mine = jnp.where(here == tm, received, mine)
            rungs = bf16((own, 2 * TILE, 2 * TILE))
            rungs = call(functools.partial(window_ladder_kernel, own), (rungs, rungs), mine)
            rim, *rungs = lax.optimization_barrier((rim, *rungs))
            propagator_own = own_block(propagator, own, 1)
        arrived = lax.all_to_all(back, both_axes, 0, 0, tiled=True)
        if sweep + 1 < PASSES:
            arrived = beside(arrived, back)
        arrived = arrived.reshape(2 * count, TILE)
        if sweep + 1 < PASSES:
            send = call(
                functools.partial(window_kernel, own),
                f32((count, TILE)),
                arrived,
                propagator_own,
                *rungs,
            ).reshape(devices, own, TILE)

    def finish(new_slice, coefficients_of, step):
        before = () if new_slice is None else (new_slice,)
        return pl.pallas_call(
            functools.partial(final_kernel, own, len(before)),
            out_shape=pltpu.HBM(hist_lesser.shape, jnp.float32),
            in_specs=[SMEM, VMEM, VMEM] + [IN_HBM] * (2 + len(before)),
            out_specs=IN_HBM,
            scratch_shapes=[
                pltpu.VMEM(ladder_shape, jnp.bfloat16),
                pltpu.VMEM(ladder_shape, jnp.bfloat16),
                pltpu.VMEM((2, own, ORB, columns), jnp.float32),
                pltpu.SemaphoreType.DMA((own, 2)),
                pltpu.SemaphoreType.DMA((own,)),
            ],
            input_output_aliases={5: 0} if before else {},
            compiler_params=limit(6),
        )(
            (here ^ step).reshape(1).astype(jnp.int32),
            coefficients_of,
            propagator,
            *[pltpu.with_memory_space_constraint(x, pltpu.HBM) if step == 0 else x for x in ladders[step]],
            *before,
        )

    def exchange(x, step):
        return lax.ppermute(x, "tm", [(t, t ^ step) for t in range(peers)])

    across = exchange(arrived, 2)
    beside_me = exchange(arrived, 1)
    new_slice = finish(None, arrived, 0)
    new_slice = finish(new_slice, beside_me, 1)
    across, new_slice = lax.optimization_barrier((across, new_slice))
    beyond = exchange(across, 1)
    new_slice = finish(new_slice, across, 2)
    return finish(new_slice, beyond, 3)


def on_device(hist_lesser, *others):
    peers = lax.axis_size("tm")
    devices = lax.axis_size("mom") * peers
    fits = devices == 2 * ORB and peers == 4 and hist_lesser.shape[1:] == (2 * ORB, ORB, 4 * TILE)
    return (on_device_tiled if fits else on_device_any)(hist_lesser, *others)


def solution(mesh):
    return jax.shard_map(
        on_device,
        mesh=mesh,
        in_specs=(
            P(None, "mom", None, "tm"),
            P(None, "mom", None, "tm"),
            P(None, "mom", None, None),
            P(),
            P(),
            P(),
        ),
        out_specs=P(None, "mom", None, "tm"),
        check_vma=False,
    )
```

```python
import functools
import math

import jax
import jax.numpy as jnp
import numpy as np
from jax import lax
from jax.experimental import pallas as pl
from jax.experimental.pallas import tpu as pltpu
from jax.sharding import PartitionSpec as P

KX = 16
KY = 16
ORB = 16
W = 8
PASSES = 3


HIGHEST = lax.Precision.HIGHEST


def shifted(x, axis, by):
    peers = lax.axis_size(axis)
    pairs = [(i, i + by) for i in range(peers) if 0 <= i + by < peers]
    return lax.ppermute(x, axis, pairs)


def broadcast(x, axis, root):
    mine = lax.axis_index(axis) == root
    return lax.psum(jnp.where(mine, x, jnp.zeros_like(x)), axis)


def momentum_tables():
    index = jnp.arange(KX * KY, dtype=jnp.int32)
    first = index // KY
    second = index % KY
    turn_x = first[:, None] * first[None, :] % KX
    turn_y = second[:, None] * second[None, :] % KY
    phase = 2.0 * math.pi * (turn_x.astype(jnp.float32) / KX + turn_y.astype(jnp.float32) / KY)
    scale = 1.0 / math.sqrt(KX * KY)
    return (jnp.cos(phase) * scale, jnp.sin(phase) * scale)


def complex_product(pattern, first, second):
    real = jnp.einsum(pattern, first[0], second[0], precision=HIGHEST) - jnp.einsum(
        pattern, first[1], second[1], precision=HIGHEST
    )
    imaginary = jnp.einsum(pattern, first[0], second[1], precision=HIGHEST) + jnp.einsum(
        pattern, first[1], second[0], precision=HIGHEST
    )
    return jnp.stack([real, imaginary])


def back_to_momenta(real, imaginary, cosine, sine):
    out_real = jnp.dot(cosine, real, precision=HIGHEST) + jnp.dot(
        sine, imaginary, precision=HIGHEST
    )
    out_imag = jnp.dot(cosine, imaginary, precision=HIGHEST) - jnp.dot(
        sine, real, precision=HIGHEST
    )
    return jnp.stack([out_real, out_imag])


def local_products(arrived, cosine, sine, strength, lag_mark):
    lag_count = lag_mark.shape[0]
    space_real = jnp.dot(cosine, arrived[0], precision=HIGHEST) - jnp.dot(
        sine, arrived[1], precision=HIGHEST
    )
    space_imag = jnp.dot(cosine, arrived[1], precision=HIGHEST) + jnp.dot(
        sine, arrived[0], precision=HIGHEST
    )
    column_strength = jnp.repeat(strength, lag_count)
    magnitude = column_strength * (space_real * space_real + space_imag * space_imag)
    lesser_real = magnitude * space_real
    lesser_imag = magnitude * space_imag
    pair_real = column_strength * (space_real * space_real - space_imag * space_imag)
    pair_imag = column_strength * 2.0 * space_real * space_imag
    return (
        back_to_momenta(lesser_real, lesser_imag, cosine, sine),
        back_to_momenta(pair_real, pair_imag, cosine, sine),
    )


def self_energies(window, cosine, sine, strength, mf_weight, last_mark):
    momenta_here = window.shape[1]
    outgoing = window.reshape(2, momenta_here, ORB * ORB * W)
    arrived = lax.all_to_all(outgoing, "mom", split_axis=2, concat_axis=1, tiled=True)
    lesser_r, pair_r = local_products(arrived, cosine, sine, strength, last_mark)
    back_lesser, back_pair = (
        lax.all_to_all(lesser_r, "mom", split_axis=1, concat_axis=2, tiled=True),
        lax.all_to_all(pair_r, "mom", split_axis=1, concat_axis=2, tiled=True),
    )
    sigma = back_lesser.reshape(2, momenta_here, ORB, ORB, W)
    pair_k = back_pair.reshape(2, momenta_here, ORB, ORB, W)
    own_total = jnp.sum(window[..., W - 1], axis=1)
    occupation = lax.psum(own_total, "mom") / (KX * KY)
    sigma = sigma + (mf_weight.reshape(ORB, ORB) * occupation)[:, None, :, :, None] * last_mark
    return (sigma, pair_k)


def collide(sigma, pair_k, lag_weight, padded_r, padded_l, first, count):
    weighted_sigma = sigma * lag_weight
    weighted_pair = pair_k * lag_weight

    def ladder(padded):
        region = lax.dynamic_slice_in_dim(padded, first * ORB, (count + W - 1) * ORB, 3)
        return jnp.stack(
            [region[..., offset * ORB : (offset + count) * ORB] for offset in range(W)], axis=3
        )

    return complex_product("kabm,kbmx->kax", weighted_sigma, ladder(padded_r)) + complex_product(
        "kabm,kbmx->kax", weighted_pair, ladder(padded_l)
    )


def on_device_any(hist_lesser, hist_retarded, propagator, coupling, mf_weight, lag_weight):
    momenta_here = hist_lesser.shape[1]
    times_here = hist_lesser.shape[3] // ORB
    cosine, sine = momentum_tables()
    lesser = hist_lesser.reshape(2, momenta_here, ORB, times_here, ORB)
    start = complex_product("kab,kbjc->kajc", propagator, lesser).reshape(
        2, momenta_here, ORB, times_here * ORB
    )
    rim_width = (W - 1) * ORB
    rim_retarded, rim_lesser = shifted(
        (
            hist_retarded[..., times_here * ORB - rim_width :],
            hist_lesser[..., times_here * ORB - rim_width :],
        ),
        "tm",
        1,
    )
    padded_r = jnp.concatenate([rim_retarded, hist_retarded], axis=3)
    padded_l = jnp.concatenate([rim_lesser, hist_lesser], axis=3)
    block = min(32, times_here)
    count_blocks = times_here // block
    window_start = (times_here - W) * ORB
    pair_count = ORB * ORB // lax.axis_size("mom")
    strength = lax.dynamic_slice_in_dim(
        coupling * coupling, lax.axis_index("mom") * pair_count, pair_count, 0
    )
    last_mark = (jnp.arange(W) == W - 1).astype(jnp.float32)
    owner = lax.axis_size("tm") - 1
    current = start[..., window_start:]
    full_slice = start
    for sweep in range(PASSES):
        shared = broadcast(current, "tm", owner)
        window = jnp.transpose(shared.reshape(2, momenta_here, ORB, W, ORB), (0, 1, 2, 4, 3))
        sigma, pair_k = self_energies(window, cosine, sine, strength, mf_weight, last_mark)
        if sweep + 1 < PASSES:
            collision = collide(sigma, pair_k, lag_weight, padded_r, padded_l, times_here - W, W)
            current = start[..., window_start:] + jnp.stack([collision[1], -collision[0]])
        else:
            blocks_out = lax.map(
                lambda number: collide(
                    sigma, pair_k, lag_weight, padded_r, padded_l, number * block, block
                ),
                jnp.arange(count_blocks, dtype=jnp.int32),
            )
            collision = jnp.moveaxis(blocks_out, 0, 3).reshape(
                2, momenta_here, ORB, times_here * ORB
            )
            full_slice = start + jnp.stack([collision[1], -collision[0]])
            current = full_slice[..., window_start:]
    return full_slice


VMEM = pl.BlockSpec(memory_space=pltpu.VMEM)
SMEM = pl.BlockSpec(memory_space=pltpu.SMEM)
IN_HBM = pl.BlockSpec(memory_space=pltpu.HBM)
HALF = W * ORB // 2
TILE = W * ORB


def limit(mebibytes):
    return pltpu.CompilerParams(vmem_limit_bytes=mebibytes * 1024 * 1024)


def halves(x):
    high = x.astype(jnp.bfloat16)
    return high, (x - high.astype(jnp.float32)).astype(jnp.bfloat16)


def matmul(first, second):
    return jnp.dot(first, second, preferred_element_type=jnp.float32)


def fourier_tables():
    index = np.arange(KX * KY)
    turn = np.outer(index // KY, index // KY) / KX + np.outer(index % KY, index % KY) / KY
    phase = 2.0 * np.pi * (turn % 1.0)
    table = np.concatenate([np.cos(phase), np.sin(phase)]) / math.sqrt(KX * KY)
    high = table.astype(jnp.bfloat16)
    low = (table - high.astype(np.float64)).astype(jnp.bfloat16)
    return jnp.asarray(high), jnp.asarray(low)


def lower_lanes(shape):
    return lax.broadcasted_iota(jnp.int32, shape, 1) < HALF


def store_window(send_ref, k, own, real, imag):
    lower = lower_lanes(real.shape)
    turned_real = pltpu.roll(real, HALF, 1)
    turned_imag = pltpu.roll(imag, HALF, 1)
    send_ref[pl.ds(k, ORB, stride=2 * own), :] = jnp.where(lower, real, turned_imag)
    send_ref[pl.ds(own + k, ORB, stride=2 * own), :] = jnp.where(lower, turned_real, imag)


def start_all(copies):
    for copy in copies:
        copy.start()
    return copies


def wait_all(copies):
    for copy in copies:
        copy.wait()


def region_copies(retarded_ref, lesser_ref, near_refs, momenta, own, semaphores):
    copies = []
    for kind, ref in enumerate((retarded_ref, lesser_ref)):
        both = pl.ds(2 * kind, 2)
        last = ref.shape[3]
        for number, (tm, near_ref) in enumerate(zip(momenta, near_refs)):
            source = ref.at[:, tm * own : (tm + 1) * own, :, last - 2 * TILE :]
            copies.append(pltpu.make_async_copy(source, near_ref.at[both], semaphores.at[kind, number]))
    return copies


def regions_kernel(own, momenta, retarded_ref, lesser_ref, *others):
    *near_refs, rim_ref, passing = others
    copies = region_copies(retarded_ref, lesser_ref, near_refs, momenta, own, passing)
    for kind, ref in enumerate((retarded_ref, lesser_ref)):
        source = ref.at[:, :, :, ref.shape[3] - TILE :]
        copies.append(pltpu.make_async_copy(source, rim_ref.at[pl.ds(2 * kind, 2)], passing.at[kind, len(near_refs)]))
    wait_all(start_all(copies))


def first_window_kernel(own, propagator_ref, retarded_ref, lesser_ref, low_ref, high_ref, *others):
    *near_refs, window_ref, arrive, pass_on = others
    momenta, columns = lesser_ref.shape[1], lesser_ref.shape[3]
    half = momenta // 2
    fetches = start_all(
        [
            pltpu.make_async_copy(
                lesser_ref.at[:, first : first + own, :, columns - TILE :],
                window_ref.at[:, first : first + own],
                arrive.at[number],
            )
            for number, first in enumerate(range(0, momenta, own))
        ]
    )
    copies = start_all(region_copies(retarded_ref, lesser_ref, near_refs, (0, 1), own, pass_on))
    for number, fetch in enumerate(fetches):
        fetch.wait()
        for k in range(number * own, (number + 1) * own):
            left = jnp.concatenate([propagator_ref[0, k], propagator_ref[1, k]], axis=0)
            right = jnp.concatenate([window_ref[0, k], window_ref[1, k]], axis=1)
            imag, real = contract(*halves(left), *halves(right), TILE)
            store_window(low_ref if k < half else high_ref, k % half, half, -real, imag)
    wait_all(copies)


def fourier_kernel(arrived_ref, high_ref, low_ref, strength_ref, mean_ref, out_ref):
    count = KX * KY
    useful = count // (arrived_ref.shape[0] * arrived_ref.shape[2])
    x_high, x_low = halves(arrived_ref[:, arrived_ref.shape[1] - useful :].reshape(count, TILE))
    main = matmul(high_ref[...], jnp.concatenate([x_high, x_low], axis=1))
    turned = main[:, :TILE] + main[:, TILE:] + matmul(low_ref[...], x_high)
    lower = lower_lanes((count, TILE))
    sine_part = pltpu.roll(turned[count:], HALF, 1)
    here = turned[:count] + jnp.where(lower, -sine_part, sine_part)
    swapped = pltpu.roll(here, HALF, 1)
    real = jnp.where(lower, here, swapped)
    imag = jnp.where(lower, swapped, here)
    real_square = real * real
    imag_square = imag * imag
    size = real_square + imag_square
    strength = strength_ref[...]
    out_real = strength * jnp.where(lower, size * real, real_square - imag_square)
    out_imag = strength * jnp.where(lower, size * imag, 2.0 * real * imag)
    origin = (lax.broadcasted_iota(jnp.int32, (count, TILE), 0) == 0).astype(jnp.float32)
    mean = origin * mean_ref[...]
    out_real = out_real + mean * real
    out_imag = out_imag + mean * imag
    real_high, real_low = halves(out_real)
    imag_high, imag_low = halves(out_imag)
    y_high = jnp.concatenate([real_high, imag_high], axis=1)
    y_low = jnp.concatenate([real_low, imag_low], axis=1)
    back = matmul(high_ref[...], y_high) + matmul(low_ref[...], y_high) + matmul(high_ref[...], y_low)
    devices, rows, _ = out_ref.shape
    own = rows // 2
    out_ref[:, :own] = (back[:count, :TILE] + back[count:, TILE:]).reshape(devices, own, TILE)
    out_ref[:, own:] = (back[:count, TILE:] - back[count:, :TILE]).reshape(devices, own, TILE)


def coefficients(arrived_ref, propagator_ref, k, own):
    pieces = []
    for part, start in enumerate((-propagator_ref[1], propagator_ref[0])):
        first, second = (
            arrived_ref[pl.ds((2 * half + part) * own + k, ORB, stride=4 * own), :] for half in range(2)
        )
        start = jnp.concatenate([jnp.zeros((ORB, TILE - ORB), jnp.float32), start], axis=1)
        pieces.append((first, second + start))
    return pieces


def ladder(regions, width):
    rows = []
    for half in range(2):
        for kind in range(2):
            for lag in range(W // 2):
                offset = ORB * (1 + half * (W // 2) + lag)
                rows.append(jnp.concatenate([x[:, offset : offset + width] for x in regions[kind]], axis=1))
    return jnp.concatenate(rows, axis=0)


def contract(left_high, left_low, right_high, right_low, width):
    rows = left_high.shape[0]
    main = matmul(jnp.concatenate([left_high, left_low], axis=0), right_high)
    both = main[:rows] + main[rows:] + matmul(left_high, right_low)
    half = rows // 2
    real = both[:half, :width] - both[half:, width:]
    imag = both[:half, width:] + both[half:, :width]
    return imag, -real


def window_ladder_kernel(own, near_ref, high_ref, low_ref):
    for k in range(own):
        regions = [[near_ref[2 * kind + part, k] for part in range(2)] for kind in range(2)]
        high_ref[k], low_ref[k] = halves(ladder(regions, TILE))


def window_kernel(own, arrived_ref, propagator_ref, high_ref, low_ref, send_ref):
    for k in range(own):
        pieces = coefficients(arrived_ref, propagator_ref.at[:, k], k, own)
        left_high, left_low = halves(jnp.concatenate([jnp.concatenate(pair, axis=1) for pair in pieces], axis=0))
        real, imag = contract(left_high, left_low, high_ref[k], low_ref[k], TILE)
        store_window(send_ref, k, own, real, imag)


def trade(tiles):
    group = lax.broadcasted_iota(jnp.int32, tiles[0].shape, 1) // ORB
    for bit in (2, 1):
        first = (group & bit) == 0
        shift = bit * ORB
        traded = list(tiles)
        for i in range(4):
            if not i & bit:
                x, y = tiles[i], tiles[i | bit]
                traded[i] = jnp.where(first, x, pltpu.roll(y, shift, 1))
                traded[i | bit] = jnp.where(first, pltpu.roll(x, TILE - shift, 1), y)
        tiles = traded
    return tiles


def final_ladder_kernel(tm_ref, retarded_ref, lesser_ref, rim_ref, *others):
    *outs, region_ref, ladder_ref, arrive, leave = others
    count, rows_each = ladder_ref.shape[0], ladder_ref.shape[1] // 2
    high_ref = ladder_ref.at[:, :rows_each]
    low_ref = ladder_ref.at[:, rows_each:]
    own = count // 2
    momenta = pl.ds(tm_ref[0] // 2 * count, count)
    fetches = []
    for kind, ref in enumerate((retarded_ref, lesser_ref)):
        both = pl.ds(2 * kind, 2)
        fetches += start_all(
            [
                pltpu.make_async_copy(
                    ref.at[:, momenta], region_ref.at[both, :, :, pl.ds(TILE, ref.shape[3])], arrive.at[kind, 0]
                ),
                pltpu.make_async_copy(
                    rim_ref.at[both, momenta], region_ref.at[both, :, :, pl.ds(0, TILE)], arrive.at[kind, 1]
                ),
            ]
        )
    wait_all(fetches)

    def leaving(block, n):
        k = block * own + n
        return [pltpu.make_async_copy(ladder_ref.at[k], outs[block].at[n], leave.at[k])]

    def one(block, n, carry):
        k = block * own + n
        source = (tm_ref[0] % 2 ^ block) * own + n
        for part in range(2):
            region = jnp.concatenate([region_ref[2 * kind + part, source] for kind in range(2)], axis=0)
            lanes = pl.ds(part * TILE, TILE)
            tiles = [region[:, t * TILE : (t + 1) * TILE] for t in range(5)]
            first, third = trade(tiles[:4]), trade(tiles[1:])
            lower = lower_lanes(tiles[0].shape)
            second = [pltpu.roll(jnp.where(lower, z, x), HALF, 1) for x, z in zip(first, third)]
            for step, tile in enumerate((first + second + third)[1:]):
                high, low = halves(tile)
                for kind in range(2):
                    rows = pl.ds(step // 4 * TILE + kind * HALF + step % 4 * ORB, ORB)
                    high_ref[k, rows, lanes] = high[kind * ORB : (kind + 1) * ORB]
                    low_ref[k, rows, lanes] = low[kind * ORB : (kind + 1) * ORB]
            for kind in range(2):
                rows = pl.ds(2 * TILE + kind * HALF + 3 * ORB, ORB)
                high_ref[k, rows, lanes] = jnp.zeros((ORB, TILE), jnp.bfloat16)
                low_ref[k, rows, lanes] = jnp.zeros((ORB, TILE), jnp.bfloat16)
        start_all(leaving(block, n))
        return carry

    for block in range(2):
        lax.fori_loop(0, own, functools.partial(one, block), 0)
    for block in range(2):
        lax.fori_loop(0, own, lambda n, c: (wait_all(leaving(block, n)), c)[1], 0)


def stepped(pair):
    first, second = pair
    place = lax.broadcasted_iota(jnp.int32, first.shape, 1) // ORB % 4
    rows = [jnp.concatenate([first, second, jnp.zeros_like(first)], axis=1)]
    for s in range(1, 4):
        stay = place >= s
        up, over = s * ORB, TILE + (s - 4) * ORB
        rows.append(
            jnp.concatenate(
                [
                    jnp.where(stay, pltpu.roll(first, up, 1), 0.0),
                    jnp.where(stay, pltpu.roll(second, up, 1), pltpu.roll(first, over, 1)),
                    jnp.where(stay, 0.0, pltpu.roll(second, over, 1)),
                ],
                axis=1,
            )
        )
    return jnp.concatenate(rows, axis=0)


def final_kernel(own, before, tm_ref, arrived_ref, propagator_ref, ladder_ref, *others):
    out_ref, ladder_here, out_here, arrive, leave = others[before:]
    base = tm_ref[0] * own
    group = own // 2
    rows_each = ladder_here.shape[1] // 2

    def arriving(number):
        momenta = pl.ds(number * group, group)
        return [pltpu.make_async_copy(ladder_ref.at[momenta], ladder_here.at[momenta], arrive.at[number])]

    def leaving(number):
        momenta = pl.ds(number * group, group)
        source, target = out_here.at[:, momenta], out_ref.at[:, pl.ds(base + number * group, group)]
        return [pltpu.make_async_copy(source, target, leave.at[number])]

    def one(number, carry):
        wait_all(arriving(number))
        for n in range(group):
            k = number * group + n
            pieces = coefficients(arrived_ref, propagator_ref.at[:, base + k], k, own)
            left_high, left_low = halves(jnp.concatenate([stepped(pair) for pair in pieces], axis=0))
            right = ladder_here.at[k]
            parts = contract(left_high, left_low, right[:rows_each], right[rows_each:], TILE)
            for part, value in enumerate(parts):
                tiles = trade([value[s * ORB : (s + 1) * ORB] for s in range(4)])
                for t, tile in enumerate(tiles):
                    out_here[part, k, :, t * TILE : (t + 1) * TILE] = tile
        start_all(leaving(number))
        return carry

    groups = own // group
    for number in range(groups):
        start_all(arriving(number))
    lax.fori_loop(0, groups, one, 0)
    for number in range(groups):
        wait_all(leaving(number))


def own_block(x, own, axis):
    return lax.dynamic_slice_in_dim(x, lax.axis_index("tm") * own, own, axis)


def on_device_tiled(hist_lesser, hist_retarded, propagator, coupling, mf_weight, lag_weight):
    both_axes = ("mom", "tm")
    momenta_here = hist_lesser.shape[1]
    columns = hist_lesser.shape[3]
    peers = lax.axis_size("tm")
    devices = lax.axis_size("mom") * peers
    own = momenta_here // peers
    count = KX * KY

    f32 = functools.partial(jax.ShapeDtypeStruct, dtype=jnp.float32)
    bf16 = functools.partial(jax.ShapeDtypeStruct, dtype=jnp.bfloat16)

    def call(kernel, shapes, *operands):
        return pl.pallas_call(
            kernel,
            out_shape=shapes,
            in_specs=[VMEM] * len(operands),
            out_specs=jax.tree.map(lambda _: VMEM, shapes),
            compiler_params=limit(12),
        )(*operands)

    half = momenta_here // 2
    sent = f32((devices * half, TILE))
    near_shape = f32((4, own, ORB, 2 * TILE))
    low, high, *near = pl.pallas_call(
        functools.partial(first_window_kernel, own),
        out_shape=(sent, sent, near_shape, near_shape),
        in_specs=[VMEM, IN_HBM, IN_HBM],
        out_specs=(VMEM,) * 4,
        scratch_shapes=[
            pltpu.VMEM((2, momenta_here, ORB, TILE), jnp.float32),
            pltpu.SemaphoreType.DMA((peers,)),
            pltpu.SemaphoreType.DMA((2, 2)),
        ],
        compiler_params=limit(8),
    )(propagator, *(pltpu.with_memory_space_constraint(x, pltpu.HBM) for x in (hist_retarded, hist_lesser)))
    here = lax.axis_index("tm")
    last = here == peers - 1
    low = lax.ppermute(low, "tm", [(3, 2)])
    near = [lax.ppermute(block, "tm", [(3, tm)]) for tm, block in enumerate(near)]
    send = jnp.where(last, high, low).reshape(devices, half, TILE)
    send, hist_lesser, hist_retarded, coupling, mf_weight, lag_weight = lax.optimization_barrier(
        (send, hist_lesser, hist_retarded, coupling, mf_weight, lag_weight)
    )
    two, mine, rim = pl.pallas_call(
        functools.partial(regions_kernel, own, (2, 3)),
        out_shape=(near_shape, near_shape, f32((4, momenta_here, ORB, TILE))),
        in_specs=[IN_HBM, IN_HBM],
        out_specs=(VMEM,) * 3,
        scratch_shapes=[pltpu.SemaphoreType.DMA((2, 3))],
        compiler_params=limit(4),
    )(*(pltpu.with_memory_space_constraint(x, pltpu.HBM) for x in (hist_retarded, hist_lesser)))
    near.append(lax.ppermute(two, "tm", [(3, 2)]))
    rim = shifted(rim, "tm", 1)
    me = lax.axis_index("mom") * peers + lax.axis_index("tm")
    last_mark = (jnp.arange(W) == W - 1).astype(jnp.float32)
    strong = (coupling * coupling).reshape(ORB, 1, ORB) * lag_weight[:, None]
    mean = mf_weight.reshape(ORB, 1, ORB) * (lag_weight * last_mark)[:, None]
    strong = lax.dynamic_slice_in_dim(strong.reshape(devices, HALF), me, 1, 0)
    mean = lax.dynamic_slice_in_dim(mean.reshape(devices, HALF), me, 1, 0)
    strength = jnp.concatenate([strong, strong], axis=1)
    mean = jnp.concatenate([mean, jnp.zeros_like(mean)], axis=1)
    table_high, table_low = fourier_tables()

    ladders = []
    ladder_shape = (own, 2 * 3 * TILE, 2 * TILE)

    def send_beside(sent):
        sent, retarded, lesser, edge = lax.optimization_barrier((sent, hist_retarded, hist_lesser, rim))
        arrived = lax.all_to_all(sent, both_axes, 0, 0, tiled=True)
        momenta = (here ^ len(ladders)).reshape(1).astype(jnp.int32)
        ladder = pl.pallas_call(
            final_ladder_kernel,
            out_shape=(pltpu.HBM(ladder_shape, jnp.bfloat16),) * 2,
            in_specs=[SMEM, IN_HBM, IN_HBM, IN_HBM],
            out_specs=(IN_HBM,) * 2,
            scratch_shapes=[
                pltpu.VMEM((4, 2 * own, ORB, TILE + columns), jnp.float32),
                pltpu.VMEM((2 * own, *ladder_shape[1:]), jnp.bfloat16),
                pltpu.SemaphoreType.DMA((2, 2)),
                pltpu.SemaphoreType.DMA((2 * own,)),
            ],
            compiler_params=limit(12),
        )(momenta, *(pltpu.with_memory_space_constraint(x, pltpu.HBM) for x in (retarded, lesser, edge)))
        arrived, *ladder = lax.optimization_barrier((arrived, *ladder))
        ladders.extend(ladder)
        return arrived

    for sweep in range(PASSES):
        arrived = lax.all_to_all(send, both_axes, 0, 0, tiled=True)
        if sweep == 0:
            arrived, *near[:2] = lax.optimization_barrier((arrived, *near[:2]))
        back = call(
            fourier_kernel,
            f32((devices, 2 * own, TILE)),
            arrived.reshape(devices // peers, peers, -1, TILE),
            table_high,
            table_low,
            strength,
            mean,
        )
        if sweep == 0:
            near[2], _ = lax.optimization_barrier((near[2], back))
            for tm, received in enumerate(near):
                mine = jnp.where(here == tm, received, mine)
            rungs = bf16((own, 2 * TILE, 2 * TILE))
            rungs = call(functools.partial(window_ladder_kernel, own), (rungs, rungs), mine)
            rim, *rungs = lax.optimization_barrier((rim, *rungs))
            propagator_own = own_block(propagator, own, 1)
        arrived = send_beside(back) if sweep else lax.all_to_all(back, both_axes, 0, 0, tiled=True)
        arrived = arrived.reshape(2 * count, TILE)
        if sweep + 1 < PASSES:
            send = call(
                functools.partial(window_kernel, own),
                f32((count, TILE)),
                arrived,
                propagator_own,
                *rungs,
            ).reshape(devices, own, TILE)

    def finish(new_slice, coefficients_of, step):
        before = () if new_slice is None else (new_slice,)
        return pl.pallas_call(
            functools.partial(final_kernel, own, len(before)),
            out_shape=pltpu.HBM(hist_lesser.shape, jnp.float32),
            in_specs=[SMEM, VMEM, VMEM] + [IN_HBM] * (1 + len(before)),
            out_specs=IN_HBM,
            scratch_shapes=[
                pltpu.VMEM(ladder_shape, jnp.bfloat16),
                pltpu.VMEM((2, own, ORB, columns), jnp.float32),
                pltpu.SemaphoreType.DMA((own,)),
                pltpu.SemaphoreType.DMA((own,)),
            ],
            input_output_aliases={4: 0} if before else {},
            compiler_params=limit(6),
        )(
            (here ^ step).reshape(1).astype(jnp.int32),
            coefficients_of,
            propagator,
            pltpu.with_memory_space_constraint(ladders[step], pltpu.HBM) if step < 3 else ladders[step],
            *before,
        )

    def exchange(x, step):
        return lax.ppermute(x, "tm", [(t, t ^ step) for t in range(peers)])

    across = exchange(arrived, 2)
    beside_me = exchange(arrived, 1)
    new_slice = finish(None, arrived, 0)
    new_slice = finish(new_slice, beside_me, 1)
    across, new_slice = lax.optimization_barrier((across, new_slice))
    beyond = exchange(across, 1)
    new_slice = finish(new_slice, across, 2)
    return finish(new_slice, beyond, 3)


def on_device(hist_lesser, *others):
    peers = lax.axis_size("tm")
    devices = lax.axis_size("mom") * peers
    fits = devices == 2 * ORB and peers == 4 and hist_lesser.shape[1:] == (2 * ORB, ORB, 4 * TILE)
    return (on_device_tiled if fits else on_device_any)(hist_lesser, *others)


def solution(mesh):
    return jax.shard_map(
        on_device,
        mesh=mesh,
        in_specs=(
            P(None, "mom", None, "tm"),
            P(None, "mom", None, "tm"),
            P(None, "mom", None, None),
            P(),
            P(),
            P(),
        ),
        out_specs=P(None, "mom", None, "tm"),
        check_vma=False,
    )
```

```python
import functools
import math

import jax
import jax.numpy as jnp
import numpy as np
from jax import lax
from jax.experimental import pallas as pl
from jax.experimental.pallas import tpu as pltpu
from jax.sharding import PartitionSpec as P

KX = 16
KY = 16
ORB = 16
W = 8
PASSES = 3


HIGHEST = lax.Precision.HIGHEST


def shifted(x, axis, by):
    peers = lax.axis_size(axis)
    pairs = [(i, i + by) for i in range(peers) if 0 <= i + by < peers]
    return lax.ppermute(x, axis, pairs)


def broadcast(x, axis, root):
    mine = lax.axis_index(axis) == root
    return lax.psum(jnp.where(mine, x, jnp.zeros_like(x)), axis)


def momentum_tables():
    index = jnp.arange(KX * KY, dtype=jnp.int32)
    first = index // KY
    second = index % KY
    turn_x = first[:, None] * first[None, :] % KX
    turn_y = second[:, None] * second[None, :] % KY
    phase = 2.0 * math.pi * (turn_x.astype(jnp.float32) / KX + turn_y.astype(jnp.float32) / KY)
    scale = 1.0 / math.sqrt(KX * KY)
    return (jnp.cos(phase) * scale, jnp.sin(phase) * scale)


def complex_product(pattern, first, second):
    real = jnp.einsum(pattern, first[0], second[0], precision=HIGHEST) - jnp.einsum(
        pattern, first[1], second[1], precision=HIGHEST
    )
    imaginary = jnp.einsum(pattern, first[0], second[1], precision=HIGHEST) + jnp.einsum(
        pattern, first[1], second[0], precision=HIGHEST
    )
    return jnp.stack([real, imaginary])


def back_to_momenta(real, imaginary, cosine, sine):
    out_real = jnp.dot(cosine, real, precision=HIGHEST) + jnp.dot(
        sine, imaginary, precision=HIGHEST
    )
    out_imag = jnp.dot(cosine, imaginary, precision=HIGHEST) - jnp.dot(
        sine, real, precision=HIGHEST
    )
    return jnp.stack([out_real, out_imag])


def local_products(arrived, cosine, sine, strength, lag_mark):
    lag_count = lag_mark.shape[0]
    space_real = jnp.dot(cosine, arrived[0], precision=HIGHEST) - jnp.dot(
        sine, arrived[1], precision=HIGHEST
    )
    space_imag = jnp.dot(cosine, arrived[1], precision=HIGHEST) + jnp.dot(
        sine, arrived[0], precision=HIGHEST
    )
    column_strength = jnp.repeat(strength, lag_count)
    magnitude = column_strength * (space_real * space_real + space_imag * space_imag)
    lesser_real = magnitude * space_real
    lesser_imag = magnitude * space_imag
    pair_real = column_strength * (space_real * space_real - space_imag * space_imag)
    pair_imag = column_strength * 2.0 * space_real * space_imag
    return (
        back_to_momenta(lesser_real, lesser_imag, cosine, sine),
        back_to_momenta(pair_real, pair_imag, cosine, sine),
    )


def self_energies(window, cosine, sine, strength, mf_weight, last_mark):
    momenta_here = window.shape[1]
    outgoing = window.reshape(2, momenta_here, ORB * ORB * W)
    arrived = lax.all_to_all(outgoing, "mom", split_axis=2, concat_axis=1, tiled=True)
    lesser_r, pair_r = local_products(arrived, cosine, sine, strength, last_mark)
    back_lesser, back_pair = (
        lax.all_to_all(lesser_r, "mom", split_axis=1, concat_axis=2, tiled=True),
        lax.all_to_all(pair_r, "mom", split_axis=1, concat_axis=2, tiled=True),
    )
    sigma = back_lesser.reshape(2, momenta_here, ORB, ORB, W)
    pair_k = back_pair.reshape(2, momenta_here, ORB, ORB, W)
    own_total = jnp.sum(window[..., W - 1], axis=1)
    occupation = lax.psum(own_total, "mom") / (KX * KY)
    sigma = sigma + (mf_weight.reshape(ORB, ORB) * occupation)[:, None, :, :, None] * last_mark
    return (sigma, pair_k)


def collide(sigma, pair_k, lag_weight, padded_r, padded_l, first, count):
    weighted_sigma = sigma * lag_weight
    weighted_pair = pair_k * lag_weight

    def ladder(padded):
        region = lax.dynamic_slice_in_dim(padded, first * ORB, (count + W - 1) * ORB, 3)
        return jnp.stack(
            [region[..., offset * ORB : (offset + count) * ORB] for offset in range(W)], axis=3
        )

    return complex_product("kabm,kbmx->kax", weighted_sigma, ladder(padded_r)) + complex_product(
        "kabm,kbmx->kax", weighted_pair, ladder(padded_l)
    )


def on_device_any(hist_lesser, hist_retarded, propagator, coupling, mf_weight, lag_weight):
    momenta_here = hist_lesser.shape[1]
    times_here = hist_lesser.shape[3] // ORB
    cosine, sine = momentum_tables()
    lesser = hist_lesser.reshape(2, momenta_here, ORB, times_here, ORB)
    start = complex_product("kab,kbjc->kajc", propagator, lesser).reshape(
        2, momenta_here, ORB, times_here * ORB
    )
    rim_width = (W - 1) * ORB
    rim_retarded, rim_lesser = shifted(
        (
            hist_retarded[..., times_here * ORB - rim_width :],
            hist_lesser[..., times_here * ORB - rim_width :],
        ),
        "tm",
        1,
    )
    padded_r = jnp.concatenate([rim_retarded, hist_retarded], axis=3)
    padded_l = jnp.concatenate([rim_lesser, hist_lesser], axis=3)
    block = min(32, times_here)
    count_blocks = times_here // block
    window_start = (times_here - W) * ORB
    pair_count = ORB * ORB // lax.axis_size("mom")
    strength = lax.dynamic_slice_in_dim(
        coupling * coupling, lax.axis_index("mom") * pair_count, pair_count, 0
    )
    last_mark = (jnp.arange(W) == W - 1).astype(jnp.float32)
    owner = lax.axis_size("tm") - 1
    current = start[..., window_start:]
    full_slice = start
    for sweep in range(PASSES):
        shared = broadcast(current, "tm", owner)
        window = jnp.transpose(shared.reshape(2, momenta_here, ORB, W, ORB), (0, 1, 2, 4, 3))
        sigma, pair_k = self_energies(window, cosine, sine, strength, mf_weight, last_mark)
        if sweep + 1 < PASSES:
            collision = collide(sigma, pair_k, lag_weight, padded_r, padded_l, times_here - W, W)
            current = start[..., window_start:] + jnp.stack([collision[1], -collision[0]])
        else:
            blocks_out = lax.map(
                lambda number: collide(
                    sigma, pair_k, lag_weight, padded_r, padded_l, number * block, block
                ),
                jnp.arange(count_blocks, dtype=jnp.int32),
            )
            collision = jnp.moveaxis(blocks_out, 0, 3).reshape(
                2, momenta_here, ORB, times_here * ORB
            )
            full_slice = start + jnp.stack([collision[1], -collision[0]])
            current = full_slice[..., window_start:]
    return full_slice


VMEM = pl.BlockSpec(memory_space=pltpu.VMEM)
SMEM = pl.BlockSpec(memory_space=pltpu.SMEM)
IN_HBM = pl.BlockSpec(memory_space=pltpu.HBM)
HALF = W * ORB // 2
TILE = W * ORB


def limit(mebibytes):
    return pltpu.CompilerParams(vmem_limit_bytes=mebibytes * 1024 * 1024)


def halves(x):
    high = x.astype(jnp.bfloat16)
    return high, (x - high.astype(jnp.float32)).astype(jnp.bfloat16)


def matmul(first, second):
    return jnp.dot(first, second, preferred_element_type=jnp.float32)


def fourier_tables():
    index = np.arange(KX * KY)
    turn = np.outer(index // KY, index // KY) / KX + np.outer(index % KY, index % KY) / KY
    phase = 2.0 * np.pi * (turn % 1.0)
    table = np.concatenate([np.cos(phase), np.sin(phase)]) / math.sqrt(KX * KY)
    high = table.astype(jnp.bfloat16)
    low = (table - high.astype(np.float64)).astype(jnp.bfloat16)
    return jnp.asarray(high), jnp.asarray(low)


def lower_lanes(shape):
    return lax.broadcasted_iota(jnp.int32, shape, 1) < HALF


def store_window(send_ref, k, own, real, imag):
    lower = lower_lanes(real.shape)
    turned_real = pltpu.roll(real, HALF, 1)
    turned_imag = pltpu.roll(imag, HALF, 1)
    send_ref[pl.ds(k, ORB, stride=2 * own), :] = jnp.where(lower, real, turned_imag)
    send_ref[pl.ds(own + k, ORB, stride=2 * own), :] = jnp.where(lower, turned_real, imag)


def start_all(copies):
    for copy in copies:
        copy.start()
    return copies


def wait_all(copies):
    for copy in copies:
        copy.wait()


def near_copies(histories, near_ref, tm, own, semaphores):
    copies = []
    for kind, ref in enumerate(histories):
        last = ref.shape[3]
        source = ref.at[:, tm * own : (tm + 1) * own, :, last - 2 * TILE :]
        copies.append(pltpu.make_async_copy(source, near_ref.at[pl.ds(2 * kind, 2)], semaphores.at[kind]))
    return copies


def rim_copies(ref, near_ref, own, semaphores):
    copies = []
    for number in range(8):
        part, half, quarter = number // 4, number // 2 % 2, number % 2
        source = ref.at[part, pl.ds((2 * half + quarter) * own, own), :, pl.ds(ref.shape[3] - TILE, TILE)]
        target = near_ref.at[2 * part + half, :, :, pl.ds(quarter * TILE, TILE)]
        copies.append(pltpu.make_async_copy(source, target, semaphores.at[number]))
    return copies


def settings_kernel(index_ref, coupling_ref, mf_ref, lag_ref, strength_ref, mean_ref):
    lane = lax.broadcasted_iota(jnp.int32, strength_ref.shape, 1)
    first = index_ref[0] // 2 * ORB
    lag = index_ref[0] % 2 * (W // 2) + lane // ORB % (W // 2)
    zero = jnp.zeros(strength_ref.shape, jnp.float32)
    coupling, mf, weight = zero, zero, zero
    for b in range(ORB):
        coupling = jnp.where(lane % ORB == b, coupling_ref[first + b], coupling)
        mf = jnp.where(lane % ORB == b, mf_ref[first + b], mf)
    for m in range(W):
        weight = jnp.where(lag == m, lag_ref[m], weight)
    strength_ref[...] = coupling * coupling * weight
    mean_ref[...] = jnp.where((lag == W - 1) & (lane < HALF), mf * weight, zero)


def first_window_kernel(own, tm_ref, propagator_ref, retarded_ref, lesser_ref, low_ref, high_ref, *others):
    *out_refs, window_ref, arrive, pass_on = others
    histories = (retarded_ref, lesser_ref)
    momenta, columns = lesser_ref.shape[1], lesser_ref.shape[3]
    half = momenta // 2
    last = len(out_refs)
    fetches = start_all(
        [
            pltpu.make_async_copy(
                lesser_ref.at[:, first : first + own, :, columns - TILE :],
                window_ref.at[:, first : first + own],
                arrive.at[number],
            )
            for number, first in enumerate(range(0, momenta, own))
        ]
    )

    def near():
        return [c for tm, ref in enumerate(out_refs) for c in near_copies(histories, ref, tm, own, pass_on.at[tm])]

    def rims(second):
        pairs = ((0, retarded_ref), (second, lesser_ref))
        return [c for number, ref in pairs for c in rim_copies(ref, out_refs[number], own, pass_on.at[number])]

    cases = ((tm_ref[0] == last, near), (tm_ref[0] == 0, lambda: rims(2)), ((tm_ref[0] != 0) & (tm_ref[0] != last), lambda: rims(1)))
    for case, copies in cases:

        @pl.when(case)
        def _():
            start_all(copies())

    for number, fetch in enumerate(fetches):
        fetch.wait()
        for k in range(number * own, (number + 1) * own):
            left = jnp.concatenate([propagator_ref[0, k], propagator_ref[1, k]], axis=0)
            right = jnp.concatenate([window_ref[0, k], window_ref[1, k]], axis=1)
            imag, real = contract(*halves(left), *halves(right), TILE)
            store_window(low_ref if k < half else high_ref, k % half, half, -real, imag)
    for case, copies in cases:

        @pl.when(case)
        def _():
            wait_all(copies())


def fourier_kernel(arrived_ref, high_ref, low_ref, strength_ref, mean_ref, out_ref):
    count = KX * KY
    useful = count // (arrived_ref.shape[0] * arrived_ref.shape[2])
    x_high, x_low = halves(arrived_ref[:, arrived_ref.shape[1] - useful :].reshape(count, TILE))
    main = matmul(high_ref[...], jnp.concatenate([x_high, x_low], axis=1))
    turned = main[:, :TILE] + main[:, TILE:] + matmul(low_ref[...], x_high)
    lower = lower_lanes((count, TILE))
    sine_part = pltpu.roll(turned[count:], HALF, 1)
    here = turned[:count] + jnp.where(lower, -sine_part, sine_part)
    swapped = pltpu.roll(here, HALF, 1)
    real = jnp.where(lower, here, swapped)
    imag = jnp.where(lower, swapped, here)
    real_square = real * real
    imag_square = imag * imag
    size = real_square + imag_square
    strength = strength_ref[...]
    out_real = strength * jnp.where(lower, size * real, real_square - imag_square)
    out_imag = strength * jnp.where(lower, size * imag, 2.0 * real * imag)
    origin = (lax.broadcasted_iota(jnp.int32, (count, TILE), 0) == 0).astype(jnp.float32)
    mean = origin * mean_ref[...]
    out_real = out_real + mean * real
    out_imag = out_imag + mean * imag
    real_high, real_low = halves(out_real)
    imag_high, imag_low = halves(out_imag)
    y_high = jnp.concatenate([real_high, imag_high], axis=1)
    y_low = jnp.concatenate([real_low, imag_low], axis=1)
    back = matmul(high_ref[...], y_high) + matmul(low_ref[...], y_high) + matmul(high_ref[...], y_low)
    devices, rows, _ = out_ref.shape
    own = rows // 2
    out_ref[:, :own] = (back[:count, :TILE] + back[count:, TILE:]).reshape(devices, own, TILE)
    out_ref[:, own:] = (back[:count, TILE:] - back[count:, :TILE]).reshape(devices, own, TILE)


def coefficients(arrived_ref, propagator_ref, k, own):
    pieces = []
    for part, start in enumerate((-propagator_ref[1], propagator_ref[0])):
        first, second = (
            arrived_ref[pl.ds((2 * half + part) * own + k, ORB, stride=4 * own), :] for half in range(2)
        )
        start = jnp.concatenate([jnp.zeros((ORB, TILE - ORB), jnp.float32), start], axis=1)
        pieces.append((first, second + start))
    return pieces


def ladder(regions, width):
    rows = []
    for half in range(2):
        for kind in range(2):
            for lag in range(W // 2):
                offset = ORB * (1 + half * (W // 2) + lag)
                rows.append(jnp.concatenate([x[:, offset : offset + width] for x in regions[kind]], axis=1))
    return jnp.concatenate(rows, axis=0)


def contract(left_high, left_low, right_high, right_low, width):
    rows = left_high.shape[0]
    main = matmul(jnp.concatenate([left_high, left_low], axis=0), right_high)
    both = main[:rows] + main[rows:] + matmul(left_high, right_low)
    half = rows // 2
    real = both[:half, :width] - both[half:, width:]
    imag = both[:half, width:] + both[half:, :width]
    return imag, -real


def window_ladder_kernel(own, tm_ref, retarded_ref, lesser_ref, *others):
    *near_refs, high_ref, low_ref, near_ref, arrive = others
    for tm in range(len(near_refs) + 1):

        @pl.when(tm_ref[0] == tm)
        def _():
            if tm < len(near_refs):
                copies = [pltpu.make_async_copy(near_refs[tm], near_ref, arrive.at[0])]
            else:
                copies = near_copies((retarded_ref, lesser_ref), near_ref, tm, own, arrive)
            wait_all(start_all(copies))

    for k in range(own):
        regions = [[near_ref[2 * kind + part, k] for part in range(2)] for kind in range(2)]
        high_ref[k], low_ref[k] = halves(ladder(regions, TILE))


def window_kernel(own, arrived_ref, propagator_ref, high_ref, low_ref, send_ref):
    for k in range(own):
        pieces = coefficients(arrived_ref, propagator_ref.at[:, k], k, own)
        left_high, left_low = halves(jnp.concatenate([jnp.concatenate(pair, axis=1) for pair in pieces], axis=0))
        real, imag = contract(left_high, left_low, high_ref[k], low_ref[k], TILE)
        store_window(send_ref, k, own, real, imag)


def trade(tiles):
    group = lax.broadcasted_iota(jnp.int32, tiles[0].shape, 1) // ORB
    for bit in (2, 1):
        first = (group & bit) == 0
        shift = bit * ORB
        traded = list(tiles)
        for i in range(4):
            if not i & bit:
                x, y = tiles[i], tiles[i | bit]
                traded[i] = jnp.where(first, x, pltpu.roll(y, shift, 1))
                traded[i | bit] = jnp.where(first, pltpu.roll(x, TILE - shift, 1), y)
        tiles = traded
    return tiles


def final_ladder_kernel(tm_ref, retarded_ref, lesser_ref, *others):
    *others, region_ref, ladder_ref, arrive, arrive_rim, leave = others
    outs, rim_refs = others[-2:], others[:-2]
    count, rows_each = ladder_ref.shape[0], ladder_ref.shape[1] // 2
    high_ref = ladder_ref.at[:, :rows_each]
    low_ref = ladder_ref.at[:, rows_each:]
    own = count // len(outs)
    half = tm_ref[1] // len(outs)
    fetches = start_all(
        [
            pltpu.make_async_copy(
                ref.at[:, pl.ds(half * count, count)],
                region_ref.at[pl.ds(2 * kind, 2), :, :, pl.ds(TILE, ref.shape[3])],
                arrive.at[kind],
            )
            for kind, ref in enumerate((retarded_ref, lesser_ref))
        ]
    )

    def rims(second):
        copies = []
        for kind, ref in enumerate((rim_refs[0], rim_refs[second])):
            for part in range(2):
                for quarter in range(2):
                    source = ref.at[2 * part + half, :, :, pl.ds(quarter * TILE, TILE)]
                    target = region_ref.at[2 * kind + part, pl.ds(quarter * own, own), :, pl.ds(0, TILE)]
                    copies.append(pltpu.make_async_copy(source, target, arrive_rim.at[2 * kind + part, quarter]))
        return copies

    @pl.when(tm_ref[0] == 0)
    def _():
        region_ref[:, :, :, :TILE] = jnp.zeros((4, count, ORB, TILE), jnp.float32)

    @pl.when(tm_ref[0] == 1)
    def _():
        wait_all(start_all(rims(2)))

    @pl.when(tm_ref[0] > 1)
    def _():
        wait_all(start_all(rims(1)))

    wait_all(fetches)

    def leaving(block, n):
        k = block * own + n
        return [pltpu.make_async_copy(ladder_ref.at[k], outs[block].at[n], leave.at[k])]

    def one(block, n, carry):
        k = block * own + n
        source = (tm_ref[0] % 2 ^ block) * own + n
        for part in range(2):
            region = jnp.concatenate([region_ref[2 * kind + part, source] for kind in range(2)], axis=0)
            lanes = pl.ds(part * TILE, TILE)
            tiles = [region[:, t * TILE : (t + 1) * TILE] for t in range(5)]
            first, third = trade(tiles[:4]), trade(tiles[1:])
            lower = lower_lanes(tiles[0].shape)
            second = [pltpu.roll(jnp.where(lower, z, x), HALF, 1) for x, z in zip(first, third)]
            for step, tile in enumerate((first + second + third)[1:]):
                high, low = halves(tile)
                for kind in range(2):
                    rows = pl.ds(step // 4 * TILE + kind * HALF + step % 4 * ORB, ORB)
                    high_ref[k, rows, lanes] = high[kind * ORB : (kind + 1) * ORB]
                    low_ref[k, rows, lanes] = low[kind * ORB : (kind + 1) * ORB]
            for kind in range(2):
                rows = pl.ds(2 * TILE + kind * HALF + 3 * ORB, ORB)
                high_ref[k, rows, lanes] = jnp.zeros((ORB, TILE), jnp.bfloat16)
                low_ref[k, rows, lanes] = jnp.zeros((ORB, TILE), jnp.bfloat16)
        start_all(leaving(block, n))
        return carry

    for block in range(2):
        lax.fori_loop(0, own, functools.partial(one, block), 0)
    for block in range(2):
        lax.fori_loop(0, own, lambda n, c: (wait_all(leaving(block, n)), c)[1], 0)


def stepped(pair):
    first, second = pair
    place = lax.broadcasted_iota(jnp.int32, first.shape, 1) // ORB % 4
    rows = [jnp.concatenate([first, second, jnp.zeros_like(first)], axis=1)]
    for s in range(1, 4):
        stay = place >= s
        up, over = s * ORB, TILE + (s - 4) * ORB
        rows.append(
            jnp.concatenate(
                [
                    jnp.where(stay, pltpu.roll(first, up, 1), 0.0),
                    jnp.where(stay, pltpu.roll(second, up, 1), pltpu.roll(first, over, 1)),
                    jnp.where(stay, 0.0, pltpu.roll(second, over, 1)),
                ],
                axis=1,
            )
        )
    return jnp.concatenate(rows, axis=0)


def final_kernel(own, before, tm_ref, arrived_ref, propagator_ref, ladder_ref, *others):
    out_ref, ladder_here, out_here, arrive, leave = others[before:]
    base = tm_ref[0] * own
    group = own // 2
    rows_each = ladder_here.shape[1] // 2

    def arriving(number):
        momenta = pl.ds(number * group, group)
        return [pltpu.make_async_copy(ladder_ref.at[momenta], ladder_here.at[momenta], arrive.at[number])]

    def leaving(number):
        momenta = pl.ds(number * group, group)
        source, target = out_here.at[:, momenta], out_ref.at[:, pl.ds(base + number * group, group)]
        return [pltpu.make_async_copy(source, target, leave.at[number])]

    def one(number, carry):
        wait_all(arriving(number))
        for n in range(group):
            k = number * group + n
            pieces = coefficients(arrived_ref, propagator_ref.at[:, base + k], k, own)
            left_high, left_low = halves(jnp.concatenate([stepped(pair) for pair in pieces], axis=0))
            right = ladder_here.at[k]
            parts = contract(left_high, left_low, right[:rows_each], right[rows_each:], TILE)
            for part, value in enumerate(parts):
                tiles = trade([value[s * ORB : (s + 1) * ORB] for s in range(4)])
                for t, tile in enumerate(tiles):
                    out_here[part, k, :, t * TILE : (t + 1) * TILE] = tile
        start_all(leaving(number))
        return carry

    groups = own // group
    for number in range(groups):
        start_all(arriving(number))
    lax.fori_loop(0, groups, one, 0)
    for number in range(groups):
        wait_all(leaving(number))


def own_block(x, own, axis):
    return lax.dynamic_slice_in_dim(x, lax.axis_index("tm") * own, own, axis)


def on_device_tiled(hist_lesser, hist_retarded, propagator, coupling, mf_weight, lag_weight):
    both_axes = ("mom", "tm")
    momenta_here = hist_lesser.shape[1]
    columns = hist_lesser.shape[3]
    peers = lax.axis_size("tm")
    devices = lax.axis_size("mom") * peers
    own = momenta_here // peers
    count = KX * KY

    f32 = functools.partial(jax.ShapeDtypeStruct, dtype=jnp.float32)
    bf16 = functools.partial(jax.ShapeDtypeStruct, dtype=jnp.bfloat16)

    def call(kernel, shapes, *operands):
        return pl.pallas_call(
            kernel,
            out_shape=shapes,
            in_specs=[VMEM] * len(operands),
            out_specs=jax.tree.map(lambda _: VMEM, shapes),
            compiler_params=limit(12),
        )(*operands)

    half = momenta_here // 2
    sent = f32((devices * half, TILE))
    near_shape = f32((4, own, ORB, 2 * TILE))
    here = lax.axis_index("tm")
    last = here == peers - 1
    here_array = here.reshape(1).astype(jnp.int32)
    low, high, *near = pl.pallas_call(
        functools.partial(first_window_kernel, own),
        out_shape=(sent, sent, near_shape, near_shape, near_shape),
        in_specs=[SMEM, VMEM, IN_HBM, IN_HBM],
        out_specs=(VMEM,) * 5,
        scratch_shapes=[
            pltpu.VMEM((2, momenta_here, ORB, TILE), jnp.float32),
            pltpu.SemaphoreType.DMA((peers,)),
            pltpu.SemaphoreType.DMA((peers - 1, 8)),
        ],
        compiler_params=limit(8),
    )(here_array, propagator, *(pltpu.with_memory_space_constraint(x, pltpu.HBM) for x in (hist_retarded, hist_lesser)))
    neighbours = [(0, 1), (1, 0), (2, 3), (3, 2)]
    low = lax.ppermute(low, "tm", neighbours)
    near[0] = lax.ppermute(near[0], "tm", [(3, 0), (0, 1), (1, 2), (2, 3)])
    near[1] = lax.ppermute(near[1], "tm", [(3, 1), (1, 2), (2, 3), (0, 0)])
    send = jnp.where(last, high, low).reshape(devices, half, TILE)
    send, near[2], hist_lesser, hist_retarded, coupling, mf_weight, lag_weight = lax.optimization_barrier(
        (send, near[2], hist_lesser, hist_retarded, coupling, mf_weight, lag_weight)
    )
    near[2] = lax.ppermute(near[2], "tm", neighbours)
    histories = [pltpu.with_memory_space_constraint(x, pltpu.HBM) for x in (hist_retarded, hist_lesser)]
    me = lax.axis_index("mom") * peers + here
    strength, mean = pl.pallas_call(
        settings_kernel,
        out_shape=(f32((1, TILE)), f32((1, TILE))),
        in_specs=[SMEM] * 4,
        out_specs=(VMEM,) * 2,
        compiler_params=limit(4),
    )(me.reshape(1).astype(jnp.int32), coupling, mf_weight, lag_weight)
    table_high, table_low = fourier_tables()

    ladders = []
    ladder_shape = (own, 2 * 3 * TILE, 2 * TILE)

    def send_beside(sent):
        sent, retarded, lesser, *edges = lax.optimization_barrier((sent, hist_retarded, hist_lesser, *near))
        arrived = lax.all_to_all(sent, both_axes, 0, 0, tiled=True)
        ladder = pl.pallas_call(
            final_ladder_kernel,
            out_shape=(pltpu.HBM(ladder_shape, jnp.bfloat16),) * 2,
            in_specs=[SMEM] + [IN_HBM] * 5,
            out_specs=(IN_HBM,) * 2,
            scratch_shapes=[
                pltpu.VMEM((4, 2 * own, ORB, TILE + columns), jnp.float32),
                pltpu.VMEM((2 * own, *ladder_shape[1:]), jnp.bfloat16),
                pltpu.SemaphoreType.DMA((2,)),
                pltpu.SemaphoreType.DMA((4, 2)),
                pltpu.SemaphoreType.DMA((2 * own,)),
            ],
            compiler_params=limit(12),
        )(
            jnp.stack([here, here ^ len(ladders)]).astype(jnp.int32),
            *(pltpu.with_memory_space_constraint(x, pltpu.HBM) for x in (retarded, lesser, *edges)),
        )
        arrived, *ladder = lax.optimization_barrier((arrived, *ladder))
        ladders.extend(ladder)
        return arrived

    for sweep in range(PASSES):
        arrived = lax.all_to_all(send, both_axes, 0, 0, tiled=True)
        back = call(
            fourier_kernel,
            f32((devices, 2 * own, TILE)),
            arrived.reshape(devices // peers, peers, -1, TILE),
            table_high,
            table_low,
            strength,
            mean,
        )
        if sweep == 0:
            near[2], _ = lax.optimization_barrier((near[2], back))
            rungs = bf16((own, 2 * TILE, 2 * TILE))
            rungs = pl.pallas_call(
                functools.partial(window_ladder_kernel, own),
                out_shape=(rungs, rungs),
                in_specs=[SMEM] + [IN_HBM] * 5,
                out_specs=(VMEM, VMEM),
                scratch_shapes=[pltpu.VMEM(near_shape.shape, jnp.float32), pltpu.SemaphoreType.DMA((2,))],
                compiler_params=limit(8),
            )(here_array, *histories, *[pltpu.with_memory_space_constraint(x, pltpu.HBM) for x in near])
            propagator_own = own_block(propagator, own, 1)
        arrived = send_beside(back) if sweep else lax.all_to_all(back, both_axes, 0, 0, tiled=True)
        arrived = arrived.reshape(2 * count, TILE)
        if sweep + 1 < PASSES:
            send = call(
                functools.partial(window_kernel, own),
                f32((count, TILE)),
                arrived,
                propagator_own,
                *rungs,
            ).reshape(devices, own, TILE)

    def finish(new_slice, coefficients_of, step):
        before = () if new_slice is None else (new_slice,)
        return pl.pallas_call(
            functools.partial(final_kernel, own, len(before)),
            out_shape=pltpu.HBM(hist_lesser.shape, jnp.float32),
            in_specs=[SMEM, VMEM, VMEM] + [IN_HBM] * (1 + len(before)),
            out_specs=IN_HBM,
            scratch_shapes=[
                pltpu.VMEM(ladder_shape, jnp.bfloat16),
                pltpu.VMEM((2, own, ORB, columns), jnp.float32),
                pltpu.SemaphoreType.DMA((own,)),
                pltpu.SemaphoreType.DMA((own,)),
            ],
            input_output_aliases={4: 0} if before else {},
            compiler_params=limit(6),
        )(
            (here ^ step).reshape(1).astype(jnp.int32),
            coefficients_of,
            propagator,
            pltpu.with_memory_space_constraint(ladders[step], pltpu.HBM) if step < 3 else ladders[step],
            *before,
        )

    def exchange(x, step):
        return lax.ppermute(x, "tm", [(t, t ^ step) for t in range(peers)])

    across = exchange(arrived, 2)
    beside_me = exchange(arrived, 1)
    new_slice = finish(None, arrived, 0)
    new_slice = finish(new_slice, beside_me, 1)
    across, new_slice = lax.optimization_barrier((across, new_slice))
    beyond = exchange(across, 1)
    new_slice = finish(new_slice, across, 2)
    return finish(new_slice, beyond, 3)


def on_device(hist_lesser, *others):
    peers = lax.axis_size("tm")
    devices = lax.axis_size("mom") * peers
    fits = devices == 2 * ORB and peers == 4 and hist_lesser.shape[1:] == (2 * ORB, ORB, 4 * TILE)
    return (on_device_tiled if fits else on_device_any)(hist_lesser, *others)


def solution(mesh):
    return jax.shard_map(
        on_device,
        mesh=mesh,
        in_specs=(
            P(None, "mom", None, "tm"),
            P(None, "mom", None, "tm"),
            P(None, "mom", None, None),
            P(),
            P(),
            P(),
        ),
        out_specs=P(None, "mom", None, "tm"),
        check_vma=False,
    )
```

```python
import functools
import math

import jax
import jax.numpy as jnp
import numpy as np
from jax import lax
from jax.experimental import pallas as pl
from jax.experimental.pallas import tpu as pltpu
from jax.sharding import PartitionSpec as P

KX = 16
KY = 16
ORB = 16
W = 8
PASSES = 3


HIGHEST = lax.Precision.HIGHEST


def shifted(x, axis, by):
    peers = lax.axis_size(axis)
    pairs = [(i, i + by) for i in range(peers) if 0 <= i + by < peers]
    return lax.ppermute(x, axis, pairs)


def broadcast(x, axis, root):
    mine = lax.axis_index(axis) == root
    return lax.psum(jnp.where(mine, x, jnp.zeros_like(x)), axis)


def momentum_tables():
    index = jnp.arange(KX * KY, dtype=jnp.int32)
    first = index // KY
    second = index % KY
    turn_x = first[:, None] * first[None, :] % KX
    turn_y = second[:, None] * second[None, :] % KY
    phase = 2.0 * math.pi * (turn_x.astype(jnp.float32) / KX + turn_y.astype(jnp.float32) / KY)
    scale = 1.0 / math.sqrt(KX * KY)
    return (jnp.cos(phase) * scale, jnp.sin(phase) * scale)


def complex_product(pattern, first, second):
    real = jnp.einsum(pattern, first[0], second[0], precision=HIGHEST) - jnp.einsum(
        pattern, first[1], second[1], precision=HIGHEST
    )
    imaginary = jnp.einsum(pattern, first[0], second[1], precision=HIGHEST) + jnp.einsum(
        pattern, first[1], second[0], precision=HIGHEST
    )
    return jnp.stack([real, imaginary])


def back_to_momenta(real, imaginary, cosine, sine):
    out_real = jnp.dot(cosine, real, precision=HIGHEST) + jnp.dot(
        sine, imaginary, precision=HIGHEST
    )
    out_imag = jnp.dot(cosine, imaginary, precision=HIGHEST) - jnp.dot(
        sine, real, precision=HIGHEST
    )
    return jnp.stack([out_real, out_imag])


def local_products(arrived, cosine, sine, strength, lag_mark):
    lag_count = lag_mark.shape[0]
    space_real = jnp.dot(cosine, arrived[0], precision=HIGHEST) - jnp.dot(
        sine, arrived[1], precision=HIGHEST
    )
    space_imag = jnp.dot(cosine, arrived[1], precision=HIGHEST) + jnp.dot(
        sine, arrived[0], precision=HIGHEST
    )
    column_strength = jnp.repeat(strength, lag_count)
    magnitude = column_strength * (space_real * space_real + space_imag * space_imag)
    lesser_real = magnitude * space_real
    lesser_imag = magnitude * space_imag
    pair_real = column_strength * (space_real * space_real - space_imag * space_imag)
    pair_imag = column_strength * 2.0 * space_real * space_imag
    return (
        back_to_momenta(lesser_real, lesser_imag, cosine, sine),
        back_to_momenta(pair_real, pair_imag, cosine, sine),
    )


def self_energies(window, cosine, sine, strength, mf_weight, last_mark):
    momenta_here = window.shape[1]
    outgoing = window.reshape(2, momenta_here, ORB * ORB * W)
    arrived = lax.all_to_all(outgoing, "mom", split_axis=2, concat_axis=1, tiled=True)
    lesser_r, pair_r = local_products(arrived, cosine, sine, strength, last_mark)
    back_lesser, back_pair = (
        lax.all_to_all(lesser_r, "mom", split_axis=1, concat_axis=2, tiled=True),
        lax.all_to_all(pair_r, "mom", split_axis=1, concat_axis=2, tiled=True),
    )
    sigma = back_lesser.reshape(2, momenta_here, ORB, ORB, W)
    pair_k = back_pair.reshape(2, momenta_here, ORB, ORB, W)
    own_total = jnp.sum(window[..., W - 1], axis=1)
    occupation = lax.psum(own_total, "mom") / (KX * KY)
    sigma = sigma + (mf_weight.reshape(ORB, ORB) * occupation)[:, None, :, :, None] * last_mark
    return (sigma, pair_k)


def collide(sigma, pair_k, lag_weight, padded_r, padded_l, first, count):
    weighted_sigma = sigma * lag_weight
    weighted_pair = pair_k * lag_weight

    def ladder(padded):
        region = lax.dynamic_slice_in_dim(padded, first * ORB, (count + W - 1) * ORB, 3)
        return jnp.stack(
            [region[..., offset * ORB : (offset + count) * ORB] for offset in range(W)], axis=3
        )

    return complex_product("kabm,kbmx->kax", weighted_sigma, ladder(padded_r)) + complex_product(
        "kabm,kbmx->kax", weighted_pair, ladder(padded_l)
    )


def on_device_any(hist_lesser, hist_retarded, propagator, coupling, mf_weight, lag_weight):
    momenta_here = hist_lesser.shape[1]
    times_here = hist_lesser.shape[3] // ORB
    cosine, sine = momentum_tables()
    lesser = hist_lesser.reshape(2, momenta_here, ORB, times_here, ORB)
    start = complex_product("kab,kbjc->kajc", propagator, lesser).reshape(
        2, momenta_here, ORB, times_here * ORB
    )
    rim_width = (W - 1) * ORB
    rim_retarded, rim_lesser = shifted(
        (
            hist_retarded[..., times_here * ORB - rim_width :],
            hist_lesser[..., times_here * ORB - rim_width :],
        ),
        "tm",
        1,
    )
    padded_r = jnp.concatenate([rim_retarded, hist_retarded], axis=3)
    padded_l = jnp.concatenate([rim_lesser, hist_lesser], axis=3)
    block = min(32, times_here)
    count_blocks = times_here // block
    window_start = (times_here - W) * ORB
    pair_count = ORB * ORB // lax.axis_size("mom")
    strength = lax.dynamic_slice_in_dim(
        coupling * coupling, lax.axis_index("mom") * pair_count, pair_count, 0
    )
    last_mark = (jnp.arange(W) == W - 1).astype(jnp.float32)
    owner = lax.axis_size("tm") - 1
    current = start[..., window_start:]
    full_slice = start
    for sweep in range(PASSES):
        shared = broadcast(current, "tm", owner)
        window = jnp.transpose(shared.reshape(2, momenta_here, ORB, W, ORB), (0, 1, 2, 4, 3))
        sigma, pair_k = self_energies(window, cosine, sine, strength, mf_weight, last_mark)
        if sweep + 1 < PASSES:
            collision = collide(sigma, pair_k, lag_weight, padded_r, padded_l, times_here - W, W)
            current = start[..., window_start:] + jnp.stack([collision[1], -collision[0]])
        else:
            blocks_out = lax.map(
                lambda number: collide(
                    sigma, pair_k, lag_weight, padded_r, padded_l, number * block, block
                ),
                jnp.arange(count_blocks, dtype=jnp.int32),
            )
            collision = jnp.moveaxis(blocks_out, 0, 3).reshape(
                2, momenta_here, ORB, times_here * ORB
            )
            full_slice = start + jnp.stack([collision[1], -collision[0]])
            current = full_slice[..., window_start:]
    return full_slice


VMEM = pl.BlockSpec(memory_space=pltpu.VMEM)
SMEM = pl.BlockSpec(memory_space=pltpu.SMEM)
IN_HBM = pl.BlockSpec(memory_space=pltpu.HBM)
HALF = W * ORB // 2
TILE = W * ORB


def limit(mebibytes):
    return pltpu.CompilerParams(vmem_limit_bytes=mebibytes * 1024 * 1024)


def halves(x):
    high = x.astype(jnp.bfloat16)
    return high, (x - high.astype(jnp.float32)).astype(jnp.bfloat16)


def matmul(first, second):
    return jnp.dot(first, second, preferred_element_type=jnp.float32)


def fourier_tables():
    index = np.arange(KX * KY)
    turn = np.outer(index // KY, index // KY) / KX + np.outer(index % KY, index % KY) / KY
    phase = 2.0 * np.pi * (turn % 1.0)
    table = np.concatenate([np.cos(phase), np.sin(phase)]) / math.sqrt(KX * KY)
    high = table.astype(jnp.bfloat16)
    low = (table - high.astype(np.float64)).astype(jnp.bfloat16)
    return jnp.asarray(high), jnp.asarray(low)


def lower_lanes(shape):
    return lax.broadcasted_iota(jnp.int32, shape, 1) < HALF


def store_window(send_ref, k, own, real, imag):
    lower = lower_lanes(real.shape)
    turned_real = pltpu.roll(real, HALF, 1)
    turned_imag = pltpu.roll(imag, HALF, 1)
    send_ref[pl.ds(k, ORB, stride=2 * own), :] = jnp.where(lower, real, turned_imag)
    send_ref[pl.ds(own + k, ORB, stride=2 * own), :] = jnp.where(lower, turned_real, imag)


def start_all(copies):
    for copy in copies:
        copy.start()
    return copies


def wait_all(copies):
    for copy in copies:
        copy.wait()


def near_copies(histories, near_ref, tm, own, semaphores):
    copies = []
    for kind, ref in enumerate(histories):
        last = ref.shape[3]
        source = ref.at[:, tm * own : (tm + 1) * own, :, last - 2 * TILE :]
        copies.append(pltpu.make_async_copy(source, near_ref.at[pl.ds(2 * kind, 2)], semaphores.at[kind]))
    return copies


def rim_copies(ref, near_ref, own, semaphores):
    copies = []
    for number in range(8):
        part, half, quarter = number // 4, number // 2 % 2, number % 2
        source = ref.at[part, pl.ds((2 * half + quarter) * own, own), :, pl.ds(ref.shape[3] - TILE, TILE)]
        target = near_ref.at[2 * part + half, :, :, pl.ds(quarter * TILE, TILE)]
        copies.append(pltpu.make_async_copy(source, target, semaphores.at[number]))
    return copies


def settings_kernel(index_ref, coupling_ref, mf_ref, lag_ref, strength_ref, mean_ref):
    lane = lax.broadcasted_iota(jnp.int32, strength_ref.shape, 1)
    first = index_ref[0] // 2 * ORB
    lag = index_ref[0] % 2 * (W // 2) + lane // ORB % (W // 2)
    zero = jnp.zeros(strength_ref.shape, jnp.float32)
    coupling, mf, weight = zero, zero, zero
    for b in range(ORB):
        coupling = jnp.where(lane % ORB == b, coupling_ref[first + b], coupling)
        mf = jnp.where(lane % ORB == b, mf_ref[first + b], mf)
    for m in range(W):
        weight = jnp.where(lag == m, lag_ref[m], weight)
    strength_ref[...] = coupling * coupling * weight
    mean_ref[...] = jnp.where((lag == W - 1) & (lane < HALF), mf * weight, zero)


def regions_kernel(own, tm_ref, retarded_ref, lesser_ref, low_ref, high_ref, *others):
    *out_refs, arrive, pass_on = others
    histories = (retarded_ref, lesser_ref)
    momenta, columns = lesser_ref.shape[1], lesser_ref.shape[3]
    half = momenta // 2
    last = len(out_refs)
    windows = start_all(
        [
            pltpu.make_async_copy(
                lesser_ref.at[:, number * half : (number + 1) * half, :, columns - TILE :], ref, arrive.at[number]
            )
            for number, ref in enumerate((low_ref, high_ref))
        ]
    )

    def near():
        return [c for tm, ref in enumerate(out_refs) for c in near_copies(histories, ref, tm, own, pass_on.at[tm])]

    def rims(second):
        pairs = ((0, retarded_ref), (second, lesser_ref))
        return [c for number, ref in pairs for c in rim_copies(ref, out_refs[number], own, pass_on.at[number])]

    edge = (tm_ref[0] == 0) | (tm_ref[0] == last)
    for case, copies in (
        (tm_ref[0] == last, near),
        (tm_ref[0] == 0, lambda: rims(2)),
        (jnp.logical_not(edge), lambda: rims(1)),
    ):

        @pl.when(case)
        def _():
            wait_all(start_all(copies()))

    wait_all(windows)


def first_window_kernel(tm_ref, last, propagator_ref, low_ref, high_ref, send_ref):
    half = low_ref.shape[1]
    upper = tm_ref[0] == last
    first = jnp.where(upper, half, 0)
    for k in range(half):
        left = jnp.concatenate([propagator_ref[part, first + k] for part in range(2)], axis=0)
        window = [jnp.where(upper, high_ref[part, k], low_ref[part, k]) for part in range(2)]
        imag, real = contract(*halves(left), *halves(jnp.concatenate(window, axis=1)), TILE)
        store_window(send_ref, k, half, -real, imag)


def fourier_kernel(arrived_ref, high_ref, low_ref, strength_ref, mean_ref, out_ref):
    count = KX * KY
    useful = count // (arrived_ref.shape[0] * arrived_ref.shape[2])
    x_high, x_low = halves(arrived_ref[:, arrived_ref.shape[1] - useful :].reshape(count, TILE))
    main = matmul(high_ref[...], jnp.concatenate([x_high, x_low], axis=1))
    turned = main[:, :TILE] + main[:, TILE:] + matmul(low_ref[...], x_high)
    lower = lower_lanes((count, TILE))
    sine_part = pltpu.roll(turned[count:], HALF, 1)
    here = turned[:count] + jnp.where(lower, -sine_part, sine_part)
    swapped = pltpu.roll(here, HALF, 1)
    real = jnp.where(lower, here, swapped)
    imag = jnp.where(lower, swapped, here)
    real_square = real * real
    imag_square = imag * imag
    size = real_square + imag_square
    strength = strength_ref[...]
    out_real = strength * jnp.where(lower, size * real, real_square - imag_square)
    out_imag = strength * jnp.where(lower, size * imag, 2.0 * real * imag)
    origin = (lax.broadcasted_iota(jnp.int32, (count, TILE), 0) == 0).astype(jnp.float32)
    mean = origin * mean_ref[...]
    out_real = out_real + mean * real
    out_imag = out_imag + mean * imag
    real_high, real_low = halves(out_real)
    imag_high, imag_low = halves(out_imag)
    y_high = jnp.concatenate([real_high, imag_high], axis=1)
    y_low = jnp.concatenate([real_low, imag_low], axis=1)
    back = matmul(high_ref[...], y_high) + matmul(low_ref[...], y_high) + matmul(high_ref[...], y_low)
    devices, rows, _ = out_ref.shape
    own = rows // 2
    out_ref[:, :own] = (back[:count, :TILE] + back[count:, TILE:]).reshape(devices, own, TILE)
    out_ref[:, own:] = (back[:count, TILE:] - back[count:, :TILE]).reshape(devices, own, TILE)


def coefficients(arrived_ref, propagator_ref, k, own):
    pieces = []
    for part, start in enumerate((-propagator_ref[1], propagator_ref[0])):
        first, second = (
            arrived_ref[pl.ds((2 * half + part) * own + k, ORB, stride=4 * own), :] for half in range(2)
        )
        start = jnp.concatenate([jnp.zeros((ORB, TILE - ORB), jnp.float32), start], axis=1)
        pieces.append((first, second + start))
    return pieces


def ladder(regions, width):
    rows = []
    for half in range(2):
        for kind in range(2):
            for lag in range(W // 2):
                offset = ORB * (1 + half * (W // 2) + lag)
                rows.append(jnp.concatenate([x[:, offset : offset + width] for x in regions[kind]], axis=1))
    return jnp.concatenate(rows, axis=0)


def contract(left_high, left_low, right_high, right_low, width):
    rows = left_high.shape[0]
    main = matmul(jnp.concatenate([left_high, left_low], axis=0), right_high)
    both = main[:rows] + main[rows:] + matmul(left_high, right_low)
    half = rows // 2
    real = both[:half, :width] - both[half:, width:]
    imag = both[:half, width:] + both[half:, :width]
    return imag, -real


def window_ladder_kernel(own, tm_ref, retarded_ref, lesser_ref, *others):
    *near_refs, high_ref, low_ref, near_ref, arrive = others
    for tm in range(len(near_refs) + 1):

        @pl.when(tm_ref[0] == tm)
        def _():
            if tm < len(near_refs):
                copies = [pltpu.make_async_copy(near_refs[tm], near_ref, arrive.at[0])]
            else:
                copies = near_copies((retarded_ref, lesser_ref), near_ref, tm, own, arrive)
            wait_all(start_all(copies))

    for k in range(own):
        regions = [[near_ref[2 * kind + part, k] for part in range(2)] for kind in range(2)]
        high_ref[k], low_ref[k] = halves(ladder(regions, TILE))


def window_kernel(own, arrived_ref, propagator_ref, high_ref, low_ref, send_ref):
    for k in range(own):
        pieces = coefficients(arrived_ref, propagator_ref.at[:, k], k, own)
        left_high, left_low = halves(jnp.concatenate([jnp.concatenate(pair, axis=1) for pair in pieces], axis=0))
        real, imag = contract(left_high, left_low, high_ref[k], low_ref[k], TILE)
        store_window(send_ref, k, own, real, imag)


def trade(tiles):
    group = lax.broadcasted_iota(jnp.int32, tiles[0].shape, 1) // ORB
    for bit in (2, 1):
        first = (group & bit) == 0
        shift = bit * ORB
        traded = list(tiles)
        for i in range(4):
            if not i & bit:
                x, y = tiles[i], tiles[i | bit]
                traded[i] = jnp.where(first, x, pltpu.roll(y, shift, 1))
                traded[i | bit] = jnp.where(first, pltpu.roll(x, TILE - shift, 1), y)
        tiles = traded
    return tiles


def final_ladder_kernel(tm_ref, retarded_ref, lesser_ref, *others):
    *others, region_ref, ladder_ref, arrive, arrive_rim, leave = others
    rim_refs, outs = others[:3], others[3:]
    count, rows_each = ladder_ref.shape[0], ladder_ref.shape[1] // 2
    high_ref = ladder_ref.at[:, :rows_each]
    low_ref = ladder_ref.at[:, rows_each:]
    own = count // len(outs)
    blocks = len(outs)
    momenta = pl.ds(tm_ref[1] // blocks * count, count)
    fetches = start_all(
        [
            pltpu.make_async_copy(
                ref.at[:, momenta],
                region_ref.at[pl.ds(2 * kind, 2), :, :, pl.ds(TILE, ref.shape[3])],
                arrive.at[kind],
            )
            for kind, ref in enumerate((retarded_ref, lesser_ref))
        ]
    )

    def rims(second, quarters):
        copies = []
        for kind, ref in enumerate((rim_refs[0], rim_refs[second])):
            for part in range(2):
                for number, quarter in enumerate(quarters):
                    source = ref.at[2 * part + tm_ref[1] // 2, :, :, pl.ds(quarter * TILE, TILE)]
                    target = region_ref.at[2 * kind + part, pl.ds(number * own, own), :, pl.ds(0, TILE)]
                    copies.append(pltpu.make_async_copy(source, target, arrive_rim.at[2 * kind + part, number]))
        return copies

    @pl.when(tm_ref[0] == 0)
    def _():
        region_ref[:, :, :, :TILE] = jnp.zeros((4, count, ORB, TILE), jnp.float32)

    for second, case in ((2, tm_ref[0] == 1), (1, tm_ref[0] > 1)):
        for quarters in [(0, 1)] if blocks == 2 else [(0,), (1,)]:

            @pl.when(case if blocks == 2 else case & (tm_ref[1] % 2 == quarters[0]))
            def _():
                wait_all(start_all(rims(second, quarters)))

    wait_all(fetches)

    def leaving(block, n):
        k = block * own + n
        return [pltpu.make_async_copy(ladder_ref.at[k], outs[block].at[n], leave.at[k])]

    def one(block, n, carry):
        k = block * own + n
        source = (tm_ref[1] % blocks ^ block) * own + n
        for part in range(2):
            region = jnp.concatenate([region_ref[2 * kind + part, source] for kind in range(2)], axis=0)
            lanes = pl.ds(part * TILE, TILE)
            tiles = [region[:, t * TILE : (t + 1) * TILE] for t in range(5)]
            first, third = trade(tiles[:4]), trade(tiles[1:])
            lower = lower_lanes(tiles[0].shape)
            second = [pltpu.roll(jnp.where(lower, z, x), HALF, 1) for x, z in zip(first, third)]
            for step, tile in enumerate((first + second + third)[1:]):
                high, low = halves(tile)
                for kind in range(2):
                    rows = pl.ds(step // 4 * TILE + kind * HALF + step % 4 * ORB, ORB)
                    high_ref[k, rows, lanes] = high[kind * ORB : (kind + 1) * ORB]
                    low_ref[k, rows, lanes] = low[kind * ORB : (kind + 1) * ORB]
            for kind in range(2):
                rows = pl.ds(2 * TILE + kind * HALF + 3 * ORB, ORB)
                high_ref[k, rows, lanes] = jnp.zeros((ORB, TILE), jnp.bfloat16)
                low_ref[k, rows, lanes] = jnp.zeros((ORB, TILE), jnp.bfloat16)
        start_all(leaving(block, n))
        return carry

    for block in range(blocks):
        lax.fori_loop(0, own, functools.partial(one, block), 0)
    for block in range(blocks):
        lax.fori_loop(0, own, lambda n, c: (wait_all(leaving(block, n)), c)[1], 0)


def stepped(pair):
    first, second = pair
    place = lax.broadcasted_iota(jnp.int32, first.shape, 1) // ORB % 4
    rows = [jnp.concatenate([first, second, jnp.zeros_like(first)], axis=1)]
    for s in range(1, 4):
        stay = place >= s
        up, over = s * ORB, TILE + (s - 4) * ORB
        rows.append(
            jnp.concatenate(
                [
                    jnp.where(stay, pltpu.roll(first, up, 1), 0.0),
                    jnp.where(stay, pltpu.roll(second, up, 1), pltpu.roll(first, over, 1)),
                    jnp.where(stay, 0.0, pltpu.roll(second, over, 1)),
                ],
                axis=1,
            )
        )
    return jnp.concatenate(rows, axis=0)


def final_kernel(own, fetched, following, before, tm_ref, arrived_ref, propagator_ref, ladder_ref, *others):
    others = list(others)
    source_ref = others.pop(0) if following else None
    others = others[before:]
    out_ref = others.pop(0)
    next_ref = others.pop(0) if following else None
    out_here, arrive, leave, *ladder_here = others
    ladder_here = ladder_ref if fetched else ladder_here[0]
    base = tm_ref[0] * own
    group = own // 2
    groups = own // group
    rows_each = ladder_here.shape[1] // 2

    def arriving(number):
        momenta = pl.ds(number * group, group)
        return [pltpu.make_async_copy(ladder_ref.at[momenta], ladder_here.at[momenta], arrive.at[number])]

    def leaving(number):
        momenta = pl.ds(number * group, group)
        source, target = out_here.at[:, momenta], out_ref.at[:, pl.ds(base + number * group, group)]
        return [pltpu.make_async_copy(source, target, leave.at[number])]

    def one(number, carry):
        if not fetched:
            wait_all(arriving(number))
        for n in range(group):
            k = number * group + n
            pieces = coefficients(arrived_ref, propagator_ref.at[:, base + k], k, own)
            left_high, left_low = halves(jnp.concatenate([stepped(pair) for pair in pieces], axis=0))
            right = ladder_here.at[k]
            parts = contract(left_high, left_low, right[:rows_each], right[rows_each:], TILE)
            for part, value in enumerate(parts):
                tiles = trade([value[s * ORB : (s + 1) * ORB] for s in range(4)])
                for t, tile in enumerate(tiles):
                    out_here[part, k, :, t * TILE : (t + 1) * TILE] = tile
        start_all(leaving(number))
        return carry

    if not fetched:
        for number in range(groups):
            start_all(arriving(number))
    coming = [pltpu.make_async_copy(source_ref, next_ref, arrive.at[groups])] if following else []
    start_all(coming)
    lax.fori_loop(0, groups, one, 0)
    wait_all(coming)
    for number in range(groups):
        wait_all(leaving(number))


def own_block(x, own, axis):
    return lax.dynamic_slice_in_dim(x, lax.axis_index("tm") * own, own, axis)


def on_device_tiled(hist_lesser, hist_retarded, propagator, coupling, mf_weight, lag_weight):
    both_axes = ("mom", "tm")
    momenta_here = hist_lesser.shape[1]
    columns = hist_lesser.shape[3]
    peers = lax.axis_size("tm")
    devices = lax.axis_size("mom") * peers
    own = momenta_here // peers
    count = KX * KY

    f32 = functools.partial(jax.ShapeDtypeStruct, dtype=jnp.float32)
    bf16 = functools.partial(jax.ShapeDtypeStruct, dtype=jnp.bfloat16)

    def call(kernel, shapes, *operands):
        return pl.pallas_call(
            kernel,
            out_shape=shapes,
            in_specs=[SMEM if x.dtype == jnp.int32 else VMEM for x in operands],
            out_specs=jax.tree.map(lambda _: VMEM, shapes),
            compiler_params=limit(12),
        )(*operands)

    half = momenta_here // 2
    window_shape = f32((2, half, ORB, TILE))
    near_shape = f32((4, own, ORB, 2 * TILE))
    here = lax.axis_index("tm")
    here_array = here.reshape(1).astype(jnp.int32)
    low, high, *near = pl.pallas_call(
        functools.partial(regions_kernel, own),
        out_shape=(window_shape, window_shape, near_shape, near_shape, near_shape),
        in_specs=[SMEM, IN_HBM, IN_HBM],
        out_specs=(VMEM,) * 5,
        scratch_shapes=[pltpu.SemaphoreType.DMA((2,)), pltpu.SemaphoreType.DMA((peers - 1, 8))],
        compiler_params=limit(4),
    )(here_array, *(pltpu.with_memory_space_constraint(x, pltpu.HBM) for x in (hist_retarded, hist_lesser)))
    neighbours = [(0, 1), (1, 0), (2, 3), (3, 2)]
    low = lax.ppermute(low, "tm", neighbours)
    send = call(
        lambda tm_ref, *refs: first_window_kernel(tm_ref, peers - 1, *refs),
        f32((devices * half, TILE)),
        here_array,
        propagator,
        low,
        high,
    ).reshape(devices, half, TILE)
    near[0] = lax.ppermute(near[0], "tm", [(3, 0), (0, 1), (1, 2), (2, 3)])
    near[1] = lax.ppermute(near[1], "tm", [(3, 1), (1, 2), (2, 3), (0, 0)])
    send, near[2], hist_lesser, hist_retarded, coupling, mf_weight, lag_weight = lax.optimization_barrier(
        (send, near[2], hist_lesser, hist_retarded, coupling, mf_weight, lag_weight)
    )
    near[2] = lax.ppermute(near[2], "tm", neighbours)
    histories = [pltpu.with_memory_space_constraint(x, pltpu.HBM) for x in (hist_retarded, hist_lesser)]
    me = lax.axis_index("mom") * peers + here
    strength, mean = pl.pallas_call(
        settings_kernel,
        out_shape=(f32((1, TILE)), f32((1, TILE))),
        in_specs=[SMEM] * 4,
        out_specs=(VMEM,) * 2,
        compiler_params=limit(4),
    )(me.reshape(1).astype(jnp.int32), coupling, mf_weight, lag_weight)
    table_high, table_low = fourier_tables()

    ladders = {}
    ladder_shape = (own, 2 * 3 * TILE, 2 * TILE)

    def send_beside(sent, step, blocks):
        edges = [hist_retarded, hist_lesser, *near]
        if step:
            sent, *edges = lax.optimization_barrier((sent, *edges))
        arrived = lax.all_to_all(sent, both_axes, 0, 0, tiled=True)
        ladder = pl.pallas_call(
            final_ladder_kernel,
            out_shape=[pltpu.HBM(ladder_shape, jnp.bfloat16)] * blocks,
            in_specs=[SMEM] + [IN_HBM] * 5,
            out_specs=[IN_HBM] * blocks,
            scratch_shapes=[
                pltpu.VMEM((4, blocks * own, ORB, TILE + columns), jnp.float32),
                pltpu.VMEM((blocks * own, *ladder_shape[1:]), jnp.bfloat16),
                pltpu.SemaphoreType.DMA((2,)),
                pltpu.SemaphoreType.DMA((4, 2)),
                pltpu.SemaphoreType.DMA((blocks * own,)),
            ],
            compiler_params=limit(6 * blocks),
        )(
            jnp.stack([here, here ^ step]).astype(jnp.int32),
            *(pltpu.with_memory_space_constraint(x, pltpu.HBM) for x in edges),
        )
        arrived, *ladder = lax.optimization_barrier((arrived, *ladder))
        ladders.update(zip(range(step, step + blocks), ladder))
        return arrived

    def send_alone(sent):
        return lax.all_to_all(sent, both_axes, 0, 0, tiled=True)

    send_out = [send_alone, send_alone, lambda sent: send_beside(sent, 1, 1)]
    send_back = [lambda sent: send_beside(sent, 0, 1), send_alone, lambda sent: send_beside(sent, 2, 2)]
    for sweep in range(PASSES):
        arrived = send_out[sweep](send)
        back = call(
            fourier_kernel,
            f32((devices, 2 * own, TILE)),
            arrived.reshape(devices // peers, peers, -1, TILE),
            table_high,
            table_low,
            strength,
            mean,
        )
        if sweep == 0:
            near[2], _ = lax.optimization_barrier((near[2], back))
            rungs = bf16((own, 2 * TILE, 2 * TILE))
            rungs = pl.pallas_call(
                functools.partial(window_ladder_kernel, own),
                out_shape=(rungs, rungs),
                in_specs=[SMEM] + [IN_HBM] * 5,
                out_specs=(VMEM, VMEM),
                scratch_shapes=[pltpu.VMEM(near_shape.shape, jnp.float32), pltpu.SemaphoreType.DMA((2,))],
                compiler_params=limit(8),
            )(here_array, *histories, *[pltpu.with_memory_space_constraint(x, pltpu.HBM) for x in near])
            propagator_own = own_block(propagator, own, 1)
        arrived = send_back[sweep](back)
        arrived = arrived.reshape(2 * count, TILE)
        if sweep + 1 < PASSES:
            send = call(
                functools.partial(window_kernel, own),
                f32((count, TILE)),
                arrived,
                propagator_own,
                *rungs,
            ).reshape(devices, own, TILE)

    def finish(new_slice, ladder, coefficients_of, step):
        before = [] if new_slice is None else [new_slice]
        following = [pltpu.with_memory_space_constraint(ladders[step + 1], pltpu.HBM)] if step % 2 == 0 else []
        fetched = ladder is not None
        if not fetched:
            ladder = pltpu.with_memory_space_constraint(ladders[step], pltpu.HBM)
        scratch = [
            pltpu.VMEM((2, own, ORB, columns), jnp.float32),
            pltpu.SemaphoreType.DMA((3,)),
            pltpu.SemaphoreType.DMA((2,)),
        ]
        new_slice, *ladder = pl.pallas_call(
            functools.partial(final_kernel, own, fetched, len(following), len(before)),
            out_shape=[pltpu.HBM(hist_lesser.shape, jnp.float32)] + [bf16(ladder_shape)] * len(following),
            in_specs=[SMEM, VMEM, VMEM, VMEM if fetched else IN_HBM] + [IN_HBM] * len(following + before),
            out_specs=[IN_HBM] + [VMEM] * len(following),
            scratch_shapes=scratch if fetched else scratch + [pltpu.VMEM(ladder_shape, jnp.bfloat16)],
            input_output_aliases={4 + len(following): 0} if before else {},
            compiler_params=limit(6),
        )((here ^ step).reshape(1).astype(jnp.int32), coefficients_of, propagator, ladder, *following, *before)
        return new_slice, *ladder

    def exchange(x, step):
        return lax.ppermute(x, "tm", [(t, t ^ step) for t in range(peers)])

    across = exchange(arrived, 2)
    beside_me = exchange(arrived, 1)
    new_slice, ladder = finish(None, None, arrived, 0)
    (new_slice,) = finish(new_slice, ladder, beside_me, 1)
    across, new_slice = lax.optimization_barrier((across, new_slice))
    beyond = exchange(across, 1)
    new_slice, ladder = finish(new_slice, None, across, 2)
    return finish(new_slice, ladder, beyond, 3)[0]


def on_device(hist_lesser, *others):
    peers = lax.axis_size("tm")
    devices = lax.axis_size("mom") * peers
    fits = devices == 2 * ORB and peers == 4 and hist_lesser.shape[1:] == (2 * ORB, ORB, 4 * TILE)
    return (on_device_tiled if fits else on_device_any)(hist_lesser, *others)


def solution(mesh):
    return jax.shard_map(
        on_device,
        mesh=mesh,
        in_specs=(
            P(None, "mom", None, "tm"),
            P(None, "mom", None, "tm"),
            P(None, "mom", None, None),
            P(),
            P(),
            P(),
        ),
        out_specs=P(None, "mom", None, "tm"),
        check_vma=False,
    )
```

```python
import functools
import math

import jax
import jax.numpy as jnp
import numpy as np
from jax import lax
from jax.experimental import pallas as pl
from jax.experimental.pallas import tpu as pltpu
from jax.sharding import PartitionSpec as P

KX = 16
KY = 16
ORB = 16
W = 8
PASSES = 3


HIGHEST = lax.Precision.HIGHEST


def shifted(x, axis, by):
    peers = lax.axis_size(axis)
    pairs = [(i, i + by) for i in range(peers) if 0 <= i + by < peers]
    return lax.ppermute(x, axis, pairs)


def broadcast(x, axis, root):
    mine = lax.axis_index(axis) == root
    return lax.psum(jnp.where(mine, x, jnp.zeros_like(x)), axis)


def momentum_tables():
    index = jnp.arange(KX * KY, dtype=jnp.int32)
    first = index // KY
    second = index % KY
    turn_x = first[:, None] * first[None, :] % KX
    turn_y = second[:, None] * second[None, :] % KY
    phase = 2.0 * math.pi * (turn_x.astype(jnp.float32) / KX + turn_y.astype(jnp.float32) / KY)
    scale = 1.0 / math.sqrt(KX * KY)
    return (jnp.cos(phase) * scale, jnp.sin(phase) * scale)


def complex_product(pattern, first, second):
    real = jnp.einsum(pattern, first[0], second[0], precision=HIGHEST) - jnp.einsum(
        pattern, first[1], second[1], precision=HIGHEST
    )
    imaginary = jnp.einsum(pattern, first[0], second[1], precision=HIGHEST) + jnp.einsum(
        pattern, first[1], second[0], precision=HIGHEST
    )
    return jnp.stack([real, imaginary])


def back_to_momenta(real, imaginary, cosine, sine):
    out_real = jnp.dot(cosine, real, precision=HIGHEST) + jnp.dot(
        sine, imaginary, precision=HIGHEST
    )
    out_imag = jnp.dot(cosine, imaginary, precision=HIGHEST) - jnp.dot(
        sine, real, precision=HIGHEST
    )
    return jnp.stack([out_real, out_imag])


def local_products(arrived, cosine, sine, strength, lag_mark):
    lag_count = lag_mark.shape[0]
    space_real = jnp.dot(cosine, arrived[0], precision=HIGHEST) - jnp.dot(
        sine, arrived[1], precision=HIGHEST
    )
    space_imag = jnp.dot(cosine, arrived[1], precision=HIGHEST) + jnp.dot(
        sine, arrived[0], precision=HIGHEST
    )
    column_strength = jnp.repeat(strength, lag_count)
    magnitude = column_strength * (space_real * space_real + space_imag * space_imag)
    lesser_real = magnitude * space_real
    lesser_imag = magnitude * space_imag
    pair_real = column_strength * (space_real * space_real - space_imag * space_imag)
    pair_imag = column_strength * 2.0 * space_real * space_imag
    return (
        back_to_momenta(lesser_real, lesser_imag, cosine, sine),
        back_to_momenta(pair_real, pair_imag, cosine, sine),
    )


def self_energies(window, cosine, sine, strength, mf_weight, last_mark):
    momenta_here = window.shape[1]
    outgoing = window.reshape(2, momenta_here, ORB * ORB * W)
    arrived = lax.all_to_all(outgoing, "mom", split_axis=2, concat_axis=1, tiled=True)
    lesser_r, pair_r = local_products(arrived, cosine, sine, strength, last_mark)
    back_lesser, back_pair = (
        lax.all_to_all(lesser_r, "mom", split_axis=1, concat_axis=2, tiled=True),
        lax.all_to_all(pair_r, "mom", split_axis=1, concat_axis=2, tiled=True),
    )
    sigma = back_lesser.reshape(2, momenta_here, ORB, ORB, W)
    pair_k = back_pair.reshape(2, momenta_here, ORB, ORB, W)
    own_total = jnp.sum(window[..., W - 1], axis=1)
    occupation = lax.psum(own_total, "mom") / (KX * KY)
    sigma = sigma + (mf_weight.reshape(ORB, ORB) * occupation)[:, None, :, :, None] * last_mark
    return (sigma, pair_k)


def collide(sigma, pair_k, lag_weight, padded_r, padded_l, first, count):
    weighted_sigma = sigma * lag_weight
    weighted_pair = pair_k * lag_weight

    def ladder(padded):
        region = lax.dynamic_slice_in_dim(padded, first * ORB, (count + W - 1) * ORB, 3)
        return jnp.stack(
            [region[..., offset * ORB : (offset + count) * ORB] for offset in range(W)], axis=3
        )

    return complex_product("kabm,kbmx->kax", weighted_sigma, ladder(padded_r)) + complex_product(
        "kabm,kbmx->kax", weighted_pair, ladder(padded_l)
    )


def on_device_any(hist_lesser, hist_retarded, propagator, coupling, mf_weight, lag_weight):
    momenta_here = hist_lesser.shape[1]
    times_here = hist_lesser.shape[3] // ORB
    cosine, sine = momentum_tables()
    lesser = hist_lesser.reshape(2, momenta_here, ORB, times_here, ORB)
    start = complex_product("kab,kbjc->kajc", propagator, lesser).reshape(
        2, momenta_here, ORB, times_here * ORB
    )
    rim_width = (W - 1) * ORB
    rim_retarded, rim_lesser = shifted(
        (
            hist_retarded[..., times_here * ORB - rim_width :],
            hist_lesser[..., times_here * ORB - rim_width :],
        ),
        "tm",
        1,
    )
    padded_r = jnp.concatenate([rim_retarded, hist_retarded], axis=3)
    padded_l = jnp.concatenate([rim_lesser, hist_lesser], axis=3)
    block = min(32, times_here)
    count_blocks = times_here // block
    window_start = (times_here - W) * ORB
    pair_count = ORB * ORB // lax.axis_size("mom")
    strength = lax.dynamic_slice_in_dim(
        coupling * coupling, lax.axis_index("mom") * pair_count, pair_count, 0
    )
    last_mark = (jnp.arange(W) == W - 1).astype(jnp.float32)
    owner = lax.axis_size("tm") - 1
    current = start[..., window_start:]
    full_slice = start
    for sweep in range(PASSES):
        shared = broadcast(current, "tm", owner)
        window = jnp.transpose(shared.reshape(2, momenta_here, ORB, W, ORB), (0, 1, 2, 4, 3))
        sigma, pair_k = self_energies(window, cosine, sine, strength, mf_weight, last_mark)
        if sweep + 1 < PASSES:
            collision = collide(sigma, pair_k, lag_weight, padded_r, padded_l, times_here - W, W)
            current = start[..., window_start:] + jnp.stack([collision[1], -collision[0]])
        else:
            blocks_out = lax.map(
                lambda number: collide(
                    sigma, pair_k, lag_weight, padded_r, padded_l, number * block, block
                ),
                jnp.arange(count_blocks, dtype=jnp.int32),
            )
            collision = jnp.moveaxis(blocks_out, 0, 3).reshape(
                2, momenta_here, ORB, times_here * ORB
            )
            full_slice = start + jnp.stack([collision[1], -collision[0]])
            current = full_slice[..., window_start:]
    return full_slice


VMEM = pl.BlockSpec(memory_space=pltpu.VMEM)
SMEM = pl.BlockSpec(memory_space=pltpu.SMEM)
IN_HBM = pl.BlockSpec(memory_space=pltpu.HBM)
HALF = W * ORB // 2
TILE = W * ORB


def limit(mebibytes):
    return pltpu.CompilerParams(vmem_limit_bytes=mebibytes * 1024 * 1024)


def halves(x):
    high = x.astype(jnp.bfloat16)
    return high, (x - high.astype(jnp.float32)).astype(jnp.bfloat16)


def matmul(first, second):
    return jnp.dot(first, second, preferred_element_type=jnp.float32)


def fourier_tables():
    index = np.arange(KX * KY)
    turn = np.outer(index // KY, index // KY) / KX + np.outer(index % KY, index % KY) / KY
    phase = 2.0 * np.pi * (turn % 1.0)
    table = np.concatenate([np.cos(phase), np.sin(phase)]) / math.sqrt(KX * KY)
    high = table.astype(jnp.bfloat16)
    low = (table - high.astype(np.float64)).astype(jnp.bfloat16)
    return jnp.asarray(high), jnp.asarray(low)


def lower_lanes(shape):
    return lax.broadcasted_iota(jnp.int32, shape, 1) < HALF


def store_window(send_ref, k, own, real, imag):
    lower = lower_lanes(real.shape)
    turned_real = pltpu.roll(real, HALF, 1)
    turned_imag = pltpu.roll(imag, HALF, 1)
    send_ref[pl.ds(k, ORB, stride=2 * own), :] = jnp.where(lower, real, turned_imag)
    send_ref[pl.ds(own + k, ORB, stride=2 * own), :] = jnp.where(lower, turned_real, imag)


def start_all(copies):
    for copy in copies:
        copy.start()
    return copies


def wait_all(copies):
    for copy in copies:
        copy.wait()


def near_copies(histories, near_ref, tm, own, semaphores):
    copies = []
    for kind, ref in enumerate(histories):
        last = ref.shape[3]
        source = ref.at[:, tm * own : (tm + 1) * own, :, last - 2 * TILE :]
        copies.append(pltpu.make_async_copy(source, near_ref.at[pl.ds(2 * kind, 2)], semaphores.at[kind]))
    return copies


def rim_copies(ref, near_ref, own, semaphores):
    copies = []
    for number in range(8):
        part, half, quarter = number // 4, number // 2 % 2, number % 2
        source = ref.at[part, pl.ds((2 * half + quarter) * own, own), :, pl.ds(ref.shape[3] - TILE, TILE)]
        target = near_ref.at[2 * part + half, :, :, pl.ds(quarter * TILE, TILE)]
        copies.append(pltpu.make_async_copy(source, target, semaphores.at[number]))
    return copies


def settings_kernel(index_ref, coupling_ref, mf_ref, lag_ref, strength_ref, mean_ref):
    lane = lax.broadcasted_iota(jnp.int32, strength_ref.shape, 1)
    first = index_ref[0] // 2 * ORB
    lag = index_ref[0] % 2 * (W // 2) + lane // ORB % (W // 2)
    zero = jnp.zeros(strength_ref.shape, jnp.float32)
    coupling, mf, weight = zero, zero, zero
    for b in range(ORB):
        coupling = jnp.where(lane % ORB == b, coupling_ref[first + b], coupling)
        mf = jnp.where(lane % ORB == b, mf_ref[first + b], mf)
    for m in range(W):
        weight = jnp.where(lag == m, lag_ref[m], weight)
    strength_ref[...] = coupling * coupling * weight
    mean_ref[...] = jnp.where((lag == W - 1) & (lane < HALF), mf * weight, zero)


def regions_kernel(own, tm_ref, retarded_ref, lesser_ref, low_ref, high_ref, *others):
    *out_refs, arrive, pass_on = others
    histories = (retarded_ref, lesser_ref)
    momenta, columns = lesser_ref.shape[1], lesser_ref.shape[3]
    half = momenta // 2
    last = len(out_refs)
    windows = start_all(
        [
            pltpu.make_async_copy(
                lesser_ref.at[:, number * half : (number + 1) * half, :, columns - TILE :], ref, arrive.at[number]
            )
            for number, ref in enumerate((low_ref, high_ref))
        ]
    )

    def near():
        return [c for tm, ref in enumerate(out_refs) for c in near_copies(histories, ref, tm, own, pass_on.at[tm])]

    def rims(second):
        pairs = ((0, retarded_ref), (second, lesser_ref))
        return [c for number, ref in pairs for c in rim_copies(ref, out_refs[number], own, pass_on.at[number])]

    edge = (tm_ref[0] == 0) | (tm_ref[0] == last)
    for case, copies in (
        (tm_ref[0] == last, near),
        (tm_ref[0] == 0, lambda: rims(2)),
        (jnp.logical_not(edge), lambda: rims(1)),
    ):

        @pl.when(case)
        def _():
            wait_all(start_all(copies()))

    wait_all(windows)


def first_window_kernel(tm_ref, last, propagator_ref, low_ref, high_ref, send_ref):
    half = low_ref.shape[1]
    upper = tm_ref[0] == last
    first = jnp.where(upper, half, 0)
    for k in range(half):
        left = jnp.concatenate([propagator_ref[part, first + k] for part in range(2)], axis=0)
        window = [jnp.where(upper, high_ref[part, k], low_ref[part, k]) for part in range(2)]
        imag, real = contract(*halves(left), *halves(jnp.concatenate(window, axis=1)), TILE)
        store_window(send_ref, k, half, -real, imag)


def fourier_kernel(arrived_ref, high_ref, low_ref, strength_ref, mean_ref, out_ref):
    count = KX * KY
    useful = count // (arrived_ref.shape[0] * arrived_ref.shape[2])
    x_high, x_low = halves(arrived_ref[:, arrived_ref.shape[1] - useful :].reshape(count, TILE))
    main = matmul(high_ref[...], jnp.concatenate([x_high, x_low], axis=1))
    turned = main[:, :TILE] + main[:, TILE:] + matmul(low_ref[...], x_high)
    lower = lower_lanes((count, TILE))
    sine_part = pltpu.roll(turned[count:], HALF, 1)
    here = turned[:count] + jnp.where(lower, -sine_part, sine_part)
    swapped = pltpu.roll(here, HALF, 1)
    real = jnp.where(lower, here, swapped)
    imag = jnp.where(lower, swapped, here)
    real_square = real * real
    imag_square = imag * imag
    size = real_square + imag_square
    strength = strength_ref[...]
    out_real = strength * jnp.where(lower, size * real, real_square - imag_square)
    out_imag = strength * jnp.where(lower, size * imag, 2.0 * real * imag)
    origin = (lax.broadcasted_iota(jnp.int32, (count, TILE), 0) == 0).astype(jnp.float32)
    mean = origin * mean_ref[...]
    out_real = out_real + mean * real
    out_imag = out_imag + mean * imag
    real_high, real_low = halves(out_real)
    imag_high, imag_low = halves(out_imag)
    y_high = jnp.concatenate([real_high, imag_high], axis=1)
    y_low = jnp.concatenate([real_low, imag_low], axis=1)
    back = matmul(high_ref[...], y_high) + matmul(low_ref[...], y_high) + matmul(high_ref[...], y_low)
    devices, rows, _ = out_ref.shape
    own = rows // 2
    out_ref[:, :own] = (back[:count, :TILE] + back[count:, TILE:]).reshape(devices, own, TILE)
    out_ref[:, own:] = (back[:count, TILE:] - back[count:, :TILE]).reshape(devices, own, TILE)


def coefficients(arrived_ref, propagator_ref, k, own):
    pieces = []
    for part, start in enumerate((-propagator_ref[1], propagator_ref[0])):
        first, second = (
            arrived_ref[pl.ds((2 * half + part) * own + k, ORB, stride=4 * own), :] for half in range(2)
        )
        start = jnp.concatenate([jnp.zeros((ORB, TILE - ORB), jnp.float32), start], axis=1)
        pieces.append((first, second + start))
    return pieces


def ladder(regions, width):
    rows = []
    for half in range(2):
        for kind in range(2):
            for lag in range(W // 2):
                offset = ORB * (1 + half * (W // 2) + lag)
                rows.append(jnp.concatenate([x[:, offset : offset + width] for x in regions[kind]], axis=1))
    return jnp.concatenate(rows, axis=0)


def contract(left_high, left_low, right_high, right_low, width):
    rows = left_high.shape[0]
    main = matmul(jnp.concatenate([left_high, left_low], axis=0), right_high)
    both = main[:rows] + main[rows:] + matmul(left_high, right_low)
    half = rows // 2
    real = both[:half, :width] - both[half:, width:]
    imag = both[:half, width:] + both[half:, :width]
    return imag, -real


def window_ladder_kernel(own, tm_ref, retarded_ref, lesser_ref, *others):
    *near_refs, high_ref, low_ref, near_ref, arrive = others
    for tm in range(len(near_refs) + 1):

        @pl.when(tm_ref[0] == tm)
        def _():
            if tm < len(near_refs):
                copies = [pltpu.make_async_copy(near_refs[tm], near_ref, arrive.at[0])]
            else:
                copies = near_copies((retarded_ref, lesser_ref), near_ref, tm, own, arrive)
            wait_all(start_all(copies))

    for k in range(own):
        regions = [[near_ref[2 * kind + part, k] for part in range(2)] for kind in range(2)]
        high_ref[k], low_ref[k] = halves(ladder(regions, TILE))


def window_kernel(own, arrived_ref, propagator_ref, high_ref, low_ref, send_ref):
    for k in range(own):
        pieces = coefficients(arrived_ref, propagator_ref.at[:, k], k, own)
        left_high, left_low = halves(jnp.concatenate([jnp.concatenate(pair, axis=1) for pair in pieces], axis=0))
        real, imag = contract(left_high, left_low, high_ref[k], low_ref[k], TILE)
        store_window(send_ref, k, own, real, imag)


def trade(tiles):
    group = lax.broadcasted_iota(jnp.int32, tiles[0].shape, 1) // ORB
    for bit in (2, 1):
        first = (group & bit) == 0
        shift = bit * ORB
        traded = list(tiles)
        for i in range(4):
            if not i & bit:
                x, y = tiles[i], tiles[i | bit]
                traded[i] = jnp.where(first, x, pltpu.roll(y, shift, 1))
                traded[i | bit] = jnp.where(first, pltpu.roll(x, TILE - shift, 1), y)
        tiles = traded
    return tiles


def final_ladder_kernel(tm_ref, retarded_ref, lesser_ref, *others, meanwhile=lambda: None):
    *others, region_ref, ladder_ref, arrive, arrive_rim, leave = others
    rim_refs, outs = others[:3], others[3:]
    count, rows_each = ladder_ref.shape[0], ladder_ref.shape[1] // 2
    high_ref = ladder_ref.at[:, :rows_each]
    low_ref = ladder_ref.at[:, rows_each:]
    own = count // len(outs)
    blocks = len(outs)
    momenta = pl.ds(tm_ref[1] // blocks * count, count)
    fetches = start_all(
        [
            pltpu.make_async_copy(
                ref.at[:, momenta],
                region_ref.at[pl.ds(2 * kind, 2), :, :, pl.ds(TILE, ref.shape[3])],
                arrive.at[kind],
            )
            for kind, ref in enumerate((retarded_ref, lesser_ref))
        ]
    )

    def rims(second, quarters):
        copies = []
        for kind, ref in enumerate((rim_refs[0], rim_refs[second])):
            for part in range(2):
                for number, quarter in enumerate(quarters):
                    source = ref.at[2 * part + tm_ref[1] // 2, :, :, pl.ds(quarter * TILE, TILE)]
                    target = region_ref.at[2 * kind + part, pl.ds(number * own, own), :, pl.ds(0, TILE)]
                    copies.append(pltpu.make_async_copy(source, target, arrive_rim.at[2 * kind + part, number]))
        return copies

    @pl.when(tm_ref[0] == 0)
    def _():
        region_ref[:, :, :, :TILE] = jnp.zeros((4, count, ORB, TILE), jnp.float32)

    def each_rims(act):
        for second, case in ((2, tm_ref[0] == 1), (1, tm_ref[0] > 1)):
            for quarters in [(0, 1)] if blocks == 2 else [(0,), (1,)]:

                @pl.when(case if blocks == 2 else case & (tm_ref[1] % 2 == quarters[0]))
                def _():
                    act(rims(second, quarters))

    each_rims(start_all)
    meanwhile()
    each_rims(wait_all)
    wait_all(fetches)

    def leaving(block, n):
        k = block * own + n
        return [pltpu.make_async_copy(ladder_ref.at[k], outs[block].at[n], leave.at[k])]

    def one(block, n, carry):
        k = block * own + n
        source = (tm_ref[1] % blocks ^ block) * own + n
        for part in range(2):
            region = jnp.concatenate([region_ref[2 * kind + part, source] for kind in range(2)], axis=0)
            lanes = pl.ds(part * TILE, TILE)
            tiles = [region[:, t * TILE : (t + 1) * TILE] for t in range(5)]
            first, third = trade(tiles[:4]), trade(tiles[1:])
            lower = lower_lanes(tiles[0].shape)
            second = [pltpu.roll(jnp.where(lower, z, x), HALF, 1) for x, z in zip(first, third)]
            for step, tile in enumerate((first + second + third)[1:]):
                high, low = halves(tile)
                for kind in range(2):
                    rows = pl.ds(step // 4 * TILE + kind * HALF + step % 4 * ORB, ORB)
                    high_ref[k, rows, lanes] = high[kind * ORB : (kind + 1) * ORB]
                    low_ref[k, rows, lanes] = low[kind * ORB : (kind + 1) * ORB]
            for kind in range(2):
                rows = pl.ds(2 * TILE + kind * HALF + 3 * ORB, ORB)
                high_ref[k, rows, lanes] = jnp.zeros((ORB, TILE), jnp.bfloat16)
                low_ref[k, rows, lanes] = jnp.zeros((ORB, TILE), jnp.bfloat16)
        start_all(leaving(block, n))
        return carry

    for block in range(blocks):
        lax.fori_loop(0, own, functools.partial(one, block), 0)
    for block in range(blocks):
        lax.fori_loop(0, own, lambda n, c: (wait_all(leaving(block, n)), c)[1], 0)


def both_ladders_kernel(own, tm_ref, retarded_ref, lesser_ref, *others):
    regions, outs, near, others = others[:3], others[3:6], others[6:8], others[8:]
    histories = (tm_ref, retarded_ref, lesser_ref, *regions)
    window = functools.partial(window_ladder_kernel, own, *histories, *outs[:2], *near)
    final_ladder_kernel(*histories, outs[2], *others, meanwhile=window)


def stepped(pair):
    first, second = pair
    place = lax.broadcasted_iota(jnp.int32, first.shape, 1) // ORB % 4
    rows = [jnp.concatenate([first, second, jnp.zeros_like(first)], axis=1)]
    for s in range(1, 4):
        stay = place >= s
        up, over = s * ORB, TILE + (s - 4) * ORB
        rows.append(
            jnp.concatenate(
                [
                    jnp.where(stay, pltpu.roll(first, up, 1), 0.0),
                    jnp.where(stay, pltpu.roll(second, up, 1), pltpu.roll(first, over, 1)),
                    jnp.where(stay, 0.0, pltpu.roll(second, over, 1)),
                ],
                axis=1,
            )
        )
    return jnp.concatenate(rows, axis=0)


def final_kernel(own, fetched, following, before, tm_ref, arrived_ref, propagator_ref, ladder_ref, *others):
    others = list(others)
    source_ref = others.pop(0) if following else None
    others = others[before:]
    out_ref = others.pop(0)
    next_ref = others.pop(0) if following else None
    out_here, arrive, leave, *ladder_here = others
    ladder_here = ladder_ref if fetched else ladder_here[0]
    base = tm_ref[0] * own
    group = own // 2
    groups = own // group
    rows_each = ladder_here.shape[1] // 2

    def arriving(number):
        momenta = pl.ds(number * group, group)
        return [pltpu.make_async_copy(ladder_ref.at[momenta], ladder_here.at[momenta], arrive.at[number])]

    def leaving(number):
        momenta = pl.ds(number * group, group)
        source, target = out_here.at[:, momenta], out_ref.at[:, pl.ds(base + number * group, group)]
        return [pltpu.make_async_copy(source, target, leave.at[number])]

    def one(number, carry):
        if not fetched:
            wait_all(arriving(number))
        for n in range(group):
            k = number * group + n
            pieces = coefficients(arrived_ref, propagator_ref.at[:, base + k], k, own)
            left_high, left_low = halves(jnp.concatenate([stepped(pair) for pair in pieces], axis=0))
            right = ladder_here.at[k]
            parts = contract(left_high, left_low, right[:rows_each], right[rows_each:], TILE)
            for part, value in enumerate(parts):
                tiles = trade([value[s * ORB : (s + 1) * ORB] for s in range(4)])
                for t, tile in enumerate(tiles):
                    out_here[part, k, :, t * TILE : (t + 1) * TILE] = tile
        start_all(leaving(number))
        return carry

    if not fetched:
        for number in range(groups):
            start_all(arriving(number))
    coming = [pltpu.make_async_copy(source_ref, next_ref, arrive.at[groups])] if following else []
    start_all(coming)
    lax.fori_loop(0, groups, one, 0)
    wait_all(coming)
    for number in range(groups):
        wait_all(leaving(number))


def own_block(x, own, axis):
    return lax.dynamic_slice_in_dim(x, lax.axis_index("tm") * own, own, axis)


def on_device_tiled(hist_lesser, hist_retarded, propagator, coupling, mf_weight, lag_weight):
    both_axes = ("mom", "tm")
    momenta_here = hist_lesser.shape[1]
    columns = hist_lesser.shape[3]
    peers = lax.axis_size("tm")
    devices = lax.axis_size("mom") * peers
    own = momenta_here // peers
    count = KX * KY

    f32 = functools.partial(jax.ShapeDtypeStruct, dtype=jnp.float32)
    bf16 = functools.partial(jax.ShapeDtypeStruct, dtype=jnp.bfloat16)

    def call(kernel, shapes, *operands):
        return pl.pallas_call(
            kernel,
            out_shape=shapes,
            in_specs=[SMEM if x.dtype == jnp.int32 else VMEM for x in operands],
            out_specs=jax.tree.map(lambda _: VMEM, shapes),
            compiler_params=limit(12),
        )(*operands)

    half = momenta_here // 2
    window_shape = f32((2, half, ORB, TILE))
    near_shape = f32((4, own, ORB, 2 * TILE))
    here = lax.axis_index("tm")
    here_array = here.reshape(1).astype(jnp.int32)
    low, high, *near = pl.pallas_call(
        functools.partial(regions_kernel, own),
        out_shape=(window_shape, window_shape, near_shape, near_shape, near_shape),
        in_specs=[SMEM, IN_HBM, IN_HBM],
        out_specs=(VMEM,) * 5,
        scratch_shapes=[pltpu.SemaphoreType.DMA((2,)), pltpu.SemaphoreType.DMA((peers - 1, 8))],
        compiler_params=limit(4),
    )(here_array, *(pltpu.with_memory_space_constraint(x, pltpu.HBM) for x in (hist_retarded, hist_lesser)))
    neighbours = [(0, 1), (1, 0), (2, 3), (3, 2)]
    low = lax.ppermute(low, "tm", neighbours)
    send = call(
        lambda tm_ref, *refs: first_window_kernel(tm_ref, peers - 1, *refs),
        f32((devices * half, TILE)),
        here_array,
        propagator,
        low,
        high,
    ).reshape(devices, half, TILE)
    near[0] = lax.ppermute(near[0], "tm", [(3, 0), (0, 1), (1, 2), (2, 3)])
    near[1] = lax.ppermute(near[1], "tm", [(3, 1), (1, 2), (2, 3), (0, 0)])
    send, near[2], hist_lesser, hist_retarded, coupling, mf_weight, lag_weight = lax.optimization_barrier(
        (send, near[2], hist_lesser, hist_retarded, coupling, mf_weight, lag_weight)
    )
    near[2] = lax.ppermute(near[2], "tm", neighbours)
    histories = [pltpu.with_memory_space_constraint(x, pltpu.HBM) for x in (hist_retarded, hist_lesser)]
    me = lax.axis_index("mom") * peers + here
    strength, mean = pl.pallas_call(
        settings_kernel,
        out_shape=(f32((1, TILE)), f32((1, TILE))),
        in_specs=[SMEM] * 4,
        out_specs=(VMEM,) * 2,
        compiler_params=limit(4),
    )(me.reshape(1).astype(jnp.int32), coupling, mf_weight, lag_weight)
    table_high, table_low = fourier_tables()

    ladders = {}
    ladder_shape = (own, 2 * 3 * TILE, 2 * TILE)

    def ladder_scratch(blocks):
        return [
            pltpu.VMEM((4, blocks * own, ORB, TILE + columns), jnp.float32),
            pltpu.VMEM((blocks * own, *ladder_shape[1:]), jnp.bfloat16),
            pltpu.SemaphoreType.DMA((2,)),
            pltpu.SemaphoreType.DMA((4, 2)),
            pltpu.SemaphoreType.DMA((blocks * own,)),
        ]

    def send_beside(sent, step, blocks):
        sent, *edges = lax.optimization_barrier((sent, hist_retarded, hist_lesser, *near))
        arrived = lax.all_to_all(sent, both_axes, 0, 0, tiled=True)
        ladder = pl.pallas_call(
            final_ladder_kernel,
            out_shape=[pltpu.HBM(ladder_shape, jnp.bfloat16)] * blocks,
            in_specs=[SMEM] + [IN_HBM] * 5,
            out_specs=[IN_HBM] * blocks,
            scratch_shapes=ladder_scratch(blocks),
            compiler_params=limit(6 * blocks),
        )(
            jnp.stack([here, here ^ step]).astype(jnp.int32),
            *(pltpu.with_memory_space_constraint(x, pltpu.HBM) for x in edges),
        )
        arrived, *ladder = lax.optimization_barrier((arrived, *ladder))
        ladders.update(zip(range(step, step + blocks), ladder))
        return arrived

    def send_alone(sent):
        return lax.all_to_all(sent, both_axes, 0, 0, tiled=True)

    send_out = [send_alone, send_alone, lambda sent: send_beside(sent, 1, 1)]
    send_back = [send_alone, send_alone, lambda sent: send_beside(sent, 2, 2)]
    for sweep in range(PASSES):
        arrived = send_out[sweep](send)
        back = call(
            fourier_kernel,
            f32((devices, 2 * own, TILE)),
            arrived.reshape(devices // peers, peers, -1, TILE),
            table_high,
            table_low,
            strength,
            mean,
        )
        if sweep == 0:
            near[2], _ = lax.optimization_barrier((near[2], back))
            rungs = bf16((own, 2 * TILE, 2 * TILE))
            *rungs, ladders[0] = pl.pallas_call(
                functools.partial(both_ladders_kernel, own),
                out_shape=(rungs, rungs, pltpu.HBM(ladder_shape, jnp.bfloat16)),
                in_specs=[SMEM] + [IN_HBM] * 5,
                out_specs=(VMEM, VMEM, IN_HBM),
                scratch_shapes=[
                    pltpu.VMEM(near_shape.shape, jnp.float32),
                    pltpu.SemaphoreType.DMA((2,)),
                    *ladder_scratch(1),
                ],
                compiler_params=limit(10),
            )(
                jnp.stack([here, here]).astype(jnp.int32),
                *histories,
                *[pltpu.with_memory_space_constraint(x, pltpu.HBM) for x in near],
            )
            propagator_own = own_block(propagator, own, 1)
        arrived = send_back[sweep](back)
        arrived = arrived.reshape(2 * count, TILE)
        if sweep + 1 < PASSES:
            send = call(
                functools.partial(window_kernel, own),
                f32((count, TILE)),
                arrived,
                propagator_own,
                *rungs,
            ).reshape(devices, own, TILE)

    def finish(new_slice, ladder, coefficients_of, step):
        before = [] if new_slice is None else [new_slice]
        following = [pltpu.with_memory_space_constraint(ladders[step + 1], pltpu.HBM)] if step % 2 == 0 else []
        fetched = ladder is not None
        if not fetched:
            ladder = pltpu.with_memory_space_constraint(ladders[step], pltpu.HBM)
        scratch = [
            pltpu.VMEM((2, own, ORB, columns), jnp.float32),
            pltpu.SemaphoreType.DMA((3,)),
            pltpu.SemaphoreType.DMA((2,)),
        ]
        new_slice, *ladder = pl.pallas_call(
            functools.partial(final_kernel, own, fetched, len(following), len(before)),
            out_shape=[pltpu.HBM(hist_lesser.shape, jnp.float32)] + [bf16(ladder_shape)] * len(following),
            in_specs=[SMEM, VMEM, VMEM, VMEM if fetched else IN_HBM] + [IN_HBM] * len(following + before),
            out_specs=[IN_HBM] + [VMEM] * len(following),
            scratch_shapes=scratch if fetched else scratch + [pltpu.VMEM(ladder_shape, jnp.bfloat16)],
            input_output_aliases={4 + len(following): 0} if before else {},
            compiler_params=limit(6),
        )((here ^ step).reshape(1).astype(jnp.int32), coefficients_of, propagator, ladder, *following, *before)
        return new_slice, *ladder

    def exchange(x, step):
        return lax.ppermute(x, "tm", [(t, t ^ step) for t in range(peers)])

    across = exchange(arrived, 2)
    beside_me = exchange(arrived, 1)
    new_slice, ladder = finish(None, None, arrived, 0)
    (new_slice,) = finish(new_slice, ladder, beside_me, 1)
    across, new_slice = lax.optimization_barrier((across, new_slice))
    beyond = exchange(across, 1)
    new_slice, ladder = finish(new_slice, None, across, 2)
    return finish(new_slice, ladder, beyond, 3)[0]


def on_device(hist_lesser, *others):
    peers = lax.axis_size("tm")
    devices = lax.axis_size("mom") * peers
    fits = devices == 2 * ORB and peers == 4 and hist_lesser.shape[1:] == (2 * ORB, ORB, 4 * TILE)
    return (on_device_tiled if fits else on_device_any)(hist_lesser, *others)


def solution(mesh):
    return jax.shard_map(
        on_device,
        mesh=mesh,
        in_specs=(
            P(None, "mom", None, "tm"),
            P(None, "mom", None, "tm"),
            P(None, "mom", None, None),
            P(),
            P(),
            P(),
        ),
        out_specs=P(None, "mom", None, "tm"),
        check_vma=False,
    )
```

```python
import functools
import math

import jax
import jax.numpy as jnp
import numpy as np
from jax import lax
from jax.experimental import pallas as pl
from jax.experimental.pallas import tpu as pltpu
from jax.sharding import PartitionSpec as P

KX = 16
KY = 16
ORB = 16
W = 8
PASSES = 3


HIGHEST = lax.Precision.HIGHEST


def shifted(x, axis, by):
    peers = lax.axis_size(axis)
    pairs = [(i, i + by) for i in range(peers) if 0 <= i + by < peers]
    return lax.ppermute(x, axis, pairs)


def broadcast(x, axis, root):
    mine = lax.axis_index(axis) == root
    return lax.psum(jnp.where(mine, x, jnp.zeros_like(x)), axis)


def momentum_tables():
    index = jnp.arange(KX * KY, dtype=jnp.int32)
    first = index // KY
    second = index % KY
    turn_x = first[:, None] * first[None, :] % KX
    turn_y = second[:, None] * second[None, :] % KY
    phase = 2.0 * math.pi * (turn_x.astype(jnp.float32) / KX + turn_y.astype(jnp.float32) / KY)
    scale = 1.0 / math.sqrt(KX * KY)
    return (jnp.cos(phase) * scale, jnp.sin(phase) * scale)


def complex_product(pattern, first, second):
    real = jnp.einsum(pattern, first[0], second[0], precision=HIGHEST) - jnp.einsum(
        pattern, first[1], second[1], precision=HIGHEST
    )
    imaginary = jnp.einsum(pattern, first[0], second[1], precision=HIGHEST) + jnp.einsum(
        pattern, first[1], second[0], precision=HIGHEST
    )
    return jnp.stack([real, imaginary])


def back_to_momenta(real, imaginary, cosine, sine):
    out_real = jnp.dot(cosine, real, precision=HIGHEST) + jnp.dot(
        sine, imaginary, precision=HIGHEST
    )
    out_imag = jnp.dot(cosine, imaginary, precision=HIGHEST) - jnp.dot(
        sine, real, precision=HIGHEST
    )
    return jnp.stack([out_real, out_imag])


def local_products(arrived, cosine, sine, strength, lag_mark):
    lag_count = lag_mark.shape[0]
    space_real = jnp.dot(cosine, arrived[0], precision=HIGHEST) - jnp.dot(
        sine, arrived[1], precision=HIGHEST
    )
    space_imag = jnp.dot(cosine, arrived[1], precision=HIGHEST) + jnp.dot(
        sine, arrived[0], precision=HIGHEST
    )
    column_strength = jnp.repeat(strength, lag_count)
    magnitude = column_strength * (space_real * space_real + space_imag * space_imag)
    lesser_real = magnitude * space_real
    lesser_imag = magnitude * space_imag
    pair_real = column_strength * (space_real * space_real - space_imag * space_imag)
    pair_imag = column_strength * 2.0 * space_real * space_imag
    return (
        back_to_momenta(lesser_real, lesser_imag, cosine, sine),
        back_to_momenta(pair_real, pair_imag, cosine, sine),
    )


def self_energies(window, cosine, sine, strength, mf_weight, last_mark):
    momenta_here = window.shape[1]
    outgoing = window.reshape(2, momenta_here, ORB * ORB * W)
    arrived = lax.all_to_all(outgoing, "mom", split_axis=2, concat_axis=1, tiled=True)
    lesser_r, pair_r = local_products(arrived, cosine, sine, strength, last_mark)
    back_lesser, back_pair = (
        lax.all_to_all(lesser_r, "mom", split_axis=1, concat_axis=2, tiled=True),
        lax.all_to_all(pair_r, "mom", split_axis=1, concat_axis=2, tiled=True),
    )
    sigma = back_lesser.reshape(2, momenta_here, ORB, ORB, W)
    pair_k = back_pair.reshape(2, momenta_here, ORB, ORB, W)
    own_total = jnp.sum(window[..., W - 1], axis=1)
    occupation = lax.psum(own_total, "mom") / (KX * KY)
    sigma = sigma + (mf_weight.reshape(ORB, ORB) * occupation)[:, None, :, :, None] * last_mark
    return (sigma, pair_k)


def collide(sigma, pair_k, lag_weight, padded_r, padded_l, first, count):
    weighted_sigma = sigma * lag_weight
    weighted_pair = pair_k * lag_weight

    def ladder(padded):
        region = lax.dynamic_slice_in_dim(padded, first * ORB, (count + W - 1) * ORB, 3)
        return jnp.stack(
            [region[..., offset * ORB : (offset + count) * ORB] for offset in range(W)], axis=3
        )

    return complex_product("kabm,kbmx->kax", weighted_sigma, ladder(padded_r)) + complex_product(
        "kabm,kbmx->kax", weighted_pair, ladder(padded_l)
    )


def on_device_any(hist_lesser, hist_retarded, propagator, coupling, mf_weight, lag_weight):
    momenta_here = hist_lesser.shape[1]
    times_here = hist_lesser.shape[3] // ORB
    cosine, sine = momentum_tables()
    lesser = hist_lesser.reshape(2, momenta_here, ORB, times_here, ORB)
    start = complex_product("kab,kbjc->kajc", propagator, lesser).reshape(
        2, momenta_here, ORB, times_here * ORB
    )
    rim_width = (W - 1) * ORB
    rim_retarded, rim_lesser = shifted(
        (
            hist_retarded[..., times_here * ORB - rim_width :],
            hist_lesser[..., times_here * ORB - rim_width :],
        ),
        "tm",
        1,
    )
    padded_r = jnp.concatenate([rim_retarded, hist_retarded], axis=3)
    padded_l = jnp.concatenate([rim_lesser, hist_lesser], axis=3)
    block = min(32, times_here)
    count_blocks = times_here // block
    window_start = (times_here - W) * ORB
    pair_count = ORB * ORB // lax.axis_size("mom")
    strength = lax.dynamic_slice_in_dim(
        coupling * coupling, lax.axis_index("mom") * pair_count, pair_count, 0
    )
    last_mark = (jnp.arange(W) == W - 1).astype(jnp.float32)
    owner = lax.axis_size("tm") - 1
    current = start[..., window_start:]
    full_slice = start
    for sweep in range(PASSES):
        shared = broadcast(current, "tm", owner)
        window = jnp.transpose(shared.reshape(2, momenta_here, ORB, W, ORB), (0, 1, 2, 4, 3))
        sigma, pair_k = self_energies(window, cosine, sine, strength, mf_weight, last_mark)
        if sweep + 1 < PASSES:
            collision = collide(sigma, pair_k, lag_weight, padded_r, padded_l, times_here - W, W)
            current = start[..., window_start:] + jnp.stack([collision[1], -collision[0]])
        else:
            blocks_out = lax.map(
                lambda number: collide(
                    sigma, pair_k, lag_weight, padded_r, padded_l, number * block, block
                ),
                jnp.arange(count_blocks, dtype=jnp.int32),
            )
            collision = jnp.moveaxis(blocks_out, 0, 3).reshape(
                2, momenta_here, ORB, times_here * ORB
            )
            full_slice = start + jnp.stack([collision[1], -collision[0]])
            current = full_slice[..., window_start:]
    return full_slice


VMEM = pl.BlockSpec(memory_space=pltpu.VMEM)
SMEM = pl.BlockSpec(memory_space=pltpu.SMEM)
IN_HBM = pl.BlockSpec(memory_space=pltpu.HBM)
HALF = W * ORB // 2
TILE = W * ORB


def limit(mebibytes):
    return pltpu.CompilerParams(vmem_limit_bytes=mebibytes * 1024 * 1024)


def halves(x):
    high = x.astype(jnp.bfloat16)
    return high, (x - high.astype(jnp.float32)).astype(jnp.bfloat16)


def matmul(first, second):
    return jnp.dot(first, second, preferred_element_type=jnp.float32)


def fourier_tables():
    index = np.arange(KX * KY)
    turn = np.outer(index // KY, index // KY) / KX + np.outer(index % KY, index % KY) / KY
    phase = 2.0 * np.pi * (turn % 1.0)
    table = np.concatenate([np.cos(phase), np.sin(phase)]) / math.sqrt(KX * KY)
    high = table.astype(jnp.bfloat16)
    low = (table - high.astype(np.float64)).astype(jnp.bfloat16)
    return jnp.asarray(high), jnp.asarray(low)


def lower_lanes(shape):
    return lax.broadcasted_iota(jnp.int32, shape, 1) < HALF


def store_window(send_ref, k, own, real, imag):
    lower = lower_lanes(real.shape)
    turned_real = pltpu.roll(real, HALF, 1)
    turned_imag = pltpu.roll(imag, HALF, 1)
    send_ref[pl.ds(k, ORB, stride=2 * own), :] = jnp.where(lower, real, turned_imag)
    send_ref[pl.ds(own + k, ORB, stride=2 * own), :] = jnp.where(lower, turned_real, imag)


def start_all(copies):
    for copy in copies:
        copy.start()
    return copies


def wait_all(copies):
    for copy in copies:
        copy.wait()


def near_copies(histories, near_ref, tm, own, semaphores):
    copies = []
    for kind, ref in enumerate(histories):
        last = ref.shape[3]
        source = ref.at[:, tm * own : (tm + 1) * own, :, last - 2 * TILE :]
        copies.append(pltpu.make_async_copy(source, near_ref.at[pl.ds(2 * kind, 2)], semaphores.at[kind]))
    return copies


def rim_copies(ref, near_ref, own, semaphores):
    copies = []
    for number in range(8):
        part, half, quarter = number // 4, number // 2 % 2, number % 2
        source = ref.at[part, pl.ds((2 * half + quarter) * own, own), :, pl.ds(ref.shape[3] - TILE, TILE)]
        target = near_ref.at[2 * part + half, :, :, pl.ds(quarter * TILE, TILE)]
        copies.append(pltpu.make_async_copy(source, target, semaphores.at[number]))
    return copies


def settings_kernel(index_ref, coupling_ref, mf_ref, lag_ref, strength_ref, mean_ref):
    lane = lax.broadcasted_iota(jnp.int32, strength_ref.shape, 1)
    first = index_ref[0] // 2 * ORB
    lag = index_ref[0] % 2 * (W // 2) + lane // ORB % (W // 2)
    zero = jnp.zeros(strength_ref.shape, jnp.float32)
    coupling, mf, weight = zero, zero, zero
    for b in range(ORB):
        coupling = jnp.where(lane % ORB == b, coupling_ref[first + b], coupling)
        mf = jnp.where(lane % ORB == b, mf_ref[first + b], mf)
    for m in range(W):
        weight = jnp.where(lag == m, lag_ref[m], weight)
    strength_ref[...] = coupling * coupling * weight
    mean_ref[...] = jnp.where((lag == W - 1) & (lane < HALF), mf * weight, zero)


def regions_kernel(own, tm_ref, retarded_ref, lesser_ref, low_ref, high_ref, *others):
    *out_refs, arrive, pass_on = others
    histories = (retarded_ref, lesser_ref)
    momenta, columns = lesser_ref.shape[1], lesser_ref.shape[3]
    half = momenta // 2
    last = len(out_refs)
    windows = start_all(
        [
            pltpu.make_async_copy(
                lesser_ref.at[:, number * half : (number + 1) * half, :, columns - TILE :], ref, arrive.at[number]
            )
            for number, ref in enumerate((low_ref, high_ref))
        ]
    )

    def near():
        return [c for tm, ref in enumerate(out_refs) for c in near_copies(histories, ref, tm, own, pass_on.at[tm])]

    def rims(second):
        pairs = ((0, retarded_ref), (second, lesser_ref))
        return [c for number, ref in pairs for c in rim_copies(ref, out_refs[number], own, pass_on.at[number])]

    edge = (tm_ref[0] == 0) | (tm_ref[0] == last)
    for case, copies in (
        (tm_ref[0] == last, near),
        (tm_ref[0] == 0, lambda: rims(2)),
        (jnp.logical_not(edge), lambda: rims(1)),
    ):

        @pl.when(case)
        def _():
            wait_all(start_all(copies()))

    wait_all(windows)


def first_window_kernel(tm_ref, last, propagator_ref, low_ref, high_ref, send_ref):
    half = low_ref.shape[1]
    upper = tm_ref[0] == last
    first = jnp.where(upper, half, 0)
    for k in range(half):
        left = jnp.concatenate([propagator_ref[part, first + k] for part in range(2)], axis=0)
        window = [jnp.where(upper, high_ref[part, k], low_ref[part, k]) for part in range(2)]
        imag, real = contract(*halves(left), *halves(jnp.concatenate(window, axis=1)), TILE)
        store_window(send_ref, k, half, -real, imag)


def fourier_kernel(arrived_ref, high_ref, low_ref, strength_ref, mean_ref, out_ref):
    count = KX * KY
    useful = count // (arrived_ref.shape[0] * arrived_ref.shape[2])
    x_high, x_low = halves(arrived_ref[:, arrived_ref.shape[1] - useful :].reshape(count, TILE))
    main = matmul(high_ref[...], jnp.concatenate([x_high, x_low], axis=1))
    turned = main[:, :TILE] + main[:, TILE:] + matmul(low_ref[...], x_high)
    lower = lower_lanes((count, TILE))
    sine_part = pltpu.roll(turned[count:], HALF, 1)
    here = turned[:count] + jnp.where(lower, -sine_part, sine_part)
    swapped = pltpu.roll(here, HALF, 1)
    real = jnp.where(lower, here, swapped)
    imag = jnp.where(lower, swapped, here)
    real_square = real * real
    imag_square = imag * imag
    size = real_square + imag_square
    strength = strength_ref[...]
    out_real = strength * jnp.where(lower, size * real, real_square - imag_square)
    out_imag = strength * jnp.where(lower, size * imag, 2.0 * real * imag)
    origin = (lax.broadcasted_iota(jnp.int32, (count, TILE), 0) == 0).astype(jnp.float32)
    mean = origin * mean_ref[...]
    out_real = out_real + mean * real
    out_imag = out_imag + mean * imag
    real_high, real_low = halves(out_real)
    imag_high, imag_low = halves(out_imag)
    y_high = jnp.concatenate([real_high, imag_high], axis=1)
    y_low = jnp.concatenate([real_low, imag_low], axis=1)
    back = matmul(high_ref[...], y_high) + matmul(low_ref[...], y_high) + matmul(high_ref[...], y_low)
    devices, rows, _ = out_ref.shape
    own = rows // 2
    out_ref[:, :own] = (back[:count, :TILE] + back[count:, TILE:]).reshape(devices, own, TILE)
    out_ref[:, own:] = (back[:count, TILE:] - back[count:, :TILE]).reshape(devices, own, TILE)


def coefficients(arrived_ref, propagator_ref, k, own):
    pieces = []
    for part, start in enumerate((-propagator_ref[1], propagator_ref[0])):
        first, second = (
            arrived_ref[pl.ds((2 * half + part) * own + k, ORB, stride=4 * own), :] for half in range(2)
        )
        start = jnp.concatenate([jnp.zeros((ORB, TILE - ORB), jnp.float32), start], axis=1)
        pieces.append((first, second + start))
    return pieces


def ladder(regions, width):
    rows = []
    for half in range(2):
        for kind in range(2):
            for lag in range(W // 2):
                offset = ORB * (1 + half * (W // 2) + lag)
                rows.append(jnp.concatenate([x[:, offset : offset + width] for x in regions[kind]], axis=1))
    return jnp.concatenate(rows, axis=0)


def contract(left_high, left_low, right_high, right_low, width):
    rows = left_high.shape[0]
    main = matmul(jnp.concatenate([left_high, left_low], axis=0), right_high)
    both = main[:rows] + main[rows:] + matmul(left_high, right_low)
    half = rows // 2
    real = both[:half, :width] - both[half:, width:]
    imag = both[:half, width:] + both[half:, :width]
    return imag, -real


def window_ladder_kernel(own, tm_ref, retarded_ref, lesser_ref, *others):
    *near_refs, high_ref, low_ref, near_ref, arrive = others
    for tm in range(len(near_refs) + 1):

        @pl.when(tm_ref[0] == tm)
        def _():
            if tm < len(near_refs):
                copies = [pltpu.make_async_copy(near_refs[tm], near_ref, arrive.at[0])]
            else:
                copies = near_copies((retarded_ref, lesser_ref), near_ref, tm, own, arrive)
            wait_all(start_all(copies))

    for k in range(own):
        regions = [[near_ref[2 * kind + part, k] for part in range(2)] for kind in range(2)]
        high_ref[k], low_ref[k] = halves(ladder(regions, TILE))


def window_kernel(own, arrived_ref, propagator_ref, high_ref, low_ref, send_ref):
    for k in range(own):
        pieces = coefficients(arrived_ref, propagator_ref.at[:, k], k, own)
        left_high, left_low = halves(jnp.concatenate([jnp.concatenate(pair, axis=1) for pair in pieces], axis=0))
        real, imag = contract(left_high, left_low, high_ref[k], low_ref[k], TILE)
        store_window(send_ref, k, own, real, imag)


def trade(tiles):
    group = lax.broadcasted_iota(jnp.int32, tiles[0].shape, 1) // ORB
    for bit in (2, 1):
        first = (group & bit) == 0
        shift = bit * ORB
        traded = list(tiles)
        for i in range(4):
            if not i & bit:
                x, y = tiles[i], tiles[i | bit]
                traded[i] = jnp.where(first, x, pltpu.roll(y, shift, 1))
                traded[i | bit] = jnp.where(first, pltpu.roll(x, TILE - shift, 1), y)
        tiles = traded
    return tiles


def final_ladder_kernel(tm_ref, retarded_ref, lesser_ref, *others, meanwhile=lambda: None):
    *others, region_ref, ladder_ref, arrive, arrive_rim, leave = others
    rim_refs, outs = others[:3], others[3:]
    count, rows_each = ladder_ref.shape[0], ladder_ref.shape[1] // 2
    high_ref = ladder_ref.at[:, :rows_each]
    low_ref = ladder_ref.at[:, rows_each:]
    own = count // len(outs)
    blocks = len(outs)
    momenta = pl.ds(tm_ref[1] // blocks * count, count)
    fetches = start_all(
        [
            pltpu.make_async_copy(
                ref.at[:, momenta],
                region_ref.at[pl.ds(2 * kind, 2), :, :, pl.ds(TILE, ref.shape[3])],
                arrive.at[kind],
            )
            for kind, ref in enumerate((retarded_ref, lesser_ref))
        ]
    )

    def rims(second, quarters):
        copies = []
        for kind, ref in enumerate((rim_refs[0], rim_refs[second])):
            for part in range(2):
                for number, quarter in enumerate(quarters):
                    source = ref.at[2 * part + tm_ref[1] // 2, :, :, pl.ds(quarter * TILE, TILE)]
                    target = region_ref.at[2 * kind + part, pl.ds(number * own, own), :, pl.ds(0, TILE)]
                    copies.append(pltpu.make_async_copy(source, target, arrive_rim.at[2 * kind + part, number]))
        return copies

    @pl.when(tm_ref[0] == 0)
    def _():
        region_ref[:, :, :, :TILE] = jnp.zeros((4, count, ORB, TILE), jnp.float32)

    def each_rims(act):
        for second, case in ((2, tm_ref[0] == 1), (1, tm_ref[0] > 1)):
            for quarters in [(0, 1)] if blocks == 2 else [(0,), (1,)]:

                @pl.when(case if blocks == 2 else case & (tm_ref[1] % 2 == quarters[0]))
                def _():
                    act(rims(second, quarters))

    each_rims(start_all)
    meanwhile()
    each_rims(wait_all)
    wait_all(fetches)

    def leaving(block, n):
        k = block * own + n
        return [pltpu.make_async_copy(ladder_ref.at[k], outs[block].at[n], leave.at[k])]

    def one(block, n, carry):
        k = block * own + n
        source = (tm_ref[1] % blocks ^ block) * own + n
        for part in range(2):
            region = jnp.concatenate([region_ref[2 * kind + part, source] for kind in range(2)], axis=0)
            lanes = pl.ds(part * TILE, TILE)
            tiles = [region[:, t * TILE : (t + 1) * TILE] for t in range(5)]
            first, third = trade(tiles[:4]), trade(tiles[1:])
            lower = lower_lanes(tiles[0].shape)
            second = [pltpu.roll(jnp.where(lower, z, x), HALF, 1) for x, z in zip(first, third)]
            for step, tile in enumerate((first + second + third)[1:]):
                high, low = halves(tile)
                for kind in range(2):
                    rows = pl.ds(step // 4 * TILE + kind * HALF + step % 4 * ORB, ORB)
                    high_ref[k, rows, lanes] = high[kind * ORB : (kind + 1) * ORB]
                    low_ref[k, rows, lanes] = low[kind * ORB : (kind + 1) * ORB]
            for kind in range(2):
                rows = pl.ds(2 * TILE + kind * HALF + 3 * ORB, ORB)
                high_ref[k, rows, lanes] = jnp.zeros((ORB, TILE), jnp.bfloat16)
                low_ref[k, rows, lanes] = jnp.zeros((ORB, TILE), jnp.bfloat16)
        start_all(leaving(block, n))
        return carry

    for block in range(blocks):
        lax.fori_loop(0, own, functools.partial(one, block), 0)
    for block in range(blocks):
        lax.fori_loop(0, own, lambda n, c: (wait_all(leaving(block, n)), c)[1], 0)


def both_ladders_kernel(own, tm_ref, retarded_ref, lesser_ref, *others):
    regions, outs, near, others = others[:3], others[3:6], others[6:8], others[8:]
    histories = (tm_ref, retarded_ref, lesser_ref, *regions)
    window = functools.partial(window_ladder_kernel, own, *histories, *outs[:2], *near)
    final_ladder_kernel(*histories, outs[2], *others, meanwhile=window)


def stepped(pair):
    first, second = pair
    place = lax.broadcasted_iota(jnp.int32, first.shape, 1) // ORB % 4
    rows = [jnp.concatenate([first, second, jnp.zeros_like(first)], axis=1)]
    for s in range(1, 4):
        stay = place >= s
        up, over = s * ORB, TILE + (s - 4) * ORB
        rows.append(
            jnp.concatenate(
                [
                    jnp.where(stay, pltpu.roll(first, up, 1), 0.0),
                    jnp.where(stay, pltpu.roll(second, up, 1), pltpu.roll(first, over, 1)),
                    jnp.where(stay, 0.0, pltpu.roll(second, over, 1)),
                ],
                axis=1,
            )
        )
    return jnp.concatenate(rows, axis=0)


def final_kernel(own, fetched, following, before, tm_ref, arrived_ref, propagator_ref, ladder_ref, *others):
    others = list(others)
    source_ref = others.pop(0) if following else None
    others = others[before:]
    out_ref = others.pop(0)
    next_ref = others.pop(0) if following else None
    out_here, arrive, leave, *ladder_here = others
    ladder_here = ladder_ref if fetched else ladder_here[0]
    base = tm_ref[0] * own
    group = own // 2
    groups = own // group
    rows_each = ladder_here.shape[1] // 2

    def arriving(number):
        momenta = pl.ds(number * group, group)
        return [pltpu.make_async_copy(ladder_ref.at[momenta], ladder_here.at[momenta], arrive.at[number])]

    def leaving(number):
        momenta = pl.ds(number * group, group)
        source, target = out_here.at[:, momenta], out_ref.at[:, pl.ds(base + number * group, group)]
        return [pltpu.make_async_copy(source, target, leave.at[number])]

    def one(number, carry):
        if not fetched:
            wait_all(arriving(number))
        for n in range(group):
            k = number * group + n
            pieces = coefficients(arrived_ref, propagator_ref.at[:, base + k], k, own)
            left_high, left_low = halves(jnp.concatenate([stepped(pair) for pair in pieces], axis=0))
            right = ladder_here.at[k]
            parts = contract(left_high, left_low, right[:rows_each], right[rows_each:], TILE)
            for part, value in enumerate(parts):
                tiles = trade([value[s * ORB : (s + 1) * ORB] for s in range(4)])
                for t, tile in enumerate(tiles):
                    out_here[part, k, :, t * TILE : (t + 1) * TILE] = tile
        start_all(leaving(number))
        return carry

    if not fetched:
        for number in range(groups):
            start_all(arriving(number))
    coming = [pltpu.make_async_copy(source_ref, next_ref, arrive.at[groups])] if following else []
    start_all(coming)
    for number in range(groups):
        one(number, 0)
    wait_all(coming)
    for number in range(groups):
        wait_all(leaving(number))


def own_block(x, own, axis):
    return lax.dynamic_slice_in_dim(x, lax.axis_index("tm") * own, own, axis)


def on_device_tiled(hist_lesser, hist_retarded, propagator, coupling, mf_weight, lag_weight):
    both_axes = ("mom", "tm")
    momenta_here = hist_lesser.shape[1]
    columns = hist_lesser.shape[3]
    peers = lax.axis_size("tm")
    devices = lax.axis_size("mom") * peers
    own = momenta_here // peers
    count = KX * KY

    f32 = functools.partial(jax.ShapeDtypeStruct, dtype=jnp.float32)
    bf16 = functools.partial(jax.ShapeDtypeStruct, dtype=jnp.bfloat16)

    def call(kernel, shapes, *operands):
        return pl.pallas_call(
            kernel,
            out_shape=shapes,
            in_specs=[SMEM if x.dtype == jnp.int32 else VMEM for x in operands],
            out_specs=jax.tree.map(lambda _: VMEM, shapes),
            compiler_params=limit(12),
        )(*operands)

    half = momenta_here // 2
    window_shape = f32((2, half, ORB, TILE))
    near_shape = f32((4, own, ORB, 2 * TILE))
    here = lax.axis_index("tm")
    here_array = here.reshape(1).astype(jnp.int32)
    low, high, *near = pl.pallas_call(
        functools.partial(regions_kernel, own),
        out_shape=(window_shape, window_shape, near_shape, near_shape, near_shape),
        in_specs=[SMEM, IN_HBM, IN_HBM],
        out_specs=(VMEM,) * 5,
        scratch_shapes=[pltpu.SemaphoreType.DMA((2,)), pltpu.SemaphoreType.DMA((peers - 1, 8))],
        compiler_params=limit(4),
    )(here_array, *(pltpu.with_memory_space_constraint(x, pltpu.HBM) for x in (hist_retarded, hist_lesser)))
    neighbours = [(0, 1), (1, 0), (2, 3), (3, 2)]
    low = lax.ppermute(low, "tm", neighbours)
    send = call(
        lambda tm_ref, *refs: first_window_kernel(tm_ref, peers - 1, *refs),
        f32((devices * half, TILE)),
        here_array,
        propagator,
        low,
        high,
    ).reshape(devices, half, TILE)
    near[0] = lax.ppermute(near[0], "tm", [(3, 0), (0, 1), (1, 2), (2, 3)])
    near[1] = lax.ppermute(near[1], "tm", [(3, 1), (1, 2), (2, 3), (0, 0)])
    send, near[2], hist_lesser, hist_retarded, coupling, mf_weight, lag_weight = lax.optimization_barrier(
        (send, near[2], hist_lesser, hist_retarded, coupling, mf_weight, lag_weight)
    )
    near[2] = lax.ppermute(near[2], "tm", neighbours)
    histories = [pltpu.with_memory_space_constraint(x, pltpu.HBM) for x in (hist_retarded, hist_lesser)]
    me = lax.axis_index("mom") * peers + here
    strength, mean = pl.pallas_call(
        settings_kernel,
        out_shape=(f32((1, TILE)), f32((1, TILE))),
        in_specs=[SMEM] * 4,
        out_specs=(VMEM,) * 2,
        compiler_params=limit(4),
    )(me.reshape(1).astype(jnp.int32), coupling, mf_weight, lag_weight)
    table_high, table_low = fourier_tables()

    ladders = {}
    ladder_shape = (own, 2 * 3 * TILE, 2 * TILE)

    def ladder_scratch(blocks):
        return [
            pltpu.VMEM((4, blocks * own, ORB, TILE + columns), jnp.float32),
            pltpu.VMEM((blocks * own, *ladder_shape[1:]), jnp.bfloat16),
            pltpu.SemaphoreType.DMA((2,)),
            pltpu.SemaphoreType.DMA((4, 2)),
            pltpu.SemaphoreType.DMA((blocks * own,)),
        ]

    def send_beside(sent, step, blocks):
        sent, *edges = lax.optimization_barrier((sent, hist_retarded, hist_lesser, *near))
        arrived = lax.all_to_all(sent, both_axes, 0, 0, tiled=True)
        ladder = pl.pallas_call(
            final_ladder_kernel,
            out_shape=[pltpu.HBM(ladder_shape, jnp.bfloat16)] * blocks,
            in_specs=[SMEM] + [IN_HBM] * 5,
            out_specs=[IN_HBM] * blocks,
            scratch_shapes=ladder_scratch(blocks),
            compiler_params=limit(6 * blocks),
        )(
            jnp.stack([here, here ^ step]).astype(jnp.int32),
            *(pltpu.with_memory_space_constraint(x, pltpu.HBM) for x in edges),
        )
        arrived, *ladder = lax.optimization_barrier((arrived, *ladder))
        ladders.update(zip(range(step, step + blocks), ladder))
        return arrived

    def send_alone(sent):
        return lax.all_to_all(sent, both_axes, 0, 0, tiled=True)

    send_out = [send_alone, send_alone, lambda sent: send_beside(sent, 1, 1)]
    send_back = [send_alone, send_alone, lambda sent: send_beside(sent, 2, 2)]
    for sweep in range(PASSES):
        arrived = send_out[sweep](send)
        back = call(
            fourier_kernel,
            f32((devices, 2 * own, TILE)),
            arrived.reshape(devices // peers, peers, -1, TILE),
            table_high,
            table_low,
            strength,
            mean,
        )
        if sweep == 0:
            near[2], _ = lax.optimization_barrier((near[2], back))
            rungs = bf16((own, 2 * TILE, 2 * TILE))
            *rungs, ladders[0] = pl.pallas_call(
                functools.partial(both_ladders_kernel, own),
                out_shape=(rungs, rungs, pltpu.HBM(ladder_shape, jnp.bfloat16)),
                in_specs=[SMEM] + [IN_HBM] * 5,
                out_specs=(VMEM, VMEM, IN_HBM),
                scratch_shapes=[
                    pltpu.VMEM(near_shape.shape, jnp.float32),
                    pltpu.SemaphoreType.DMA((2,)),
                    *ladder_scratch(1),
                ],
                compiler_params=limit(10),
            )(
                jnp.stack([here, here]).astype(jnp.int32),
                *histories,
                *[pltpu.with_memory_space_constraint(x, pltpu.HBM) for x in near],
            )
            propagator_own = own_block(propagator, own, 1)
        arrived = send_back[sweep](back)
        arrived = arrived.reshape(2 * count, TILE)
        if sweep + 1 < PASSES:
            send = call(
                functools.partial(window_kernel, own),
                f32((count, TILE)),
                arrived,
                propagator_own,
                *rungs,
            ).reshape(devices, own, TILE)

    def finish(new_slice, ladder, coefficients_of, step):
        before = [] if new_slice is None else [new_slice]
        following = [pltpu.with_memory_space_constraint(ladders[step + 1], pltpu.HBM)] if step % 2 == 0 else []
        fetched = ladder is not None
        if not fetched:
            ladder = pltpu.with_memory_space_constraint(ladders[step], pltpu.HBM)
        scratch = [
            pltpu.VMEM((2, own, ORB, columns), jnp.float32),
            pltpu.SemaphoreType.DMA((3,)),
            pltpu.SemaphoreType.DMA((2,)),
        ]
        new_slice, *ladder = pl.pallas_call(
            functools.partial(final_kernel, own, fetched, len(following), len(before)),
            out_shape=[pltpu.HBM(hist_lesser.shape, jnp.float32)] + [bf16(ladder_shape)] * len(following),
            in_specs=[SMEM, VMEM, VMEM, VMEM if fetched else IN_HBM] + [IN_HBM] * len(following + before),
            out_specs=[IN_HBM] + [VMEM] * len(following),
            scratch_shapes=scratch if fetched else scratch + [pltpu.VMEM(ladder_shape, jnp.bfloat16)],
            input_output_aliases={4 + len(following): 0} if before else {},
            compiler_params=limit(6),
        )((here ^ step).reshape(1).astype(jnp.int32), coefficients_of, propagator, ladder, *following, *before)
        return new_slice, *ladder

    def exchange(x, step):
        return lax.ppermute(x, "tm", [(t, t ^ step) for t in range(peers)])

    across = exchange(arrived, 2)
    beside_me = exchange(arrived, 1)
    new_slice, ladder = finish(None, None, arrived, 0)
    (new_slice,) = finish(new_slice, ladder, beside_me, 1)
    across, new_slice = lax.optimization_barrier((across, new_slice))
    beyond = exchange(across, 1)
    new_slice, ladder = finish(new_slice, None, across, 2)
    return finish(new_slice, ladder, beyond, 3)[0]


def on_device(hist_lesser, *others):
    peers = lax.axis_size("tm")
    devices = lax.axis_size("mom") * peers
    fits = devices == 2 * ORB and peers == 4 and hist_lesser.shape[1:] == (2 * ORB, ORB, 4 * TILE)
    return (on_device_tiled if fits else on_device_any)(hist_lesser, *others)


def solution(mesh):
    return jax.shard_map(
        on_device,
        mesh=mesh,
        in_specs=(
            P(None, "mom", None, "tm"),
            P(None, "mom", None, "tm"),
            P(None, "mom", None, None),
            P(),
            P(),
            P(),
        ),
        out_specs=P(None, "mom", None, "tm"),
        check_vma=False,
    )
```

```python
import functools
import math

import jax
import jax.numpy as jnp
import numpy as np
from jax import lax
from jax.experimental import pallas as pl
from jax.experimental.pallas import tpu as pltpu
from jax.sharding import PartitionSpec as P

KX = 16
KY = 16
ORB = 16
W = 8
PASSES = 3


HIGHEST = lax.Precision.HIGHEST


def shifted(x, axis, by):
    peers = lax.axis_size(axis)
    pairs = [(i, i + by) for i in range(peers) if 0 <= i + by < peers]
    return lax.ppermute(x, axis, pairs)


def broadcast(x, axis, root):
    mine = lax.axis_index(axis) == root
    return lax.psum(jnp.where(mine, x, jnp.zeros_like(x)), axis)


def momentum_tables():
    index = jnp.arange(KX * KY, dtype=jnp.int32)
    first = index // KY
    second = index % KY
    turn_x = first[:, None] * first[None, :] % KX
    turn_y = second[:, None] * second[None, :] % KY
    phase = 2.0 * math.pi * (turn_x.astype(jnp.float32) / KX + turn_y.astype(jnp.float32) / KY)
    scale = 1.0 / math.sqrt(KX * KY)
    return (jnp.cos(phase) * scale, jnp.sin(phase) * scale)


def complex_product(pattern, first, second):
    real = jnp.einsum(pattern, first[0], second[0], precision=HIGHEST) - jnp.einsum(
        pattern, first[1], second[1], precision=HIGHEST
    )
    imaginary = jnp.einsum(pattern, first[0], second[1], precision=HIGHEST) + jnp.einsum(
        pattern, first[1], second[0], precision=HIGHEST
    )
    return jnp.stack([real, imaginary])


def back_to_momenta(real, imaginary, cosine, sine):
    out_real = jnp.dot(cosine, real, precision=HIGHEST) + jnp.dot(
        sine, imaginary, precision=HIGHEST
    )
    out_imag = jnp.dot(cosine, imaginary, precision=HIGHEST) - jnp.dot(
        sine, real, precision=HIGHEST
    )
    return jnp.stack([out_real, out_imag])


def local_products(arrived, cosine, sine, strength, lag_mark):
    lag_count = lag_mark.shape[0]
    space_real = jnp.dot(cosine, arrived[0], precision=HIGHEST) - jnp.dot(
        sine, arrived[1], precision=HIGHEST
    )
    space_imag = jnp.dot(cosine, arrived[1], precision=HIGHEST) + jnp.dot(
        sine, arrived[0], precision=HIGHEST
    )
    column_strength = jnp.repeat(strength, lag_count)
    magnitude = column_strength * (space_real * space_real + space_imag * space_imag)
    lesser_real = magnitude * space_real
    lesser_imag = magnitude * space_imag
    pair_real = column_strength * (space_real * space_real - space_imag * space_imag)
    pair_imag = column_strength * 2.0 * space_real * space_imag
    return (
        back_to_momenta(lesser_real, lesser_imag, cosine, sine),
        back_to_momenta(pair_real, pair_imag, cosine, sine),
    )


def self_energies(window, cosine, sine, strength, mf_weight, last_mark):
    momenta_here = window.shape[1]
    outgoing = window.reshape(2, momenta_here, ORB * ORB * W)
    arrived = lax.all_to_all(outgoing, "mom", split_axis=2, concat_axis=1, tiled=True)
    lesser_r, pair_r = local_products(arrived, cosine, sine, strength, last_mark)
    back_lesser, back_pair = (
        lax.all_to_all(lesser_r, "mom", split_axis=1, concat_axis=2, tiled=True),
        lax.all_to_all(pair_r, "mom", split_axis=1, concat_axis=2, tiled=True),
    )
    sigma = back_lesser.reshape(2, momenta_here, ORB, ORB, W)
    pair_k = back_pair.reshape(2, momenta_here, ORB, ORB, W)
    own_total = jnp.sum(window[..., W - 1], axis=1)
    occupation = lax.psum(own_total, "mom") / (KX * KY)
    sigma = sigma + (mf_weight.reshape(ORB, ORB) * occupation)[:, None, :, :, None] * last_mark
    return (sigma, pair_k)


def collide(sigma, pair_k, lag_weight, padded_r, padded_l, first, count):
    weighted_sigma = sigma * lag_weight
    weighted_pair = pair_k * lag_weight

    def ladder(padded):
        region = lax.dynamic_slice_in_dim(padded, first * ORB, (count + W - 1) * ORB, 3)
        return jnp.stack(
            [region[..., offset * ORB : (offset + count) * ORB] for offset in range(W)], axis=3
        )

    return complex_product("kabm,kbmx->kax", weighted_sigma, ladder(padded_r)) + complex_product(
        "kabm,kbmx->kax", weighted_pair, ladder(padded_l)
    )


def on_device_any(hist_lesser, hist_retarded, propagator, coupling, mf_weight, lag_weight):
    momenta_here = hist_lesser.shape[1]
    times_here = hist_lesser.shape[3] // ORB
    cosine, sine = momentum_tables()
    lesser = hist_lesser.reshape(2, momenta_here, ORB, times_here, ORB)
    start = complex_product("kab,kbjc->kajc", propagator, lesser).reshape(
        2, momenta_here, ORB, times_here * ORB
    )
    rim_width = (W - 1) * ORB
    rim_retarded, rim_lesser = shifted(
        (
            hist_retarded[..., times_here * ORB - rim_width :],
            hist_lesser[..., times_here * ORB - rim_width :],
        ),
        "tm",
        1,
    )
    padded_r = jnp.concatenate([rim_retarded, hist_retarded], axis=3)
    padded_l = jnp.concatenate([rim_lesser, hist_lesser], axis=3)
    block = min(32, times_here)
    count_blocks = times_here // block
    window_start = (times_here - W) * ORB
    pair_count = ORB * ORB // lax.axis_size("mom")
    strength = lax.dynamic_slice_in_dim(
        coupling * coupling, lax.axis_index("mom") * pair_count, pair_count, 0
    )
    last_mark = (jnp.arange(W) == W - 1).astype(jnp.float32)
    owner = lax.axis_size("tm") - 1
    current = start[..., window_start:]
    full_slice = start
    for sweep in range(PASSES):
        shared = broadcast(current, "tm", owner)
        window = jnp.transpose(shared.reshape(2, momenta_here, ORB, W, ORB), (0, 1, 2, 4, 3))
        sigma, pair_k = self_energies(window, cosine, sine, strength, mf_weight, last_mark)
        if sweep + 1 < PASSES:
            collision = collide(sigma, pair_k, lag_weight, padded_r, padded_l, times_here - W, W)
            current = start[..., window_start:] + jnp.stack([collision[1], -collision[0]])
        else:
            blocks_out = lax.map(
                lambda number: collide(
                    sigma, pair_k, lag_weight, padded_r, padded_l, number * block, block
                ),
                jnp.arange(count_blocks, dtype=jnp.int32),
            )
            collision = jnp.moveaxis(blocks_out, 0, 3).reshape(
                2, momenta_here, ORB, times_here * ORB
            )
            full_slice = start + jnp.stack([collision[1], -collision[0]])
            current = full_slice[..., window_start:]
    return full_slice


VMEM = pl.BlockSpec(memory_space=pltpu.VMEM)
SMEM = pl.BlockSpec(memory_space=pltpu.SMEM)
IN_HBM = pl.BlockSpec(memory_space=pltpu.HBM)
HALF = W * ORB // 2
TILE = W * ORB


def limit(mebibytes):
    return pltpu.CompilerParams(vmem_limit_bytes=mebibytes * 1024 * 1024)


def halves(x):
    high = x.astype(jnp.bfloat16)
    return high, (x - high.astype(jnp.float32)).astype(jnp.bfloat16)


def matmul(first, second):
    return jnp.dot(first, second, preferred_element_type=jnp.float32)


def fourier_tables():
    index = np.arange(KX * KY)
    turn = np.outer(index // KY, index // KY) / KX + np.outer(index % KY, index % KY) / KY
    phase = 2.0 * np.pi * (turn % 1.0)
    table = np.concatenate([np.cos(phase), np.sin(phase)]) / math.sqrt(KX * KY)
    high = table.astype(jnp.bfloat16)
    low = (table - high.astype(np.float64)).astype(jnp.bfloat16)
    return jnp.asarray(high), jnp.asarray(low)


def lower_lanes(shape):
    return lax.broadcasted_iota(jnp.int32, shape, 1) < HALF


def store_window(send_ref, k, own, real, imag):
    lower = lower_lanes(real.shape)
    turned_real = pltpu.roll(real, HALF, 1)
    turned_imag = pltpu.roll(imag, HALF, 1)
    send_ref[pl.ds(k, ORB, stride=2 * own), :] = jnp.where(lower, real, turned_imag)
    send_ref[pl.ds(own + k, ORB, stride=2 * own), :] = jnp.where(lower, turned_real, imag)


def start_all(copies):
    for copy in copies:
        copy.start()
    return copies


def wait_all(copies):
    for copy in copies:
        copy.wait()


def near_copies(histories, near_ref, tm, own, semaphores):
    copies = []
    for kind, ref in enumerate(histories):
        last = ref.shape[3]
        source = ref.at[:, tm * own : (tm + 1) * own, :, last - 2 * TILE :]
        copies.append(pltpu.make_async_copy(source, near_ref.at[pl.ds(2 * kind, 2)], semaphores.at[kind]))
    return copies


def rim_copies(ref, near_ref, own, semaphores):
    copies = []
    for number in range(8):
        part, half, quarter = number // 4, number // 2 % 2, number % 2
        source = ref.at[part, pl.ds((2 * half + quarter) * own, own), :, pl.ds(ref.shape[3] - TILE, TILE)]
        target = near_ref.at[2 * half + part, :, :, pl.ds(quarter * TILE, TILE)]
        copies.append(pltpu.make_async_copy(source, target, semaphores.at[number]))
    return copies


def settings_kernel(index_ref, coupling_ref, mf_ref, lag_ref, strength_ref, mean_ref):
    lane = lax.broadcasted_iota(jnp.int32, strength_ref.shape, 1)
    first = index_ref[0] // 2 * ORB
    lag = index_ref[0] % 2 * (W // 2) + lane // ORB % (W // 2)
    zero = jnp.zeros(strength_ref.shape, jnp.float32)
    coupling, mf, weight = zero, zero, zero
    for b in range(ORB):
        coupling = jnp.where(lane % ORB == b, coupling_ref[first + b], coupling)
        mf = jnp.where(lane % ORB == b, mf_ref[first + b], mf)
    for m in range(W):
        weight = jnp.where(lag == m, lag_ref[m], weight)
    strength_ref[...] = coupling * coupling * weight
    mean_ref[...] = jnp.where((lag == W - 1) & (lane < HALF), mf * weight, zero)


def regions_kernel(own, tm_ref, retarded_ref, lesser_ref, low_ref, high_ref, *others):
    *out_refs, arrive, pass_on = others
    histories = (retarded_ref, lesser_ref)
    momenta, columns = lesser_ref.shape[1], lesser_ref.shape[3]
    half = momenta // 2
    last = len(out_refs)
    windows = start_all(
        [
            pltpu.make_async_copy(
                lesser_ref.at[:, number * half : (number + 1) * half, :, columns - TILE :], ref, arrive.at[number]
            )
            for number, ref in enumerate((low_ref, high_ref))
        ]
    )

    def near():
        return [c for tm, ref in enumerate(out_refs) for c in near_copies(histories, ref, tm, own, pass_on.at[tm])]

    def rims(second):
        pairs = ((0, retarded_ref), (second, lesser_ref))
        return [c for number, ref in pairs for c in rim_copies(ref, out_refs[number], own, pass_on.at[number])]

    edge = (tm_ref[0] == 0) | (tm_ref[0] == last)
    for case, copies in (
        (tm_ref[0] == last, near),
        (tm_ref[0] == 0, lambda: rims(2)),
        (jnp.logical_not(edge), lambda: rims(1)),
    ):

        @pl.when(case)
        def _():
            wait_all(start_all(copies()))

    wait_all(windows)


def first_window_kernel(tm_ref, last, propagator_ref, low_ref, high_ref, send_ref):
    half = low_ref.shape[1]
    upper = tm_ref[0] == last
    first = jnp.where(upper, half, 0)
    for k in range(half):
        left = jnp.concatenate([propagator_ref[part, first + k] for part in range(2)], axis=0)
        window = [jnp.where(upper, high_ref[part, k], low_ref[part, k]) for part in range(2)]
        imag, real = contract(*halves(left), *halves(jnp.concatenate(window, axis=1)), TILE)
        store_window(send_ref, k, half, -real, imag)


def fourier_kernel(arrived_ref, high_ref, low_ref, strength_ref, mean_ref, out_ref):
    count = KX * KY
    useful = count // (arrived_ref.shape[0] * arrived_ref.shape[2])
    x_high, x_low = halves(arrived_ref[:, arrived_ref.shape[1] - useful :].reshape(count, TILE))
    main = matmul(high_ref[...], jnp.concatenate([x_high, x_low], axis=1))
    turned = main[:, :TILE] + main[:, TILE:] + matmul(low_ref[...], x_high)
    lower = lower_lanes((count, TILE))
    sine_part = pltpu.roll(turned[count:], HALF, 1)
    here = turned[:count] + jnp.where(lower, -sine_part, sine_part)
    swapped = pltpu.roll(here, HALF, 1)
    real = jnp.where(lower, here, swapped)
    imag = jnp.where(lower, swapped, here)
    real_square = real * real
    imag_square = imag * imag
    size = real_square + imag_square
    strength = strength_ref[...]
    out_real = strength * jnp.where(lower, size * real, real_square - imag_square)
    out_imag = strength * jnp.where(lower, size * imag, 2.0 * real * imag)
    origin = (lax.broadcasted_iota(jnp.int32, (count, TILE), 0) == 0).astype(jnp.float32)
    mean = origin * mean_ref[...]
    out_real = out_real + mean * real
    out_imag = out_imag + mean * imag
    real_high, real_low = halves(out_real)
    imag_high, imag_low = halves(out_imag)
    y_high = jnp.concatenate([real_high, imag_high], axis=1)
    y_low = jnp.concatenate([real_low, imag_low], axis=1)
    back = matmul(high_ref[...], y_high) + matmul(low_ref[...], y_high) + matmul(high_ref[...], y_low)
    devices, rows, _ = out_ref.shape
    own = rows // 2
    out_ref[:, :own] = (back[:count, :TILE] + back[count:, TILE:]).reshape(devices, own, TILE)
    out_ref[:, own:] = (back[:count, TILE:] - back[count:, :TILE]).reshape(devices, own, TILE)


def coefficients(arrived_ref, propagator_ref, k, own):
    pieces = []
    for part, start in enumerate((-propagator_ref[1], propagator_ref[0])):
        first, second = (
            arrived_ref[pl.ds((2 * half + part) * own + k, ORB, stride=4 * own), :] for half in range(2)
        )
        start = jnp.concatenate([jnp.zeros((ORB, TILE - ORB), jnp.float32), start], axis=1)
        pieces.append((first, second + start))
    return pieces


def ladder(regions, width):
    rows = []
    for half in range(2):
        for kind in range(2):
            for lag in range(W // 2):
                offset = ORB * (1 + half * (W // 2) + lag)
                rows.append(jnp.concatenate([x[:, offset : offset + width] for x in regions[kind]], axis=1))
    return jnp.concatenate(rows, axis=0)


def contract(left_high, left_low, right_high, right_low, width):
    rows = left_high.shape[0]
    main = matmul(jnp.concatenate([left_high, left_low], axis=0), right_high)
    both = main[:rows] + main[rows:] + matmul(left_high, right_low)
    half = rows // 2
    real = both[:half, :width] - both[half:, width:]
    imag = both[:half, width:] + both[half:, :width]
    return imag, -real


def window_ladder_kernel(own, tm_ref, retarded_ref, lesser_ref, *others):
    *near_refs, high_ref, low_ref, near_ref, arrive = others
    for tm in range(len(near_refs) + 1):

        @pl.when(tm_ref[0] == tm)
        def _():
            if tm < len(near_refs):
                copies = [pltpu.make_async_copy(near_refs[tm], near_ref, arrive.at[0])]
            else:
                copies = near_copies((retarded_ref, lesser_ref), near_ref, tm, own, arrive)
            wait_all(start_all(copies))

    for k in range(own):
        regions = [[near_ref[2 * kind + part, k] for part in range(2)] for kind in range(2)]
        high_ref[k], low_ref[k] = halves(ladder(regions, TILE))


def window_kernel(own, arrived_ref, propagator_ref, high_ref, low_ref, send_ref):
    for k in range(own):
        pieces = coefficients(arrived_ref, propagator_ref.at[:, k], k, own)
        left_high, left_low = halves(jnp.concatenate([jnp.concatenate(pair, axis=1) for pair in pieces], axis=0))
        real, imag = contract(left_high, left_low, high_ref[k], low_ref[k], TILE)
        store_window(send_ref, k, own, real, imag)


def trade(tiles):
    group = lax.broadcasted_iota(jnp.int32, tiles[0].shape, 1) // ORB
    for bit in (2, 1):
        first = (group & bit) == 0
        shift = bit * ORB
        traded = list(tiles)
        for i in range(4):
            if not i & bit:
                x, y = tiles[i], tiles[i | bit]
                traded[i] = jnp.where(first, x, pltpu.roll(y, shift, 1))
                traded[i | bit] = jnp.where(first, pltpu.roll(x, TILE - shift, 1), y)
        tiles = traded
    return tiles


def final_ladder_kernel(tm_ref, retarded_ref, lesser_ref, *others, meanwhile=lambda: None):
    *others, region_ref, ladder_ref, arrive, arrive_rim, leave = others
    rim_refs, outs = others[:3], others[3:]
    count, rows_each = ladder_ref.shape[0], ladder_ref.shape[1] // 2
    high_ref = ladder_ref.at[:, :rows_each]
    low_ref = ladder_ref.at[:, rows_each:]
    own = count // len(outs)
    blocks = len(outs)
    base = tm_ref[1] // blocks * count
    chunk = count // 2

    def fetches(number):
        rows = pl.ds(number * chunk, chunk)
        return [
            pltpu.make_async_copy(
                ref.at[:, pl.ds(base + number * chunk, chunk)],
                region_ref.at[pl.ds(2 * kind, 2), rows, :, pl.ds(TILE, ref.shape[3])],
                arrive.at[kind, number],
            )
            for kind, ref in enumerate((retarded_ref, lesser_ref))
        ]

    order = [number ^ (tm_ref[1] % blocks) for number in range(2)]
    start_all(fetches(order[0]))

    def rims(second, quarters):
        copies = []
        for kind, ref in enumerate((rim_refs[0], rim_refs[second])):
            for number, quarter in enumerate(quarters):
                source = ref.at[pl.ds(tm_ref[1] // 2 * 2, 2), :, :, pl.ds(quarter * TILE, TILE)]
                target = region_ref.at[pl.ds(2 * kind, 2), pl.ds(number * own, own), :, pl.ds(0, TILE)]
                copies.append(pltpu.make_async_copy(source, target, arrive_rim.at[kind, number]))
        return copies

    @pl.when(tm_ref[0] == 0)
    def _():
        region_ref[:, :, :, :TILE] = jnp.zeros((4, count, ORB, TILE), jnp.float32)

    def each_rims(act):
        for second, case in ((2, tm_ref[0] == 1), (1, tm_ref[0] > 1)):
            for quarters in [(0, 1)] if blocks == 2 else [(0,), (1,)]:

                @pl.when(case if blocks == 2 else case & (tm_ref[1] % 2 == quarters[0]))
                def _():
                    act(rims(second, quarters))

    each_rims(start_all)
    start_all(fetches(order[1]))
    meanwhile()
    each_rims(wait_all)

    def leaving(block, n):
        k = block * own + n
        return [pltpu.make_async_copy(ladder_ref.at[k], outs[block].at[n], leave.at[k])]

    def one(block, n, carry):
        k = block * own + n
        source = (tm_ref[1] % blocks ^ block) * own + n
        for part in range(2):
            region = jnp.concatenate([region_ref[2 * kind + part, source] for kind in range(2)], axis=0)
            lanes = pl.ds(part * TILE, TILE)
            tiles = [region[:, t * TILE : (t + 1) * TILE] for t in range(5)]
            first, third = trade(tiles[:4]), trade(tiles[1:])
            lower = lower_lanes(tiles[0].shape)
            second = [pltpu.roll(jnp.where(lower, z, x), HALF, 1) for x, z in zip(first, third)]
            for step, tile in enumerate((first + second + third)[1:]):
                high, low = halves(tile)
                for kind in range(2):
                    rows = pl.ds(step // 4 * TILE + kind * HALF + step % 4 * ORB, ORB)
                    high_ref[k, rows, lanes] = high[kind * ORB : (kind + 1) * ORB]
                    low_ref[k, rows, lanes] = low[kind * ORB : (kind + 1) * ORB]
            for kind in range(2):
                rows = pl.ds(2 * TILE + kind * HALF + 3 * ORB, ORB)
                high_ref[k, rows, lanes] = jnp.zeros((ORB, TILE), jnp.bfloat16)
                low_ref[k, rows, lanes] = jnp.zeros((ORB, TILE), jnp.bfloat16)
        start_all(leaving(block, n))
        return carry

    for number in range(2):
        wait_all(fetches(order[number]))
        block, first = (number, 0) if blocks == 2 else (0, number * chunk)
        lax.fori_loop(first, first + chunk, functools.partial(one, block), 0)
    for block in range(blocks):
        lax.fori_loop(0, own, lambda n, c: (wait_all(leaving(block, n)), c)[1], 0)


def both_ladders_kernel(own, tm_ref, retarded_ref, lesser_ref, *others):
    regions, outs, near, others = others[:3], others[3:6], others[6:8], others[8:]
    histories = (tm_ref, retarded_ref, lesser_ref, *regions)
    window = functools.partial(window_ladder_kernel, own, *histories, *outs[:2], *near)
    final_ladder_kernel(*histories, outs[2], *others, meanwhile=window)


def stepped(pair):
    first, second = pair
    place = lax.broadcasted_iota(jnp.int32, first.shape, 1) // ORB % 4
    rows = [jnp.concatenate([first, second, jnp.zeros_like(first)], axis=1)]
    for s in range(1, 4):
        stay = place >= s
        up, over = s * ORB, TILE + (s - 4) * ORB
        rows.append(
            jnp.concatenate(
                [
                    jnp.where(stay, pltpu.roll(first, up, 1), 0.0),
                    jnp.where(stay, pltpu.roll(second, up, 1), pltpu.roll(first, over, 1)),
                    jnp.where(stay, 0.0, pltpu.roll(second, over, 1)),
                ],
                axis=1,
            )
        )
    return jnp.concatenate(rows, axis=0)


def final_kernel(own, fetched, following, before, tm_ref, arrived_ref, propagator_ref, ladder_ref, *others):
    others = list(others)
    source_ref = others.pop(0) if following else None
    others = others[before:]
    out_ref = others.pop(0)
    next_ref = others.pop(0) if following else None
    out_here, arrive, leave, *ladder_here = others
    ladder_here = ladder_ref if fetched else ladder_here[0]
    base = tm_ref[0] * own
    group = own // 2
    groups = own // group
    rows_each = ladder_here.shape[1] // 2

    def arriving(number):
        momenta = pl.ds(number * group, group)
        return [pltpu.make_async_copy(ladder_ref.at[momenta], ladder_here.at[momenta], arrive.at[number])]

    def leaving(number):
        momenta = pl.ds(number * group, group)
        source, target = out_here.at[:, momenta], out_ref.at[:, pl.ds(base + number * group, group)]
        return [pltpu.make_async_copy(source, target, leave.at[number])]

    def one(number, carry):
        if not fetched:
            wait_all(arriving(number))
        for n in range(group):
            k = number * group + n
            pieces = coefficients(arrived_ref, propagator_ref.at[:, base + k], k, own)
            left_high, left_low = halves(jnp.concatenate([stepped(pair) for pair in pieces], axis=0))
            right = ladder_here.at[k]
            parts = contract(left_high, left_low, right[:rows_each], right[rows_each:], TILE)
            for part, value in enumerate(parts):
                tiles = trade([value[s * ORB : (s + 1) * ORB] for s in range(4)])
                for t, tile in enumerate(tiles):
                    out_here[part, k, :, t * TILE : (t + 1) * TILE] = tile
        start_all(leaving(number))
        return carry

    if not fetched:
        for number in range(groups):
            start_all(arriving(number))
    coming = [pltpu.make_async_copy(source_ref, next_ref, arrive.at[groups])] if following else []
    start_all(coming)
    for number in range(groups):
        one(number, 0)
    wait_all(coming)
    for number in range(groups):
        wait_all(leaving(number))


def own_block(x, own, axis):
    return lax.dynamic_slice_in_dim(x, lax.axis_index("tm") * own, own, axis)


def on_device_tiled(hist_lesser, hist_retarded, propagator, coupling, mf_weight, lag_weight):
    both_axes = ("mom", "tm")
    momenta_here = hist_lesser.shape[1]
    columns = hist_lesser.shape[3]
    peers = lax.axis_size("tm")
    devices = lax.axis_size("mom") * peers
    own = momenta_here // peers
    count = KX * KY

    f32 = functools.partial(jax.ShapeDtypeStruct, dtype=jnp.float32)
    bf16 = functools.partial(jax.ShapeDtypeStruct, dtype=jnp.bfloat16)

    def call(kernel, shapes, *operands):
        return pl.pallas_call(
            kernel,
            out_shape=shapes,
            in_specs=[SMEM if x.dtype == jnp.int32 else VMEM for x in operands],
            out_specs=jax.tree.map(lambda _: VMEM, shapes),
            compiler_params=limit(12),
        )(*operands)

    half = momenta_here // 2
    window_shape = f32((2, half, ORB, TILE))
    near_shape = f32((4, own, ORB, 2 * TILE))
    here = lax.axis_index("tm")
    here_array = here.reshape(1).astype(jnp.int32)
    low, high, *near = pl.pallas_call(
        functools.partial(regions_kernel, own),
        out_shape=(window_shape, window_shape, near_shape, near_shape, near_shape),
        in_specs=[SMEM, IN_HBM, IN_HBM],
        out_specs=(VMEM,) * 5,
        scratch_shapes=[pltpu.SemaphoreType.DMA((2,)), pltpu.SemaphoreType.DMA((peers - 1, 8))],
        compiler_params=limit(4),
    )(here_array, *(pltpu.with_memory_space_constraint(x, pltpu.HBM) for x in (hist_retarded, hist_lesser)))
    neighbours = [(0, 1), (1, 0), (2, 3), (3, 2)]
    low = lax.ppermute(low, "tm", neighbours)
    send = call(
        lambda tm_ref, *refs: first_window_kernel(tm_ref, peers - 1, *refs),
        f32((devices * half, TILE)),
        here_array,
        propagator,
        low,
        high,
    ).reshape(devices, half, TILE)
    near[0] = lax.ppermute(near[0], "tm", [(3, 0), (0, 1), (1, 2), (2, 3)])
    near[1] = lax.ppermute(near[1], "tm", [(3, 1), (1, 2), (2, 3), (0, 0)])
    send, near[2], hist_lesser, hist_retarded, coupling, mf_weight, lag_weight = lax.optimization_barrier(
        (send, near[2], hist_lesser, hist_retarded, coupling, mf_weight, lag_weight)
    )
    near[2] = lax.ppermute(near[2], "tm", neighbours)
    histories = [pltpu.with_memory_space_constraint(x, pltpu.HBM) for x in (hist_retarded, hist_lesser)]
    me = lax.axis_index("mom") * peers + here
    strength, mean = pl.pallas_call(
        settings_kernel,
        out_shape=(f32((1, TILE)), f32((1, TILE))),
        in_specs=[SMEM] * 4,
        out_specs=(VMEM,) * 2,
        compiler_params=limit(4),
    )(me.reshape(1).astype(jnp.int32), coupling, mf_weight, lag_weight)
    table_high, table_low = fourier_tables()

    ladders = {}
    ladder_shape = (own, 2 * 3 * TILE, 2 * TILE)

    def ladder_scratch(blocks):
        return [
            pltpu.VMEM((4, blocks * own, ORB, TILE + columns), jnp.float32),
            pltpu.VMEM((blocks * own, *ladder_shape[1:]), jnp.bfloat16),
            pltpu.SemaphoreType.DMA((2, 2)),
            pltpu.SemaphoreType.DMA((2, 2)),
            pltpu.SemaphoreType.DMA((blocks * own,)),
        ]

    def send_beside(sent, step, blocks):
        sent, *edges = lax.optimization_barrier((sent, hist_retarded, hist_lesser, *near))
        arrived = lax.all_to_all(sent, both_axes, 0, 0, tiled=True)
        ladder = pl.pallas_call(
            final_ladder_kernel,
            out_shape=[pltpu.HBM(ladder_shape, jnp.bfloat16)] * blocks,
            in_specs=[SMEM] + [IN_HBM] * 5,
            out_specs=[IN_HBM] * blocks,
            scratch_shapes=ladder_scratch(blocks),
            compiler_params=limit(6 * blocks),
        )(
            jnp.stack([here, here ^ step]).astype(jnp.int32),
            *(pltpu.with_memory_space_constraint(x, pltpu.HBM) for x in edges),
        )
        arrived, *ladder = lax.optimization_barrier((arrived, *ladder))
        ladders.update(zip(range(step, step + blocks), ladder))
        return arrived

    def send_alone(sent):
        return lax.all_to_all(sent, both_axes, 0, 0, tiled=True)

    send_out = [send_alone, send_alone, lambda sent: send_beside(sent, 1, 1)]
    send_back = [send_alone, send_alone, lambda sent: send_beside(sent, 2, 2)]
    for sweep in range(PASSES):
        arrived = send_out[sweep](send)
        back = call(
            fourier_kernel,
            f32((devices, 2 * own, TILE)),
            arrived.reshape(devices // peers, peers, -1, TILE),
            table_high,
            table_low,
            strength,
            mean,
        )
        if sweep == 0:
            near[2], _ = lax.optimization_barrier((near[2], back))
            rungs = bf16((own, 2 * TILE, 2 * TILE))
            *rungs, ladders[0] = pl.pallas_call(
                functools.partial(both_ladders_kernel, own),
                out_shape=(rungs, rungs, pltpu.HBM(ladder_shape, jnp.bfloat16)),
                in_specs=[SMEM] + [IN_HBM] * 5,
                out_specs=(VMEM, VMEM, IN_HBM),
                scratch_shapes=[
                    pltpu.VMEM(near_shape.shape, jnp.float32),
                    pltpu.SemaphoreType.DMA((2,)),
                    *ladder_scratch(1),
                ],
                compiler_params=limit(10),
            )(
                jnp.stack([here, here]).astype(jnp.int32),
                *histories,
                *[pltpu.with_memory_space_constraint(x, pltpu.HBM) for x in near],
            )
            propagator_own = own_block(propagator, own, 1)
        arrived = send_back[sweep](back)
        arrived = arrived.reshape(2 * count, TILE)
        if sweep + 1 < PASSES:
            send = call(
                functools.partial(window_kernel, own),
                f32((count, TILE)),
                arrived,
                propagator_own,
                *rungs,
            ).reshape(devices, own, TILE)

    def finish(new_slice, ladder, coefficients_of, step):
        before = [] if new_slice is None else [new_slice]
        following = [pltpu.with_memory_space_constraint(ladders[step + 1], pltpu.HBM)] if step % 2 == 0 else []
        fetched = ladder is not None
        if not fetched:
            ladder = pltpu.with_memory_space_constraint(ladders[step], pltpu.HBM)
        scratch = [
            pltpu.VMEM((2, own, ORB, columns), jnp.float32),
            pltpu.SemaphoreType.DMA((3,)),
            pltpu.SemaphoreType.DMA((2,)),
        ]
        new_slice, *ladder = pl.pallas_call(
            functools.partial(final_kernel, own, fetched, len(following), len(before)),
            out_shape=[pltpu.HBM(hist_lesser.shape, jnp.float32)] + [bf16(ladder_shape)] * len(following),
            in_specs=[SMEM, VMEM, VMEM, VMEM if fetched else IN_HBM] + [IN_HBM] * len(following + before),
            out_specs=[IN_HBM] + [VMEM] * len(following),
            scratch_shapes=scratch if fetched else scratch + [pltpu.VMEM(ladder_shape, jnp.bfloat16)],
            input_output_aliases={4 + len(following): 0} if before else {},
            compiler_params=limit(6),
        )((here ^ step).reshape(1).astype(jnp.int32), coefficients_of, propagator, ladder, *following, *before)
        return new_slice, *ladder

    def exchange(x, step):
        return lax.ppermute(x, "tm", [(t, t ^ step) for t in range(peers)])

    across = exchange(arrived, 2)
    beside_me = exchange(arrived, 1)
    new_slice, ladder = finish(None, None, arrived, 0)
    (new_slice,) = finish(new_slice, ladder, beside_me, 1)
    across, new_slice = lax.optimization_barrier((across, new_slice))
    beyond = exchange(across, 1)
    new_slice, ladder = finish(new_slice, None, across, 2)
    return finish(new_slice, ladder, beyond, 3)[0]


def on_device(hist_lesser, *others):
    peers = lax.axis_size("tm")
    devices = lax.axis_size("mom") * peers
    fits = devices == 2 * ORB and peers == 4 and hist_lesser.shape[1:] == (2 * ORB, ORB, 4 * TILE)
    return (on_device_tiled if fits else on_device_any)(hist_lesser, *others)


def solution(mesh):
    return jax.shard_map(
        on_device,
        mesh=mesh,
        in_specs=(
            P(None, "mom", None, "tm"),
            P(None, "mom", None, "tm"),
            P(None, "mom", None, None),
            P(),
            P(),
            P(),
        ),
        out_specs=P(None, "mom", None, "tm"),
        check_vma=False,
    )
```
